256 devices in a mesh: dp: 32 (over z_lo, x, y), tensor: 8 (over z_hi, core).
Axes of the slice: x: 4, y: 4, z: 8 (z_hi: 4, z_lo: 2; z = z_hi * 2 + z_lo), core: 2. Of those that a mesh axis runs over, the one named last changes fastest.
Arguments:
- encoder_input_states: bfloat16 [32, 64, 4096], P('dp', None, 'tensor'), may hold values from -6 to 6
- caption_lengths: int32 [32], P('dp'), may hold values from 16 to 64
- encoder_input_gain: float32 [4096], replicated, may hold values from 0.1 to 1.9
- query_head_gain: float32 [128], replicated, may hold values from 0.1 to 1.9
- key_head_gain: float32 [128], replicated, may hold values from 0.1 to 1.9
- encoder_query_weight: bfloat16 [4096, 4096], P(None, 'tensor'), may hold values from -0.09375 to 0.09375
- encoder_key_weight: bfloat16 [4096, 1024], P(None, 'tensor'), may hold values from -0.09375 to 0.09375
- encoder_value_weight: bfloat16 [4096, 1024], P(None, 'tensor'), may hold values from -0.09375 to 0.09375
- encoder_output_weight: bfloat16 [4096, 4096], P('tensor'), may hold values from -0.09375 to 0.09375
- clean_motion: bfloat16 [32, 360, 256], P('dp'), may hold values from -15 to 15
- noise: bfloat16 [32, 360, 256], P('dp'), may hold values from -15 to 15
- timestep_index: int32 [32], P('dp'), may hold values from 0 to 999
- motion_lengths: int32 [32], P('dp'), may hold values from 90 to 360
- input_weight: bfloat16 [256, 2048], P(None, 'dp'), may hold values from -0.375 to 0.375
- velocity_weight: bfloat16 [2048, 256], P('dp'), may hold values from -0.125 to 0.125
- cross_query_weight: bfloat16 [2048, 2048], P('dp', 'tensor'), may hold values from -0.125 to 0.125
- cross_key_weight: bfloat16 [4096, 2048], P('dp', 'tensor'), may hold values from -0.09375 to 0.09375
- cross_value_weight: bfloat16 [4096, 2048], P('dp', 'tensor'), may hold values from -0.09375 to 0.09375
- cross_output_weight: bfloat16 [2048, 2048], P('tensor', 'dp'), may hold values from -0.125 to 0.125
Outputs:
- loss: float32 [], replicated
- grad_wq: float32 [2048, 2048], P('dp', 'tensor')
- grad_wk: float32 [4096, 2048], P('dp', 'tensor')
- grad_wv: float32 [4096, 2048], P('dp', 'tensor')
- grad_wo: float32 [2048, 2048], P('tensor', 'dp')
The draws below stay inside these ranges and needn't reach their ends.
Inputs may be any that keep to these rules, and one draw needn't show every extreme that they name: caption tokens from index caption_lengths on are padding. Frames from index motion_lengths on are padding.
All inputs are finite; a program needn't handle non-finite values.
Results may differ from the reference program's by a relative error of at most 0.04.
Values may be sent and summed in bfloat16 or wider, within the bound.
A program may use at most 128 MiB of HBM per device.

```python
import math
import jax
import jax.numpy as jnp
from jax import lax

ENCODER_WIDTH = 4096
HQ = 32
KEYVALUE_HEADS = 8
HEAD_WIDTH = 128
MF = 256
L = 64
F = 360
STEPS = 1000
MOTION_WIDTH = 2048
MOTIONS = 32
N_DP = 32


def motion_field(key, rising):
    position = jnp.arange(MOTIONS, dtype=jnp.float32) / max(MOTIONS - 1, 1)
    ramp = (1.0 + rising * position)[:, None, None]
    values = jnp.clip(jax.random.normal(key, (MOTIONS, F, MF), jnp.float32), -6.0, 6.0)
    return (values * ramp).astype(jnp.bfloat16)


def draw_clean_motion(key, part):
    key = jax.random.fold_in(key, 11)
    return motion_field(key, 1.5)


def draw_noise(key, part):
    key = jax.random.fold_in(key, 23)
    return motion_field(key, 1.5)


def with_ends(result, key, least, high):
    shape = result.shape
    place = [jax.random.randint(jax.random.fold_in(key, axis), (), 0, shape[axis]) for axis in range(len(shape))]
    result = result.at[tuple(place)].set(least)
    longest = shape.index(max(shape))
    place[longest] = (place[longest] + 1) % shape[longest]
    return result.at[tuple(place)].set(high)


def steps_of(own_key, extent, shards, least, high):
    def one(dim, parts):
        heights = jax.random.uniform(jax.random.fold_in(jax.random.fold_in(own_key, 6), dim), (parts,), jnp.float32, least / len(shards), high / len(shards))
        return jnp.repeat(jnp.exp(heights), extent[dim] // parts).reshape((-1,) + (1,) * (len(extent) - dim - 1))

    gain = one(*shards[0])
    for cut in shards[1:]:
        gain = gain * one(*cut)
    return gain


def scatter_about(rng, extent, spread, limit, split=(), held_as=jnp.bfloat16):
    drawn = spread * jax.random.normal(rng, extent, jnp.float32)
    if split:
        drawn = drawn * steps_of(rng, extent, split, -0.22, 0.18)
    return jnp.clip(drawn, -limit, limit).astype(held_as)


def setup_inputs(seed: int = 0) -> dict:
    seeds = jax.random.split(jax.random.key(seed), 20)
    return {
        "encoder_input_states": scatter_about(seeds[0], (MOTIONS, L, ENCODER_WIDTH), 1.0, 6.0, ((0, 32), (2, 8))),
        "caption_lengths": with_ends(jax.random.randint(seeds[1], (MOTIONS,), L // 4, L + 1), jax.random.fold_in(seeds[1], 1), L // 4, L).astype(jnp.int32),
        "encoder_input_gain": jnp.clip(1.0 + 0.18 * jax.random.normal(seeds[2], (ENCODER_WIDTH,), jnp.float32), 0.1, 1.9),
        "query_head_gain": jnp.clip(1.0 + 0.18 * jax.random.normal(seeds[3], (HEAD_WIDTH,), jnp.float32), 0.1, 1.9),
        "key_head_gain": jnp.clip(1.0 + 0.18 * jax.random.normal(seeds[4], (HEAD_WIDTH,), jnp.float32), 0.1, 1.9),
        "encoder_query_weight": scatter_about(seeds[5], (ENCODER_WIDTH, HQ * HEAD_WIDTH), ENCODER_WIDTH ** -0.5, 0.09375, ((1, 8),)),
        "encoder_key_weight": scatter_about(seeds[6], (ENCODER_WIDTH, KEYVALUE_HEADS * HEAD_WIDTH), ENCODER_WIDTH ** -0.5, 0.09375, ((1, 8),)),
        "encoder_value_weight": scatter_about(seeds[7], (ENCODER_WIDTH, KEYVALUE_HEADS * HEAD_WIDTH), ENCODER_WIDTH ** -0.5, 0.09375, ((1, 8),)),
        "encoder_output_weight": scatter_about(seeds[8], (HQ * HEAD_WIDTH, ENCODER_WIDTH), (HQ * HEAD_WIDTH) ** -0.5, 0.09375, ((0, 8),)),
        "clean_motion": draw_clean_motion(jax.random.fold_in(seeds[19], 71), 0),
        "noise": draw_noise(jax.random.fold_in(seeds[19], 71), 0),
        "timestep_index": with_ends(jax.random.randint(seeds[11], (MOTIONS,), 0, STEPS), jax.random.fold_in(seeds[11], 1), 0, STEPS - 1).astype(jnp.int32),
        "motion_lengths": with_ends(jax.random.randint(seeds[12], (MOTIONS,), F // 4, F + 1), jax.random.fold_in(seeds[12], 1), F // 4, F).astype(jnp.int32),
        "input_weight": scatter_about(seeds[13], (MF, MOTION_WIDTH), MF ** -0.5, 0.375, ((1, 32),)),
        "velocity_weight": scatter_about(seeds[14], (MOTION_WIDTH, MF), MOTION_WIDTH ** -0.5, 0.125, ((0, 32),)),
        "cross_query_weight": scatter_about(seeds[15], (MOTION_WIDTH, MOTION_WIDTH), MOTION_WIDTH ** -0.5, 0.125, ((0, 32), (1, 8))),
        "cross_key_weight": scatter_about(seeds[16], (ENCODER_WIDTH, MOTION_WIDTH), ENCODER_WIDTH ** -0.5, 0.09375, ((0, 32), (1, 8))),
        "cross_value_weight": scatter_about(seeds[17], (ENCODER_WIDTH, MOTION_WIDTH), ENCODER_WIDTH ** -0.5, 0.09375, ((0, 32), (1, 8))),
        "cross_output_weight": scatter_about(seeds[18], (MOTION_WIDTH, MOTION_WIDTH), MOTION_WIDTH ** -0.5, 0.125, ((0, 8), (1, 32))),
    }


EPSILON = 1e-06

def rope_tables(sequence_length, size_of_head):
    halfway = size_of_head // 2
    inverse = 1000000.0 ** (-(jnp.arange(halfway, dtype=jnp.float32) * 2.0 / size_of_head))
    angles = jnp.arange(sequence_length, dtype=jnp.float32)[:, None] * inverse[None, :]
    angles = jnp.concatenate([angles, angles], axis=1)
    return (jnp.cos(angles)[:, None, :], jnp.sin(angles)[:, None, :])

def rotate(vectors, cosine, sine_table):
    halfway = vectors.shape[-1] // 2
    turned = jnp.concatenate([-vectors[..., halfway:], vectors[..., :halfway]], axis=-1)
    return vectors * cosine + turned * sine_table

def head_norm(vectors, scaling):
    return vectors * lax.rsqrt(lax.optimization_barrier(jnp.mean(vectors * vectors, axis=-1, keepdims=True)) + EPSILON) * scaling

def encode_heads(gathered, caption_lengths, encoder_input_gain, query_head_gain, key_head_gain, encoder_query_weight, encoder_key_weight, encoder_value_weight, encoder_output_weight):
    total_number, sequence_length, model_width = gathered.shape
    size_of_head = query_head_gain.shape[0]
    widened = gathered.astype(jnp.float32)
    normalized_rows = (widened * lax.rsqrt(lax.optimization_barrier(jnp.mean(widened * widened, axis=-1, keepdims=True)) + EPSILON) * encoder_input_gain).astype(jnp.bfloat16)
    flattened_rows = normalized_rows.reshape(total_number * sequence_length, model_width)
    query_heads = encoder_query_weight.shape[1] // size_of_head
    kv_heads = encoder_key_weight.shape[1] // size_of_head
    cosine, sine_table = rope_tables(sequence_length, size_of_head)
    query_matrix = jnp.dot(flattened_rows, encoder_query_weight, preferred_element_type=jnp.float32).reshape(total_number, sequence_length, query_heads, size_of_head)
    query_matrix = rotate(head_norm(query_matrix, query_head_gain), cosine, sine_table).astype(jnp.bfloat16)
    key_matrix = jnp.dot(flattened_rows, encoder_key_weight, preferred_element_type=jnp.float32).reshape(total_number, sequence_length, kv_heads, size_of_head)
    key_matrix = rotate(head_norm(key_matrix, key_head_gain), cosine, sine_table).astype(jnp.bfloat16)
    value_matrix = jnp.dot(flattened_rows, encoder_value_weight, preferred_element_type=jnp.float32).astype(jnp.bfloat16).reshape(total_number, sequence_length, kv_heads, size_of_head)
    repeats = query_heads // kv_heads
    key_matrix = jnp.repeat(key_matrix, repeats, axis=2)
    value_matrix = jnp.repeat(value_matrix, repeats, axis=2)
    scores = jnp.einsum('mqhd,mkhd->mhqk', query_matrix.astype(jnp.float32), key_matrix.astype(jnp.float32)) / math.sqrt(size_of_head)
    position = jnp.arange(sequence_length, dtype=jnp.int32)
    causal = position[None, :] <= position[:, None]
    padding = position[None, :] < caption_lengths[:, None]
    allowed = causal[None, None, :, :] & padding[:, None, None, :]
    scores = jnp.where(allowed, scores, -1e+30)
    weights = jax.nn.softmax(scores, axis=-1).astype(jnp.bfloat16)
    attended_rows = jnp.einsum('mhqk,mkhd->mqhd', weights.astype(jnp.float32), value_matrix.astype(jnp.float32)).astype(jnp.bfloat16)
    attended_rows = attended_rows.reshape(total_number * sequence_length, query_heads * size_of_head)
    return jnp.dot(attended_rows, encoder_output_weight, preferred_element_type=jnp.float32)

def timestep_embedding(timestep_index, model_width):
    halfway = model_width // 2
    frequency = jnp.exp(-math.log(10000.0) * jnp.arange(halfway, dtype=jnp.float32) / halfway)
    angles = timestep_index.astype(jnp.float32)[:, None] * frequency[None, :]
    return jnp.concatenate([jnp.cos(angles), jnp.sin(angles)], axis=1)

def motion_subset(caption_hidden, caption_lengths, clean_motion, noise, timestep_index, motion_lengths, input_weight, velocity_weight, cross_query_weight, cross_key_weight, cross_value_weight, cross_output_weight):
    total_number, frame_count, channels = clean_motion.shape
    sequence_length = caption_hidden.shape[1]
    text_width = caption_hidden.shape[2]
    size_of_head = HEAD_WIDTH
    row_count = total_number * frame_count
    model_width = input_weight.shape[1]
    flow_time = timestep_index.astype(jnp.float32)[:, None, None] / STEPS
    clean = clean_motion.astype(jnp.float32)
    noisy = noise.astype(jnp.float32)
    blended = ((1.0 - flow_time) * clean + flow_time * noisy).astype(jnp.bfloat16)
    target = (noisy - clean).reshape(row_count, channels)
    hidden = jnp.dot(blended.reshape(row_count, channels), input_weight, preferred_element_type=jnp.float32).reshape(total_number, frame_count, model_width)
    hidden = (hidden + timestep_embedding(timestep_index, model_width)[:, None, :]).reshape(row_count, model_width)
    centered = hidden - lax.optimization_barrier(jnp.mean(hidden, axis=-1, keepdims=True))
    normalized_rows = (centered * lax.rsqrt(lax.optimization_barrier(jnp.mean(centered * centered, axis=-1, keepdims=True)) + EPSILON)).astype(jnp.bfloat16)
    count_of_heads = cross_query_weight.shape[1] // size_of_head
    flattened_rows = caption_hidden.reshape(total_number * sequence_length, text_width)
    query_matrix = jnp.dot(normalized_rows, cross_query_weight, preferred_element_type=jnp.float32).astype(jnp.bfloat16).reshape(total_number, frame_count, count_of_heads, size_of_head)
    key_matrix = jnp.dot(flattened_rows, cross_key_weight, preferred_element_type=jnp.float32).astype(jnp.bfloat16).reshape(total_number, sequence_length, count_of_heads, size_of_head)
    value_matrix = jnp.dot(flattened_rows, cross_value_weight, preferred_element_type=jnp.float32).astype(jnp.bfloat16).reshape(total_number, sequence_length, count_of_heads, size_of_head)
    scaling = 1.0 / math.sqrt(size_of_head)
    scores = jnp.einsum('mfhd,mlhd->mhfl', query_matrix.astype(jnp.float32), key_matrix.astype(jnp.float32)) * scaling
    padding = jnp.arange(sequence_length, dtype=jnp.int32)[None, :] < caption_lengths[:, None]
    scores = jnp.where(padding[:, None, None, :], scores, -1e+30)
    weights = jax.nn.softmax(scores, axis=-1)
    weights_b = weights.astype(jnp.bfloat16)
    attended_rows = jnp.einsum('mhfl,mlhd->mfhd', weights_b.astype(jnp.float32), value_matrix.astype(jnp.float32)).astype(jnp.bfloat16)
    attended_rows = attended_rows.reshape(row_count, count_of_heads * size_of_head)
    branch_output = jnp.dot(attended_rows, cross_output_weight, preferred_element_type=jnp.float32)
    projector = velocity_weight.astype(jnp.float32)
    predicted = jnp.dot(hidden + branch_output, projector, precision=lax.Precision.HIGHEST)
    residual = predicted - target
    frame_mask = (jnp.arange(frame_count, dtype=jnp.int32)[None, :] < motion_lengths[:, None]).astype(jnp.float32)
    row_weight = (frame_mask / motion_lengths.astype(jnp.float32)[:, None]).reshape(row_count, 1)
    loss_part = jnp.sum(residual * residual * row_weight)
    d_velocity = 2.0 * residual * row_weight
    output_gradient = jnp.dot(d_velocity, projector.T, precision=lax.Precision.HIGHEST).astype(jnp.bfloat16)
    grad_wo = jnp.dot(attended_rows.T, output_gradient, preferred_element_type=jnp.float32)
    attended_gradient = jnp.dot(output_gradient, cross_output_weight.T, preferred_element_type=jnp.float32).astype(jnp.bfloat16).reshape(total_number, frame_count, count_of_heads, size_of_head)
    d_weights = jnp.einsum('mfhd,mlhd->mhfl', attended_gradient.astype(jnp.float32), value_matrix.astype(jnp.float32))
    row_delta = lax.optimization_barrier(jnp.sum(weights * d_weights, axis=-1, keepdims=True))
    d_scores = (weights * (d_weights - row_delta) * scaling).astype(jnp.bfloat16)
    d_values = jnp.einsum('mhfl,mfhd->mlhd', weights_b.astype(jnp.float32), attended_gradient.astype(jnp.float32)).astype(jnp.bfloat16)
    d_queries = jnp.einsum('mhfl,mlhd->mfhd', d_scores.astype(jnp.float32), key_matrix.astype(jnp.float32)).astype(jnp.bfloat16)
    d_keys = jnp.einsum('mhfl,mfhd->mlhd', d_scores.astype(jnp.float32), query_matrix.astype(jnp.float32)).astype(jnp.bfloat16)
    grad_wq = jnp.dot(normalized_rows.T, d_queries.reshape(row_count, count_of_heads * size_of_head), preferred_element_type=jnp.float32)
    grad_wk = jnp.dot(flattened_rows.T, d_keys.reshape(total_number * sequence_length, count_of_heads * size_of_head), preferred_element_type=jnp.float32)
    grad_wv = jnp.dot(flattened_rows.T, d_values.reshape(total_number * sequence_length, count_of_heads * size_of_head), preferred_element_type=jnp.float32)
    return (loss_part, grad_wq.astype(jnp.bfloat16), grad_wk.astype(jnp.bfloat16), grad_wv.astype(jnp.bfloat16), grad_wo.astype(jnp.bfloat16))

def reference(encoder_input_states, caption_lengths, encoder_input_gain, query_head_gain, key_head_gain, encoder_query_weight, encoder_key_weight, encoder_value_weight, encoder_output_weight, clean_motion, noise, timestep_index, motion_lengths, input_weight, velocity_weight, cross_query_weight, cross_key_weight, cross_value_weight, cross_output_weight):
    block_size = clean_motion.shape[0] // N_DP

    def one_group(block_index):
        offset = block_index * block_size

        def slice_helper(source):
            return lax.dynamic_slice_in_dim(source, offset, block_size, 0)
        gathered = slice_helper(encoder_input_states)
        sequence_lengths = slice_helper(caption_lengths)
        partial_value = encode_heads(gathered, sequence_lengths, encoder_input_gain, query_head_gain, key_head_gain, encoder_query_weight, encoder_key_weight, encoder_value_weight, encoder_output_weight)
        caption_hidden = (gathered.astype(jnp.float32) + partial_value.reshape(gathered.shape)).astype(jnp.bfloat16)
        return motion_subset(caption_hidden, sequence_lengths, slice_helper(clean_motion), slice_helper(noise), slice_helper(timestep_index), slice_helper(motion_lengths), input_weight, velocity_weight, cross_query_weight, cross_key_weight, cross_value_weight, cross_output_weight)
    results = lax.map(one_group, jnp.arange(N_DP, dtype=jnp.int32))
    loss = jnp.sum(results[0]) / (clean_motion.shape[0] * clean_motion.shape[2])
    grad_wq = lax.optimization_barrier(jnp.sum(results[1].astype(jnp.float32), axis=0))
    grad_wk = lax.optimization_barrier(jnp.sum(results[2].astype(jnp.float32), axis=0))
    grad_wv = lax.optimization_barrier(jnp.sum(results[3].astype(jnp.float32), axis=0))
    grad_wo = lax.optimization_barrier(jnp.sum(results[4].astype(jnp.float32), axis=0))
    return (loss, grad_wq, grad_wk, grad_wv, grad_wo)
```

```python
import math
import types

import jax
import jax.numpy as jnp
import numpy as np
from jax import lax
from jax.experimental import pallas as pl
from jax.experimental.pallas import tpu as pltpu
from jax.sharding import PartitionSpec as P

F32 = jnp.float32
BF16 = jnp.bfloat16
MESH = pl.DeviceIdType.MESH
HIGHEST = lax.Precision.HIGHEST
EPSILON = 1e-06
STEPS = 1000
FRAMES = 360
PADDED = 384
SCALE = 1.0 / math.sqrt(128)

INPUTS = [
    "states", "cap_len", "step_index", "motion_len", "gain", "q_gain", "k_gain", "cosine", "sine",
    "eq", "ek", "ev", "eo", "clean", "noise", "w_in", "vel", "wq", "wk", "wv", "wo",
]
OUTPUTS = ["loss", "packed"]

BUFFERS = dict(
    w_qkv=((4096, 768), BF16),
    w_out=((512, 4096), BF16),
    c0=((32, 1, 384), F32),
    gx=((8, 64, 512), BF16),
    wkv=((16, 2, 64, 512), BF16),
    zsb=((32, 16, 256), BF16),
    zrb=((32, 16, 256), BF16),
    zsf=((32, 8, 256), F32),
    zrf=((32, 8, 256), F32),
    zst=((32, 1, 768), F32),
    zrt=((32, 1, 768), F32),
    agb=((32, 16, 256), BF16),
    agf=((2, 32, 8, 256), F32),
    ra_send=((4, 64, 512), BF16),
    ra_recv=((4, 64, 512), BF16),
    rb_send=((4, 64, 512), BF16),
    rb_recv=((4, 64, 512), BF16),
    r_own=((4, 64, 512), F32),
    cap_own=((64, 512), BF16),
    caps=((4, 2, 64, 512), BF16),
    kvx_send=((64, 512), BF16),
    kvx_recv=((64, 512), BF16),
    blend=((PADDED, 256), BF16),
    query=((PADDED, 256), BF16),
    hid_v=((PADDED, 256), F32),
    va_send=((4, 48, 256), BF16),
    va_recv=((4, 48, 256), BF16),
    v_own=((4, 48, 256), F32),
    vb_send=((4, 48, 256), BF16),
    vb_recv=((4, 48, 256), BF16),
    vg=((8, 48, 256), BF16),
    dkx=((2, 2, 64, 256), BF16),
    dk=((4, 2, 64, 256), BF16),
    dv=((4, 2, 64, 256), BF16),
    cap_k=((4, 2, 64, 512), BF16),
    cap_v=((4, 4, 2, 64, 128), BF16),
    gk_send=((4, 128, 256), BF16),
    gk_recv=((4, 128, 256), BF16),
    gv_send=((4, 128, 256), BF16),
    gv_recv=((4, 128, 256), BF16),
    hs=((32, 16, 256), BF16),
    hr=((32, 16, 256), BF16),
    hp=((32, 1, 384), F32),
    hg=((32, 16, 256), BF16),
)

SEMAPHORES = dict(
    load=4,
    c0_s=1, c0_r=1,
    gx_s=8, gx_r=8,
    wkv_s=32, wkv_r=(16, 2),
    zb_s=1, zb_r=1, zf_s=1, zf_r=1, zt_s=1, zt_r=1,
    ab_s=1, ab_r=1, af_s=1, af_r=1, ap_s=1, ap_r=1,
    ra_s=4, ra_r=4, rb_s=4, rb_r=4,
    cp_s=8, cp_r=(4, 2),
    kvx_s=1, kvx_r=1,
    va_s=1, va_r=1, vb_s=4, vb_r=4, vg_s=8, vg_r=8,
    dx_s=2, dx_r=2, dk_s=4, dk_r=4, dv_s=4, dv_r=4,
    ck_s=4, ck_r=4, cv_s=4, cv_r=4,
    gk_s=4, gk_r=4, gv_s=4, gv_r=4,
    hs_s=1, hs_r=1, hp_s=1, hp_r=1, hg_s=1, hg_r=1,
)


def dot(a, b, left, right, precision=None):
    return lax.dot_general(
        a, b, (((left,), (right,)), ((), ())), precision=precision, preferred_element_type=F32
    )


def nn(a, b, precision=None):
    return dot(a, b, 1, 0, precision)


def nt(a, b, precision=None):
    return dot(a, b, 1, 1, precision)


def tn(a, b, precision=None):
    return dot(a, b, 0, 0, precision)


def softmax(scores):
    top = jnp.max(scores, axis=-1, keepdims=True)
    weights = jnp.exp(scores - top)
    return weights / jnp.sum(weights, axis=-1, keepdims=True)


def remote(source, target, send, receive, dp, tensor):
    return pltpu.make_async_remote_copy(
        src_ref=source,
        dst_ref=target,
        send_sem=send,
        recv_sem=receive,
        device_id=(dp, tensor),
        device_id_type=MESH,
    )


def kernel(*refs):
    names = INPUTS + [n + "_out" for n in OUTPUTS] + list(BUFFERS) + list(SEMAPHORES)
    r = types.SimpleNamespace(**dict(zip(names, refs, strict=True)))

    d = lax.axis_index("dp")
    t = lax.axis_index("tensor")
    zl = lax.div(d, 16)
    xy = lax.rem(d, 16)
    x = lax.div(xy, 4)
    y = lax.rem(xy, 4)
    zh = lax.div(t, 2)
    c = lax.rem(t, 2)
    mate = t + 1 - 2 * c
    other = (1 - zl) * 16 + xy
    pending = []

    def start(copy):
        copy.start()
        pending.append(copy)

    def turn(base, k, size):
        return lax.rem(base + k, size)

    def plane(xx, yy):
        return zl * 16 + xx * 4 + yy

    def arrived(slot, semaphore):
        remote(slot, slot, semaphore, semaphore, other, t).wait_recv()

    def all_arrived(buffer, semaphore):
        most = buffer.at[pl.ds(0, 31)]
        remote(most, most, semaphore, semaphore, other, t).wait_recv()

    def all_left(buffer, semaphore):
        most = buffer.at[pl.ds(0, 31)]
        remote(most, most, semaphore, semaphore, other, t).wait_send()

    def over_dp(body):
        def step(k, carry):
            body(k, turn(d, k, 32))
            return carry

        lax.fori_loop(1, 32, step, 0)

    loads = [
        pltpu.make_async_copy(r.eq, r.w_qkv.at[:, pl.ds(0, 512)], r.load.at[0]),
        pltpu.make_async_copy(r.ek, r.w_qkv.at[:, pl.ds(512, 128)], r.load.at[1]),
        pltpu.make_async_copy(r.ev, r.w_qkv.at[:, pl.ds(640, 128)], r.load.at[2]),
        pltpu.make_async_copy(r.eo, r.w_out, r.load.at[3]),
    ]
    for load in loads:
        load.start()

    barrier = pltpu.get_barrier_semaphore()

    def signal(dp, tensor):
        pl.semaphore_signal(barrier, inc=1, device_id=(dp, tensor), device_id_type=MESH)

    over_dp(lambda k, peer: signal(peer, t))
    signal(d, mate)
    for k in (1, 2, 3):
        signal(d, turn(zh, k, 4) * 2 + c)
        signal(other, turn(zh, k, 4) * 2 + c)

    r.gx[t] = r.states[0]
    wk_v = r.wk[...]
    wv_v = r.wv[...]
    for half in (0, 1):
        r.wkv[xy, half, :, 0:256] = wk_v[64 * half : 64 * half + 64]
        r.wkv[xy, half, :, 256:512] = wv_v[64 * half : 64 * half + 64]
    w_in_v = r.w_in[...]
    w_in_t = w_in_v.astype(F32)
    decay = -math.log(10000.0) / 1024.0
    step_f = jnp.full((8, 128), r.step_index[0], jnp.int32).astype(F32)
    place = (
        lax.broadcasted_iota(jnp.int32, (8, 128), 0) * 128
        + lax.broadcasted_iota(jnp.int32, (8, 128), 1)
    ).astype(F32)
    all_angles = step_f * jnp.exp(decay * place)
    all_cos = jnp.cos(all_angles)
    all_sin = jnp.sin(all_angles)

    def total(tile):
        return jnp.sum(jnp.sum(tile, axis=1, keepdims=True), axis=0, keepdims=True)

    own_mean = total(all_cos + all_sin) / 2048.0
    time_square = total((all_cos - own_mean) ** 2 + (all_sin - own_mean) ** 2)
    lane = lax.broadcasted_iota(jnp.int32, (1, 128), 1)
    r.c0[d, :, 0:256] = jnp.sum(w_in_t, axis=0, keepdims=True)
    r.c0[d, :, 256:384] = jnp.where(lane == 0, step_f[0:1], own_mean)

    pl.semaphore_wait(barrier, 38)

    for k in (2, 1, 3):
        start(remote(r.gx.at[t], r.gx.at[t], r.gx_s.at[k], r.gx_r.at[t], d, turn(zh, k, 4) * 2 + c))
    start(remote(r.gx.at[t], r.gx.at[t], r.gx_s.at[0], r.gx_r.at[t], d, mate))

    def c0_copy(k, peer):
        return remote(r.c0.at[d], r.c0.at[d], r.c0_s.at[0], r.c0_r.at[0], peer, t)

    over_dp(lambda k, peer: c0_copy(k, peer).start())

    def wkv_send(slot, half, dp, index):
        ref = r.wkv.at[slot, half]
        start(remote(ref, ref, r.wkv_s.at[index], r.wkv_r.at[slot, half], dp, t))

    for k in (1, 3, 2):
        wkv_send(xy, 0, plane(turn(x, k, 4), y), k - 1)
        wkv_send(xy, 1, plane(x, turn(y, k, 4)), 2 + k)

    all_arrived(r.c0, r.c0_r.at[0])
    facts = r.c0[...].reshape(32, 384)
    w_mean = jnp.sum(facts[:, 0:256], axis=0, keepdims=True) / 2048.0
    steps = facts[:, 256:257]
    step_means = facts[:, 257:258]
    column = (
        lax.broadcasted_iota(jnp.int32, (1, 64), 1) + lax.rem(d, 16) * 64
    ).astype(F32)
    angles = steps * jnp.exp(decay * column)
    cos_part = jnp.full((32, 64), zl, jnp.int32) == 0
    times = jnp.where(cos_part, jnp.cos(angles), jnp.sin(angles))
    times_c = times - step_means
    w_c = w_in_t - w_mean
    vel_v = r.vel[...]
    wq_v = r.wq[...]
    part_a = tn(w_c.astype(BF16), wq_v).reshape(32, 8, 256)
    part_m = tn(r.wo[...], vel_v).reshape(32, 8, 256)
    r.zsb[...] = jnp.concatenate([part_a, part_m], axis=1).astype(BF16)
    first_core = jnp.full((256, 256), c, jnp.int32) == 0
    part_f = jnp.where(first_core, tn(w_in_v, vel_v), tn(w_c, w_c, HIGHEST))
    r.zsf[...] = part_f.reshape(32, 8, 256)
    time_rows = jnp.concatenate(
        [
            nn(times_c, wq_v.astype(F32), HIGHEST),
            nn(times, vel_v.astype(F32), HIGHEST),
            nn(times_c, w_c, HIGHEST),
        ],
        axis=1,
    )
    r.zst[...] = time_rows.reshape(32, 1, 768)
    r.zrb[d] = r.zsb[d]
    r.zrf[d] = r.zsf[d]
    r.zrt[d] = r.zst[d]

    def z_copies(k, peer):
        return (
            remote(r.zsb.at[peer], r.zrb.at[d], r.zb_s.at[0], r.zb_r.at[0], peer, t),
            remote(r.zsf.at[peer], r.zrf.at[d], r.zf_s.at[0], r.zf_r.at[0], peer, t),
            remote(r.zst.at[peer], r.zrt.at[d], r.zt_s.at[0], r.zt_r.at[0], peer, t),
        )

    def z_start(k, peer):
        for copy in z_copies(k, peer):
            copy.start()

    for load in loads[:3]:
        load.wait()

    def project(slot, sums, square):
        chunk = r.gx[slot].astype(F32)
        square = square + jnp.sum(chunk * chunk, axis=1, keepdims=True)
        row = pl.multiple_of(slot * 512, 512)
        scaled = (chunk * r.gain[slot]).astype(BF16)
        return sums + nn(scaled, r.w_qkv[pl.ds(row, 512), :]), square

    sums, square = project(t, jnp.zeros((64, 768), F32), jnp.zeros((64, 1), F32))
    for k in (1, 3, 2):
        slot = turn(zh, k, 4) * 2 + c
        arrived(r.gx.at[slot], r.gx_r.at[slot])
        start(remote(r.gx.at[slot], r.gx.at[slot], r.gx_s.at[4 + k], r.gx_r.at[slot], d, mate))
        sums, square = project(slot, sums, square)

    over_dp(z_start)

    arrived(r.gx.at[mate], r.gx_r.at[mate])
    sums, square = project(mate, sums, square)
    for k in (1, 3, 2):
        slot = turn(zh, k, 4) * 2 + (1 - c)
        arrived(r.gx.at[slot], r.gx_r.at[slot])
        sums, square = project(slot, sums, square)

    def wkv_second(first, k_list):
        for k in k_list:
            if k:
                slot = turn(x, k, 4) * 4 + y
                arrived(r.wkv.at[slot, 0], r.wkv_r.at[slot, 0])
                slot = x * 4 + turn(y, k, 4)
                arrived(r.wkv.at[slot, 1], r.wkv_r.at[slot, 1])
            for j in (1, 3, 2):
                wkv_send(turn(x, k, 4) * 4 + y, 0, plane(x, turn(y, j, 4)), first + 6 * k + j - 1)
                wkv_send(
                    x * 4 + turn(y, k, 4), 1, plane(turn(x, j, 4), y), first + 6 * k + 2 + j
                )

    wkv_second(6, (0, 1, 3, 2))

    length = r.cap_len[0]
    rms = lax.rsqrt(square / 4096.0 + EPSILON)
    sums = sums * rms
    cosine = r.cosine[...]
    sine = r.sine[...]

    def turned(vectors, scaling):
        mean = jnp.mean(vectors * vectors, axis=1, keepdims=True)
        vectors = vectors * lax.rsqrt(mean + EPSILON) * scaling
        return (vectors * cosine + pltpu.roll(vectors, 64, 1) * sine).astype(BF16)

    q_gain = r.q_gain[...]
    queries = jnp.concatenate(
        [turned(sums[:, 128 * h : 128 * h + 128], q_gain) for h in range(4)], axis=0
    )
    keys = turned(sums[:, 512:640], r.k_gain[...])
    values = sums[:, 640:768].astype(BF16)
    scores = nt(queries, keys) * SCALE
    row = lax.rem(lax.broadcasted_iota(jnp.int32, (256, 64), 0), 64)
    col = lax.broadcasted_iota(jnp.int32, (256, 64), 1)
    scores = jnp.where((col <= row) & (col < length), scores, -1e30)
    mixed = nn(softmax(scores).astype(BF16), values).astype(BF16)
    mixed = jnp.concatenate([mixed[64 * h : 64 * h + 64] for h in range(4)], axis=1)

    loads[3].wait()
    for k in (1, 3, 2, 0):
        slot = turn(zh, k, 4)
        column = pl.multiple_of((slot * 2 + 1 - c) * 512, 512)
        r.ra_send[slot] = nn(mixed, r.w_out[:, pl.ds(column, 512)]).astype(BF16)
        start(
            remote(
                r.ra_send.at[slot], r.ra_recv.at[slot], r.ra_s.at[k], r.ra_r.at[slot], d, mate
            )
        )
    for k in (1, 3, 2, 0):
        slot = turn(zh, k, 4)
        column = pl.multiple_of((slot * 2 + c) * 512, 512)
        r.r_own[slot] = nn(mixed, r.w_out[:, pl.ds(column, 512)])
    for k in (2, 1, 3):
        slot = turn(zh, k, 4)
        arrived(r.ra_recv.at[slot], r.ra_r.at[slot])
        r.rb_send[slot] = (r.r_own[slot] + r.ra_recv[slot].astype(F32)).astype(BF16)
        start(
            remote(
                r.rb_send.at[slot], r.rb_recv.at[zh], r.rb_s.at[k], r.rb_r.at[zh], d, slot * 2 + c
            )
        )

    all_arrived(r.zrb, r.zb_r.at[0])
    all_arrived(r.zrf, r.zf_r.at[0])
    all_arrived(r.zrt, r.zt_r.at[0])
    r.agb[d] = jnp.sum(r.zrb[...].astype(F32), axis=0).astype(BF16)
    r.agf[c, d] = jnp.sum(r.zrf[...], axis=0)
    time_own = jnp.sum(r.zrt[...], axis=0)

    def a_copies(k, peer):
        return (
            remote(r.agb.at[d], r.agb.at[d], r.ab_s.at[0], r.ab_r.at[0], peer, t),
            remote(r.agf.at[c, d], r.agf.at[c, d], r.af_s.at[0], r.af_r.at[0], peer, t),
        )

    def a_start(k, peer):
        for copy in a_copies(k, peer):
            copy.start()

    over_dp(a_start)

    slot = zh
    arrived(r.ra_recv.at[slot], r.ra_r.at[slot])
    own = r.r_own[slot] + r.ra_recv[slot].astype(F32)
    for k in (1, 3, 2):
        slot = turn(zh, k, 4)
        arrived(r.rb_recv.at[slot], r.rb_r.at[slot])
        own = own + r.rb_recv[slot].astype(F32)
    r.cap_own[...] = (r.states[0].astype(F32) + own).astype(BF16)

    target = lax.div(zh, 2)
    mine = lax.rem(t, 4)
    inside = target == zl

    def cap_copy(k):
        return remote(
            r.cap_own,
            r.caps.at[mine, zl],
            r.cp_s.at[k],
            r.cp_r.at[mine, zl],
            target * 16 + xy,
            turn(zh, k, 4) * 2 + c,
        )

    for k in (2, 1, 3):
        start(cap_copy(k))

    @pl.when(inside)
    def _():
        r.caps[mine, zl] = r.cap_own[...]

    @pl.when(jnp.logical_not(inside))
    def _():
        cap_copy(0).start()

    clean = r.clean[0].astype(F32)
    noise = r.noise[0].astype(F32)
    tau = jnp.full((1, 256), r.step_index[0], jnp.int32).astype(F32) / STEPS
    margin = jnp.zeros((PADDED - FRAMES, 256), F32)
    blend_f = jnp.concatenate([(1.0 - tau) * clean + tau * noise, margin], axis=0)
    r.blend[...] = blend_f.astype(BF16)
    blend = r.blend[...]
    blend_f = blend.astype(F32)
    all_arrived(r.agb, r.ab_r.at[0])
    all_arrived(r.agf.at[c], r.af_r.at[0])
    start(remote(r.agf.at[c], r.agf.at[c], r.ap_s.at[0], r.ap_r.at[0], d, mate))
    matrices = r.agb[...].astype(F32)
    mat_a = matrices[:, 0:8].reshape(256, 256).astype(BF16)
    mat_m = matrices[:, 8:16].reshape(256, 256).astype(BF16)
    arrived(r.agf.at[1 - c], r.ap_r.at[0])
    mat_b = r.agf[0].reshape(256, 256)
    mat_s = r.agf[1].reshape(256, 256)
    r.hid_v[...] = nn(blend_f, mat_b, HIGHEST) + time_own[:, 256:512]
    spread = (nn(blend_f, mat_s, HIGHEST) + 2.0 * time_own[:, 512:768]) * blend_f
    variance = (jnp.sum(spread, axis=1, keepdims=True) + time_square) / 2048.0
    rstd = lax.rsqrt(jnp.maximum(variance, 0.0) + EPSILON)
    r.query[...] = ((nn(blend, mat_a) + time_own[:, 0:256]) * rstd).astype(BF16)

    for k in (0, 1, 2, 3):
        for j in (1, 2, 3):
            slot = turn(x, k, 4) * 4 + turn(y, j, 4)
            arrived(r.wkv.at[slot, 0], r.wkv_r.at[slot, 0])
            slot = turn(x, j, 4) * 4 + turn(y, k, 4)
            arrived(r.wkv.at[slot, 1], r.wkv_r.at[slot, 1])

    forwards = []
    for z in (0, 1):
        for near in (0, 1):
            chunk = near * 2 + c
            ref = r.caps.at[chunk, z]
            own_slot = inside & (chunk == mine) & (z == zl)

            @pl.when(jnp.logical_not(own_slot))
            def _(ref=ref, chunk=chunk, z=z):
                arrived(ref, r.cp_r.at[chunk, z])

            start(remote(ref, ref, r.cp_s.at[4 + 2 * z + near], r.cp_r.at[chunk, z], d, mate))

    def project_caption(chunk):
        rows = r.caps[chunk].reshape(128, 512)
        weights = r.wkv[pl.ds(chunk * 4, 4)].reshape(512, 512)
        return nn(rows, weights)

    both = project_caption(c) + project_caption(2 + c)
    for near in (0, 1):
        for z in (0, 1):
            chunk = near * 2 + 1 - c
            arrived(r.caps.at[chunk, z], r.cp_r.at[chunk, z])
        both = both + project_caption(near * 2 + 1 - c)
    second = jnp.full((64, 512), zl, jnp.int32) == 1
    r.kvx_send[...] = jnp.where(second, both[0:64], both[64:128]).astype(BF16)
    start(remote(r.kvx_send, r.kvx_recv, r.kvx_s.at[0], r.kvx_r.at[0], other, t))

    r.cap_k[x] = r.caps[x]
    for q in range(4):
        column = pl.multiple_of(y * 128, 128)
        r.cap_v[y, q] = r.caps[q, :, :, pl.ds(column, 128)]
    for k in (1, 3, 2):
        xx = turn(x, k, 4)
        start(
            remote(r.caps.at[xx], r.cap_k.at[x], r.ck_s.at[k], r.ck_r.at[x], plane(xx, y), t)
        )
        yy = turn(y, k, 4)
        column = pl.multiple_of(yy * 128, 128)
        start(
            remote(
                r.caps.at[:, :, :, pl.ds(column, 128)],
                r.cap_v.at[y],
                r.cv_s.at[k],
                r.cv_r.at[y],
                plane(x, yy),
                t,
            )
        )

    kv_own = jnp.where(second, both[64:128], both[0:64])
    arrived(r.kvx_recv, r.kvx_r.at[0])
    kv = (kv_own + r.kvx_recv[...].astype(F32)).astype(BF16)

    query = r.query[...]
    allowed = lax.broadcasted_iota(jnp.int32, (PADDED, 64), 1) < length
    probs = []
    attended = []
    for h in (0, 1):
        span = slice(128 * h, 128 * h + 128)
        scores = nt(query[:, span], kv[:, span]) * SCALE
        prob = softmax(jnp.where(allowed, scores, -1e30))
        probs.append(prob)
        attended.append(nn(prob.astype(BF16), kv[:, 256 + 128 * h : 384 + 128 * h]).astype(BF16))
    attended = jnp.concatenate(attended, axis=1)
    branch = nn(attended, mat_m).reshape(8, 48, 256)

    first_half = jnp.full((48, 256), c, jnp.int32) == 0
    for q in range(4):
        r.va_send[q] = jnp.where(first_half, branch[2 * q + 1], branch[2 * q]).astype(BF16)
        r.v_own[q] = jnp.where(first_half, branch[2 * q], branch[2 * q + 1])
    start(remote(r.va_send, r.va_recv, r.va_s.at[0], r.va_r.at[0], d, mate))
    arrived(r.va_recv, r.va_r.at[0])
    for k in (2, 1, 3):
        slot = turn(zh, k, 4)
        r.vb_send[slot] = (r.v_own[slot] + r.va_recv[slot].astype(F32)).astype(BF16)
        start(
            remote(
                r.vb_send.at[slot], r.vb_recv.at[zh], r.vb_s.at[k], r.vb_r.at[zh], d, slot * 2 + c
            )
        )
    own = r.v_own[zh] + r.va_recv[zh].astype(F32)
    for k in (1, 3, 2):
        slot = turn(zh, k, 4)
        arrived(r.vb_recv.at[slot], r.vb_r.at[slot])
        own = own + r.vb_recv[slot].astype(F32)
    r.vg[t] = own.astype(BF16)
    for k in (2, 1, 3):
        start(remote(r.vg.at[t], r.vg.at[t], r.vg_s.at[k], r.vg_r.at[t], d, turn(zh, k, 4) * 2 + c))
    start(remote(r.vg.at[t], r.vg.at[t], r.vg_s.at[0], r.vg_r.at[t], d, mate))
    for k in (1, 3, 2):
        slot = turn(zh, k, 4) * 2 + c
        arrived(r.vg.at[slot], r.vg_r.at[slot])
        start(remote(r.vg.at[slot], r.vg.at[slot], r.vg_s.at[4 + k], r.vg_r.at[slot], d, mate))
    arrived(r.vg.at[mate], r.vg_r.at[mate])
    for k in (1, 3, 2):
        slot = turn(zh, k, 4) * 2 + 1 - c
        arrived(r.vg.at[slot], r.vg_r.at[slot])

    predicted = r.hid_v[...] + r.vg[...].astype(F32).reshape(PADDED, 256)
    residual = predicted - jnp.concatenate([noise - clean, margin], axis=0)
    frames = jnp.full((PADDED, 1), r.motion_len[0], jnp.int32)
    live = lax.broadcasted_iota(jnp.int32, (PADDED, 1), 0) < frames
    row_weight = jnp.where(live, 1.0 / frames.astype(F32), 0.0)
    weighted = residual * row_weight
    loss_part = total(residual * weighted)
    d_vel = (2.0 * weighted).astype(BF16)
    d_att = nt(d_vel, mat_m).astype(BF16)

    d_keys = []
    d_values = []
    d_queries = []
    for h in (0, 1):
        span = slice(128 * h, 128 * h + 128)
        d_head = d_att[:, span]
        d_prob = nt(d_head, kv[:, 256 + 128 * h : 384 + 128 * h])
        prob = probs[h]
        delta = jnp.sum(prob * d_prob, axis=1, keepdims=True)
        d_score = (prob * (d_prob - delta) * SCALE).astype(BF16)
        d_values.append(tn(prob.astype(BF16), d_head))
        d_keys.append(tn(d_score, query[:, span]))
        d_queries.append(nn(d_score, kv[:, span]))
    r.dkx[0, zl] = jnp.concatenate(d_keys, axis=1).astype(BF16)
    r.dkx[1, zl] = jnp.concatenate(d_values, axis=1).astype(BF16)
    for i in (0, 1):
        ref = r.dkx.at[i, zl]
        start(remote(ref, ref, r.dx_s.at[i], r.dx_r.at[i], other, t))
    d_query = jnp.concatenate(d_queries, axis=1).astype(BF16).astype(F32) * rstd
    d_query_b = d_query.astype(BF16)
    mat_h = tn(blend, d_query_b).reshape(32, 8, 256)
    mat_g = tn(attended, d_vel).reshape(32, 8, 256)
    r.hs[...] = jnp.concatenate([mat_h, mat_g], axis=1).astype(BF16)
    r.hr[d] = r.hs[d]
    r.hp[d, :, 0:256] = jnp.sum(d_query, axis=0, keepdims=True)
    r.hp[d, :, 256:384] = jnp.broadcast_to(loss_part, (1, 128))

    for i in (0, 1):
        arrived(r.dkx.at[i, 1 - zl], r.dx_r.at[i])
    r.dk[x] = r.dkx[0]
    r.dv[y] = r.dkx[1]
    for k in (1, 3, 2):
        start(
            remote(
                r.dk.at[x], r.dk.at[x], r.dk_s.at[k], r.dk_r.at[x], plane(turn(x, k, 4), y), t
            )
        )
        start(
            remote(
                r.dv.at[y], r.dv.at[y], r.dv_s.at[k], r.dv_r.at[y], plane(x, turn(y, k, 4)), t
            )
        )

    def h_copies(k, peer):
        return (
            remote(r.hs.at[peer], r.hr.at[d], r.hs_s.at[0], r.hs_r.at[0], peer, t),
            remote(r.hp.at[d], r.hp.at[d], r.hp_s.at[0], r.hp_r.at[0], peer, t),
        )

    def h_start(k, peer):
        for copy in h_copies(k, peer):
            copy.start()

    over_dp(h_start)

    for k in (1, 3, 2):
        slot = turn(x, k, 4)
        arrived(r.cap_k.at[slot], r.ck_r.at[slot])
        arrived(r.dk.at[slot], r.dk_r.at[slot])
        slot = turn(y, k, 4)
        arrived(r.cap_v.at[slot], r.cv_r.at[slot])
        arrived(r.dv.at[slot], r.dv_r.at[slot])
    all_k = r.dk[...].reshape(512, 256)
    grad_k = tn(r.cap_k[...].reshape(512, 512), all_k).reshape(4, 128, 256)
    for q in range(4):
        r.gk_send[q] = grad_k[q].astype(BF16)
    r.gk_recv[y] = r.gk_send[y]
    for k in (1, 3, 2):
        yy = turn(y, k, 4)
        start(
            remote(
                r.gk_send.at[yy], r.gk_recv.at[y], r.gk_s.at[k], r.gk_r.at[y], plane(x, yy), t
            )
        )
    all_v = r.dv[...].reshape(512, 256)
    for q in range(4):
        grad_v = tn(r.cap_v[:, q].reshape(512, 128), all_v)
        r.gv_send[q] = grad_v.astype(BF16)
    r.gv_recv[x] = r.gv_send[x]
    for k in (1, 3, 2):
        xx = turn(x, k, 4)
        start(
            remote(
                r.gv_send.at[xx], r.gv_recv.at[x], r.gv_s.at[k], r.gv_r.at[x], plane(xx, y), t
            )
        )

    all_arrived(r.hr, r.hs_r.at[0])
    r.hg[d] = jnp.sum(r.hr[...].astype(F32), axis=0).astype(BF16)

    def g_copy(k, peer):
        return remote(r.hg.at[d], r.hg.at[d], r.hg_s.at[0], r.hg_r.at[0], peer, t)

    over_dp(lambda k, peer: g_copy(k, peer).start())
    all_arrived(r.hp, r.hp_r.at[0])
    sums_p = r.hp[...].reshape(32, 384)
    r.loss_out[...] = jnp.sum(sums_p[:, 256:384], axis=0, keepdims=True) / 8192.0
    all_arrived(r.hg, r.hg_r.at[0])
    grads = r.hg[...].astype(F32)
    sum_h = grads[:, 0:8].reshape(256, 256)
    sum_g = grads[:, 8:16].reshape(256, 256).astype(BF16)
    r.packed_out[0:64] = nn(w_c, sum_h, HIGHEST) + tn(times_c, sums_p[:, 0:256], HIGHEST)
    r.packed_out[320:384] = nt(r.vel[...], sum_g)
    for k in (1, 3, 2):
        slot = turn(y, k, 4)
        arrived(r.gk_recv.at[slot], r.gk_r.at[slot])
        slot = turn(x, k, 4)
        arrived(r.gv_recv.at[slot], r.gv_r.at[slot])
    r.packed_out[64:192] = jnp.sum(r.gk_recv[...].astype(F32), axis=0)
    r.packed_out[192:320] = jnp.sum(r.gv_recv[...].astype(F32), axis=0)

    for copy in pending:
        copy.wait_send()

    @pl.when(jnp.logical_not(inside))
    def _():
        cap_copy(0).wait_send()

    all_left(r.c0, r.c0_s.at[0])
    all_left(r.zrb, r.zb_s.at[0])
    all_left(r.zrf, r.zf_s.at[0])
    all_left(r.zrt, r.zt_s.at[0])
    all_left(r.agb, r.ab_s.at[0])
    all_left(r.agf.at[c], r.af_s.at[0])
    all_left(r.hr, r.hs_s.at[0])
    all_left(r.hp, r.hp_s.at[0])
    all_left(r.hg, r.hg_s.at[0])


def unpack(loss, packed, loss_out, gq, gk, gv, go):
    loss_out[...] = loss[...]
    gq[...] = packed[0:64]
    gk[...] = packed[64:192]
    gv[...] = packed[192:320]
    go[...] = packed[320:384]


def rope_tables():
    inverse = 1000000.0 ** (-(np.arange(64, dtype=np.float32) * 2.0 / 128))
    angles = np.arange(64, dtype=np.float32)[:, None] * inverse[None, :].astype(np.float32)
    angles = np.concatenate([angles, angles], axis=1).astype(np.float32)
    sign = np.where(np.arange(128) < 64, -1.0, 1.0)[None, :]
    return np.cos(angles).astype(np.float32), (np.sin(angles) * sign).astype(np.float32)


def local(
    encoder_input_states,
    caption_lengths,
    encoder_input_gain,
    query_head_gain,
    key_head_gain,
    encoder_query_weight,
    encoder_key_weight,
    encoder_value_weight,
    encoder_output_weight,
    clean_motion,
    noise,
    timestep_index,
    motion_lengths,
    input_weight,
    velocity_weight,
    cross_query_weight,
    cross_key_weight,
    cross_value_weight,
    cross_output_weight,
):
    vmem = pl.BlockSpec(memory_space=pltpu.VMEM)
    hbm = pl.BlockSpec(memory_space=pl.ANY)
    smem = pl.BlockSpec(memory_space=pltpu.SMEM)
    spec = {name: vmem for name in INPUTS}
    for name in ("cap_len", "step_index", "motion_len"):
        spec[name] = smem
    for name in ("eq", "ek", "ev", "eo"):
        spec[name] = hbm
    cosine, sine = rope_tables()
    packed = pl.pallas_call(
        kernel,
        out_shape=[
            jax.ShapeDtypeStruct((1, 128), F32),
            jax.ShapeDtypeStruct((384, 256), F32),
        ],
        in_specs=[spec[name] for name in INPUTS],
        out_specs=[vmem] * 2,
        scratch_shapes=[pltpu.VMEM(shape, kind) for shape, kind in BUFFERS.values()]
        + [
            pltpu.SemaphoreType.DMA(shape if isinstance(shape, tuple) else (shape,))
            for shape in SEMAPHORES.values()
        ],
        compiler_params=pltpu.CompilerParams(
            collective_id=0, has_side_effects=True, vmem_limit_bytes=56 * 2**20
        ),
        name="motion_block",
    )(
        encoder_input_states,
        caption_lengths,
        timestep_index,
        motion_lengths,
        encoder_input_gain.reshape(8, 1, 512),
        query_head_gain.reshape(1, 128),
        key_head_gain.reshape(1, 128),
        jnp.asarray(cosine),
        jnp.asarray(sine),
        encoder_query_weight,
        encoder_key_weight,
        encoder_value_weight,
        encoder_output_weight,
        clean_motion,
        noise,
        input_weight.T,
        velocity_weight,
        cross_query_weight,
        cross_key_weight,
        cross_value_weight,
        cross_output_weight.T,
    )
    loss, gq, gk, gv, go = pl.pallas_call(
        unpack,
        out_shape=[
            jax.ShapeDtypeStruct((1, 128), F32),
            jax.ShapeDtypeStruct((64, 256), F32),
            jax.ShapeDtypeStruct((128, 256), F32),
            jax.ShapeDtypeStruct((128, 256), F32),
            jax.ShapeDtypeStruct((64, 256), F32),
        ],
        in_specs=[vmem] * 2,
        out_specs=[vmem] * 5,
        name="unpack",
    )(*packed)
    return (loss[0, 0], gq, gk, gv, go.T)


def solution(mesh):
    placed = (
        P("dp", None, "tensor"),
        P("dp"),
        P(),
        P(),
        P(),
        P(None, "tensor"),
        P(None, "tensor"),
        P(None, "tensor"),
        P("tensor", None),
        P("dp", None, None),
        P("dp", None, None),
        P("dp"),
        P("dp"),
        P(None, "dp"),
        P("dp", None),
        P("dp", "tensor"),
        P("dp", "tensor"),
        P("dp", "tensor"),
        P("tensor", "dp"),
    )
    return jax.shard_map(
        local,
        mesh=mesh,
        in_specs=placed,
        out_specs=(P(), P("dp", "tensor"), P("dp", "tensor"), P("dp", "tensor"), P("tensor", "dp")),
        check_vma=False,
    )
```

```python
import math
import types

import jax
import jax.numpy as jnp
import numpy as np
from jax import lax
from jax.experimental import pallas as pl
from jax.experimental.pallas import tpu as pltpu
from jax.sharding import PartitionSpec as P

F32 = jnp.float32
BF16 = jnp.bfloat16
MESH = pl.DeviceIdType.MESH
HIGHEST = lax.Precision.HIGHEST
EPSILON = 1e-06
STEPS = 1000
FRAMES = 360
PADDED = 384
SCALE = 1.0 / math.sqrt(128)

INPUTS = [
    "states", "cap_len", "step_index", "motion_len", "gain", "q_gain", "k_gain", "cosine", "sine",
    "eq", "ek", "ev", "eo", "clean", "noise", "w_in", "vel", "wq", "wk", "wv", "wo",
]
OUTPUTS = ["loss", "packed"]

BUFFERS = dict(
    w_qkv=((4096, 768), BF16),
    w_out=((512, 4096), BF16),
    c0=((32, 1, 384), F32),
    gx=((8, 64, 512), BF16),
    wkv=((16, 2, 64, 512), BF16),
    zsb=((32, 16, 256), BF16),
    zrb=((32, 16, 256), BF16),
    zsf=((32, 8, 384), F32),
    zrf=((32, 8, 384), F32),
    agb=((32, 16, 256), BF16),
    agf=((2, 32, 8, 256), F32),
    ra_send=((4, 64, 512), BF16),
    ra_recv=((4, 64, 512), BF16),
    rb_send=((4, 64, 512), BF16),
    rb_recv=((4, 64, 512), BF16),
    r_own=((4, 64, 512), F32),
    cap_own=((64, 512), BF16),
    caps=((4, 2, 64, 512), BF16),
    kvx_send=((64, 512), BF16),
    kvx_recv=((64, 512), BF16),
    blend=((PADDED, 256), BF16),
    query=((PADDED, 256), BF16),
    hid_v=((PADDED, 256), F32),
    va_send=((4, 48, 256), BF16),
    va_recv=((4, 48, 256), BF16),
    v_own=((4, 48, 256), F32),
    vb_send=((4, 48, 256), BF16),
    vb_recv=((4, 48, 256), BF16),
    vg=((8, 48, 256), BF16),
    dkx=((2, 2, 64, 256), BF16),
    dk=((4, 2, 64, 256), BF16),
    dv=((4, 2, 64, 256), BF16),
    cap_k=((4, 2, 64, 512), BF16),
    cap_v=((4, 4, 2, 64, 128), BF16),
    cap_kt=((512, 512), BF16),
    cap_vt=((4, 128, 512), BF16),
    blend_t=((256, PADDED), BF16),
    att_t=((256, PADDED), BF16),
    prob_t=((2, 64, PADDED), BF16),
    gk_send=((4, 128, 256), BF16),
    gk_recv=((4, 128, 256), BF16),
    gv_send=((4, 128, 256), BF16),
    gv_recv=((4, 128, 256), BF16),
    hs=((32, 16, 384), BF16),
    hr=((32, 16, 384), BF16),
    hg=((32, 16, 256), BF16),
)

SEMAPHORES = dict(
    load=4,
    c0_s=1, c0_r=1,
    gx_s=8, gx_r=8,
    wkv_s=32, wkv_r=(16, 2),
    zb_s=1, zb_r=1, zf_s=1, zf_r=1,
    ab_s=1, ab_r=1, af_s=1, af_r=1, ap_s=1, ap_r=1,
    ra_s=4, ra_r=4, rb_s=4, rb_r=4,
    cp_s=8, cp_r=(4, 2),
    kvx_s=1, kvx_r=1,
    va_s=1, va_r=1, vb_s=4, vb_r=4, vg_s=8, vg_r=8,
    dx_s=2, dx_r=2, dk_s=4, dk_r=4, dv_s=4, dv_r=4,
    ck_s=4, ck_r=4, cv_s=4, cv_r=4,
    gk_s=4, gk_r=4, gv_s=4, gv_r=4,
    hs_s=1, hs_r=1, hg_s=1, hg_r=1,
)


def dot(a, b, left, right, precision=None):
    return lax.dot_general(
        a, b, (((left,), (right,)), ((), ())), precision=precision, preferred_element_type=F32
    )


def nn(a, b, precision=None):
    return dot(a, b, 1, 0, precision)


def nt(a, b, precision=None):
    return dot(a, b, 1, 1, precision)


def tn(a, b, precision=None):
    return dot(a, b, 0, 0, precision)


def softmax(scores):
    top = jnp.max(scores, axis=-1, keepdims=True)
    weights = jnp.exp(scores - top)
    return weights / jnp.sum(weights, axis=-1, keepdims=True)


def remote(source, target, send, receive, dp, tensor):
    return pltpu.make_async_remote_copy(
        src_ref=source,
        dst_ref=target,
        send_sem=send,
        recv_sem=receive,
        device_id=(dp, tensor),
        device_id_type=MESH,
    )


def kernel(*refs):
    names = INPUTS + [n + "_out" for n in OUTPUTS] + list(BUFFERS) + list(SEMAPHORES)
    r = types.SimpleNamespace(**dict(zip(names, refs, strict=True)))

    d = lax.axis_index("dp")
    t = lax.axis_index("tensor")
    zl = lax.div(d, 16)
    xy = lax.rem(d, 16)
    x = lax.div(xy, 4)
    y = lax.rem(xy, 4)
    zh = lax.div(t, 2)
    c = lax.rem(t, 2)
    mate = t + 1 - 2 * c
    other = (1 - zl) * 16 + xy
    pending = []

    def start(copy):
        copy.start()
        pending.append(copy)

    def turn(base, k, size):
        return lax.rem(base + k, size)

    def plane(xx, yy):
        return zl * 16 + xx * 4 + yy

    def arrived(slot, semaphore):
        remote(slot, slot, semaphore, semaphore, other, t).wait_recv()

    def all_arrived(buffer, semaphore):
        most = buffer.at[pl.ds(0, 31)]
        remote(most, most, semaphore, semaphore, other, t).wait_recv()

    def all_left(buffer, semaphore):
        most = buffer.at[pl.ds(0, 31)]
        remote(most, most, semaphore, semaphore, other, t).wait_send()

    def over_dp(body):
        def step(k, carry):
            body(k, turn(d, k, 32))
            return carry

        lax.fori_loop(1, 32, step, 0)

    loads = [
        pltpu.make_async_copy(r.eq, r.w_qkv.at[:, pl.ds(0, 512)], r.load.at[0]),
        pltpu.make_async_copy(r.ek, r.w_qkv.at[:, pl.ds(512, 128)], r.load.at[1]),
        pltpu.make_async_copy(r.ev, r.w_qkv.at[:, pl.ds(640, 128)], r.load.at[2]),
        pltpu.make_async_copy(r.eo, r.w_out, r.load.at[3]),
    ]
    for load in loads:
        load.start()

    barrier = pltpu.get_barrier_semaphore()

    def signal(dp, tensor):
        pl.semaphore_signal(barrier, inc=1, device_id=(dp, tensor), device_id_type=MESH)

    over_dp(lambda k, peer: signal(peer, t))
    signal(d, mate)
    for k in (1, 2, 3):
        signal(d, turn(zh, k, 4) * 2 + c)
        signal(other, turn(zh, k, 4) * 2 + c)

    r.gx[t] = r.states[0]
    wk_v = r.wk[...]
    wv_v = r.wv[...]
    for half in (0, 1):
        r.wkv[xy, half, :, 0:256] = wk_v[64 * half : 64 * half + 64]
        r.wkv[xy, half, :, 256:512] = wv_v[64 * half : 64 * half + 64]
    w_in_v = r.w_in[...]
    w_in_t = w_in_v.astype(F32)
    decay = -math.log(10000.0) / 1024.0
    step_f = jnp.full((8, 128), r.step_index[0], jnp.int32).astype(F32)
    place = (
        lax.broadcasted_iota(jnp.int32, (8, 128), 0) * 128
        + lax.broadcasted_iota(jnp.int32, (8, 128), 1)
    ).astype(F32)
    all_angles = step_f * jnp.exp(decay * place)
    all_cos = jnp.cos(all_angles)
    all_sin = jnp.sin(all_angles)

    def total(tile):
        return jnp.sum(jnp.sum(tile, axis=1, keepdims=True), axis=0, keepdims=True)

    own_mean = total(all_cos + all_sin) / 2048.0
    time_square = total((all_cos - own_mean) ** 2 + (all_sin - own_mean) ** 2)
    lane = lax.broadcasted_iota(jnp.int32, (1, 128), 1)
    r.c0[d, :, 0:256] = jnp.sum(w_in_t, axis=0, keepdims=True)
    r.c0[d, :, 256:384] = jnp.where(lane == 0, step_f[0:1], own_mean)

    vel_v = r.vel[...]
    wq_v = r.wq[...]
    part_m = tn(r.wo[...], vel_v).reshape(32, 8, 256)
    part_b = tn(w_in_v, vel_v)

    pl.semaphore_wait(barrier, 38)

    for k in (2, 1, 3):
        start(remote(r.gx.at[t], r.gx.at[t], r.gx_s.at[k], r.gx_r.at[t], d, turn(zh, k, 4) * 2 + c))
    start(remote(r.gx.at[t], r.gx.at[t], r.gx_s.at[0], r.gx_r.at[t], d, mate))

    def wkv_send(slot, half, dp, index):
        ref = r.wkv.at[slot, half]
        start(remote(ref, ref, r.wkv_s.at[index], r.wkv_r.at[slot, half], dp, t))

    for k in (1, 3, 2):
        wkv_send(xy, 0, plane(turn(x, k, 4), y), k - 1)
        wkv_send(xy, 1, plane(x, turn(y, k, 4)), 2 + k)

    def c0_copy(k, peer):
        return remote(r.c0.at[d], r.c0.at[d], r.c0_s.at[0], r.c0_r.at[0], peer, t)

    over_dp(lambda k, peer: c0_copy(k, peer).start())

    def wkv_second(first, k_list):
        for k in k_list:
            if k:
                slot = turn(x, k, 4) * 4 + y
                arrived(r.wkv.at[slot, 0], r.wkv_r.at[slot, 0])
                slot = x * 4 + turn(y, k, 4)
                arrived(r.wkv.at[slot, 1], r.wkv_r.at[slot, 1])
            for j in (1, 3, 2):
                wkv_send(turn(x, k, 4) * 4 + y, 0, plane(x, turn(y, j, 4)), first + 6 * k + j - 1)
                wkv_send(
                    x * 4 + turn(y, k, 4), 1, plane(turn(x, j, 4), y), first + 6 * k + 2 + j
                )

    wkv_second(6, (0, 1, 3, 2))

    for load in loads[:3]:
        load.wait()

    def project(slot, sums, square):
        chunk = r.gx[slot].astype(F32)
        square = square + jnp.sum(chunk * chunk, axis=1, keepdims=True)
        row = pl.multiple_of(slot * 512, 512)
        scaled = (chunk * r.gain[slot]).astype(BF16)
        return sums + nn(scaled, r.w_qkv[pl.ds(row, 512), :]), square

    sums, square = project(t, jnp.zeros((64, 768), F32), jnp.zeros((64, 1), F32))
    for k in (1, 3, 2):
        slot = turn(zh, k, 4) * 2 + c
        arrived(r.gx.at[slot], r.gx_r.at[slot])
        start(remote(r.gx.at[slot], r.gx.at[slot], r.gx_s.at[4 + k], r.gx_r.at[slot], d, mate))
        sums, square = project(slot, sums, square)

    arrived(r.gx.at[mate], r.gx_r.at[mate])
    sums, square = project(mate, sums, square)
    for k in (1, 3, 2):
        slot = turn(zh, k, 4) * 2 + (1 - c)
        arrived(r.gx.at[slot], r.gx_r.at[slot])
        sums, square = project(slot, sums, square)

    length = r.cap_len[0]
    rms = lax.rsqrt(square / 4096.0 + EPSILON)
    sums = sums * rms
    cosine = r.cosine[...]
    sine = r.sine[...]

    def turned(vectors, scaling):
        mean = jnp.mean(vectors * vectors, axis=1, keepdims=True)
        vectors = vectors * lax.rsqrt(mean + EPSILON) * scaling
        return (vectors * cosine + pltpu.roll(vectors, 64, 1) * sine).astype(BF16)

    q_gain = r.q_gain[...]
    queries = jnp.concatenate(
        [turned(sums[:, 128 * h : 128 * h + 128], q_gain) for h in range(4)], axis=0
    )
    keys = turned(sums[:, 512:640], r.k_gain[...])
    values = sums[:, 640:768].astype(BF16)
    scores = nt(queries, keys) * SCALE
    row = lax.rem(lax.broadcasted_iota(jnp.int32, (256, 64), 0), 64)
    col = lax.broadcasted_iota(jnp.int32, (256, 64), 1)
    scores = jnp.where((col <= row) & (col < length), scores, -1e30)
    mixed = nn(softmax(scores).astype(BF16), values).astype(BF16)
    mixed = jnp.concatenate([mixed[64 * h : 64 * h + 64] for h in range(4)], axis=1)

    loads[3].wait()
    for k in (1, 3, 2, 0):
        slot = turn(zh, k, 4)
        column = pl.multiple_of((slot * 2 + 1 - c) * 512, 512)
        r.ra_send[slot] = nn(mixed, r.w_out[:, pl.ds(column, 512)]).astype(BF16)
        start(
            remote(
                r.ra_send.at[slot], r.ra_recv.at[slot], r.ra_s.at[k], r.ra_r.at[slot], d, mate
            )
        )
    for k in (1, 3, 2, 0):
        slot = turn(zh, k, 4)
        column = pl.multiple_of((slot * 2 + c) * 512, 512)
        r.r_own[slot] = nn(mixed, r.w_out[:, pl.ds(column, 512)])
    for k in (2, 1, 3):
        slot = turn(zh, k, 4)
        arrived(r.ra_recv.at[slot], r.ra_r.at[slot])
        r.rb_send[slot] = (r.r_own[slot] + r.ra_recv[slot].astype(F32)).astype(BF16)
        start(
            remote(
                r.rb_send.at[slot], r.rb_recv.at[zh], r.rb_s.at[k], r.rb_r.at[zh], d, slot * 2 + c
            )
        )

    all_arrived(r.c0, r.c0_r.at[0])
    facts = r.c0[...].reshape(32, 384)
    w_mean = jnp.sum(facts[:, 0:256], axis=0, keepdims=True) / 2048.0
    steps = facts[:, 256:257]
    step_means = facts[:, 257:258]
    column = (
        lax.broadcasted_iota(jnp.int32, (1, 64), 1) + lax.rem(d, 16) * 64
    ).astype(F32)
    angles = steps * jnp.exp(decay * column)
    cos_part = jnp.full((32, 64), zl, jnp.int32) == 0
    times = jnp.where(cos_part, jnp.cos(angles), jnp.sin(angles))
    times_c = times - step_means
    w_c = w_in_t - w_mean
    part_a = tn(w_c.astype(BF16), wq_v).reshape(32, 8, 256)
    r.zsb[...] = jnp.concatenate([part_a, part_m], axis=1).astype(BF16)
    first_core = jnp.full((256, 256), c, jnp.int32) == 0
    part_f = jnp.where(first_core, part_b, tn(w_c, w_c, HIGHEST))
    r.zsf[:, :, 0:256] = part_f.reshape(32, 8, 256)
    time_rows = jnp.concatenate(
        [
            nn(times_c, wq_v.astype(F32), HIGHEST),
            nn(times, vel_v.astype(F32), HIGHEST),
            nn(times_c, w_c, HIGHEST),
        ],
        axis=1,
    )
    for i in range(8):
        part = time_rows[:, 128 * i : 128 * i + 128] if i < 6 else jnp.zeros((32, 128), F32)
        r.zsf[:, i, 256:384] = part
    r.zrb[d] = r.zsb[d]
    r.zrf[d] = r.zsf[d]

    def z_copies(k, peer):
        return (
            remote(r.zsb.at[peer], r.zrb.at[d], r.zb_s.at[0], r.zb_r.at[0], peer, t),
            remote(r.zsf.at[peer], r.zrf.at[d], r.zf_s.at[0], r.zf_r.at[0], peer, t),
        )

    def z_start(k, peer):
        for copy in z_copies(k, peer):
            copy.start()

    over_dp(z_start)

    slot = zh
    arrived(r.ra_recv.at[slot], r.ra_r.at[slot])
    own = r.r_own[slot] + r.ra_recv[slot].astype(F32)
    for k in (1, 3, 2):
        slot = turn(zh, k, 4)
        arrived(r.rb_recv.at[slot], r.rb_r.at[slot])
        own = own + r.rb_recv[slot].astype(F32)
    r.cap_own[...] = (r.states[0].astype(F32) + own).astype(BF16)

    target = lax.div(zh, 2)
    mine = lax.rem(t, 4)
    inside = target == zl

    def cap_copy(k):
        return remote(
            r.cap_own,
            r.caps.at[mine, zl],
            r.cp_s.at[k],
            r.cp_r.at[mine, zl],
            target * 16 + xy,
            turn(zh, k, 4) * 2 + c,
        )

    for k in (2, 1, 3):
        start(cap_copy(k))

    @pl.when(inside)
    def _():
        r.caps[mine, zl] = r.cap_own[...]

    @pl.when(jnp.logical_not(inside))
    def _():
        cap_copy(0).start()

    all_arrived(r.zrb, r.zb_r.at[0])
    all_arrived(r.zrf, r.zf_r.at[0])
    r.agb[d] = jnp.sum(r.zrb[...].astype(F32), axis=0).astype(BF16)
    slabs = jnp.sum(r.zrf[...], axis=0)
    r.agf[c, d] = slabs[:, 0:256]
    time_own = jnp.concatenate([slabs[i : i + 1, 256:384] for i in range(6)], axis=1)

    def a_copies(k, peer):
        return (
            remote(r.agb.at[d], r.agb.at[d], r.ab_s.at[0], r.ab_r.at[0], peer, t),
            remote(r.agf.at[c, d], r.agf.at[c, d], r.af_s.at[0], r.af_r.at[0], peer, t),
        )

    def a_start(k, peer):
        for copy in a_copies(k, peer):
            copy.start()

    over_dp(a_start)

    for k in (0, 1, 2, 3):
        for j in (1, 2, 3):
            slot = turn(x, k, 4) * 4 + turn(y, j, 4)
            arrived(r.wkv.at[slot, 0], r.wkv_r.at[slot, 0])
            slot = turn(x, j, 4) * 4 + turn(y, k, 4)
            arrived(r.wkv.at[slot, 1], r.wkv_r.at[slot, 1])

    forwards = []
    for z in (0, 1):
        for near in (0, 1):
            chunk = near * 2 + c
            ref = r.caps.at[chunk, z]
            own_slot = inside & (chunk == mine) & (z == zl)

            @pl.when(jnp.logical_not(own_slot))
            def _(ref=ref, chunk=chunk, z=z):
                arrived(ref, r.cp_r.at[chunk, z])

            start(remote(ref, ref, r.cp_s.at[4 + 2 * z + near], r.cp_r.at[chunk, z], d, mate))

    def project_caption(chunk):
        rows = r.caps[chunk].reshape(128, 512)
        weights = r.wkv[pl.ds(chunk * 4, 4)].reshape(512, 512)
        return nn(rows, weights)

    both = project_caption(c) + project_caption(2 + c)
    for near in (0, 1):
        for z in (0, 1):
            chunk = near * 2 + 1 - c
            arrived(r.caps.at[chunk, z], r.cp_r.at[chunk, z])
        both = both + project_caption(near * 2 + 1 - c)
    second = jnp.full((64, 512), zl, jnp.int32) == 1
    r.kvx_send[...] = jnp.where(second, both[0:64], both[64:128]).astype(BF16)
    start(remote(r.kvx_send, r.kvx_recv, r.kvx_s.at[0], r.kvx_r.at[0], other, t))

    r.cap_k[x] = r.caps[x]
    for q in range(4):
        column = pl.multiple_of(y * 128, 128)
        r.cap_v[y, q] = r.caps[q, :, :, pl.ds(column, 128)]
    for k in (1, 3, 2):
        xx = turn(x, k, 4)
        start(
            remote(r.caps.at[xx], r.cap_k.at[x], r.ck_s.at[k], r.ck_r.at[x], plane(xx, y), t)
        )
        yy = turn(y, k, 4)
        column = pl.multiple_of(yy * 128, 128)
        start(
            remote(
                r.caps.at[:, :, :, pl.ds(column, 128)],
                r.cap_v.at[y],
                r.cv_s.at[k],
                r.cv_r.at[y],
                plane(x, yy),
                t,
            )
        )

    clean = r.clean[0].astype(F32)
    noise = r.noise[0].astype(F32)
    tau = jnp.full((1, 256), r.step_index[0], jnp.int32).astype(F32) / STEPS
    margin = jnp.zeros((PADDED - FRAMES, 256), F32)
    blend_f = jnp.concatenate([(1.0 - tau) * clean + tau * noise, margin], axis=0)
    r.blend[...] = blend_f.astype(BF16)
    blend = r.blend[...]
    blend_f = blend.astype(F32)
    all_arrived(r.agb, r.ab_r.at[0])
    all_arrived(r.agf.at[c], r.af_r.at[0])
    start(remote(r.agf.at[c], r.agf.at[c], r.ap_s.at[0], r.ap_r.at[0], d, mate))
    matrices = r.agb[...].astype(F32)
    mat_a = matrices[:, 0:8].reshape(256, 256).astype(BF16)
    mat_m = matrices[:, 8:16].reshape(256, 256).astype(BF16)
    arrived(r.agf.at[1 - c], r.ap_r.at[0])
    mat_b = r.agf[0].reshape(256, 256)
    mat_s = r.agf[1].reshape(256, 256)
    r.hid_v[...] = nn(blend_f, mat_b, HIGHEST) + time_own[:, 256:512]
    spread = (nn(blend_f, mat_s, HIGHEST) + 2.0 * time_own[:, 512:768]) * blend_f
    variance = (jnp.sum(spread, axis=1, keepdims=True) + time_square) / 2048.0
    rstd = lax.rsqrt(jnp.maximum(variance, 0.0) + EPSILON)
    r.query[...] = ((nn(blend, mat_a) + time_own[:, 0:256]) * rstd).astype(BF16)

    kv_own = jnp.where(second, both[64:128], both[0:64])
    arrived(r.kvx_recv, r.kvx_r.at[0])
    kv = (kv_own + r.kvx_recv[...].astype(F32)).astype(BF16)

    query = r.query[...]
    allowed = lax.broadcasted_iota(jnp.int32, (PADDED, 64), 1) < length
    probs = []
    attended = []
    for h in (0, 1):
        span = slice(128 * h, 128 * h + 128)
        scores = nt(query[:, span], kv[:, span]) * SCALE
        prob = softmax(jnp.where(allowed, scores, -1e30))
        probs.append(prob)
        attended.append(nn(prob.astype(BF16), kv[:, 256 + 128 * h : 384 + 128 * h]).astype(BF16))
    attended = jnp.concatenate(attended, axis=1)
    branch = nn(attended, mat_m).reshape(8, 48, 256)

    first_half = jnp.full((48, 256), c, jnp.int32) == 0
    for q in range(4):
        r.va_send[q] = jnp.where(first_half, branch[2 * q + 1], branch[2 * q]).astype(BF16)
        r.v_own[q] = jnp.where(first_half, branch[2 * q], branch[2 * q + 1])
    start(remote(r.va_send, r.va_recv, r.va_s.at[0], r.va_r.at[0], d, mate))
    r.att_t[...] = attended.T
    for h in (0, 1):
        r.prob_t[h] = probs[h].astype(BF16).T
    arrived(r.va_recv, r.va_r.at[0])
    for k in (2, 1, 3):
        slot = turn(zh, k, 4)
        r.vb_send[slot] = (r.v_own[slot] + r.va_recv[slot].astype(F32)).astype(BF16)
        start(
            remote(
                r.vb_send.at[slot], r.vb_recv.at[zh], r.vb_s.at[k], r.vb_r.at[zh], d, slot * 2 + c
            )
        )
    r.blend_t[...] = blend.T
    for k in (1, 3, 2):
        slot = turn(x, k, 4)
        arrived(r.cap_k.at[slot], r.ck_r.at[slot])
    r.cap_kt[...] = r.cap_k[...].reshape(512, 512).T
    own = r.v_own[zh] + r.va_recv[zh].astype(F32)
    for k in (1, 3, 2):
        slot = turn(zh, k, 4)
        arrived(r.vb_recv.at[slot], r.vb_r.at[slot])
        own = own + r.vb_recv[slot].astype(F32)
    r.vg[t] = own.astype(BF16)
    for k in (2, 1, 3):
        start(remote(r.vg.at[t], r.vg.at[t], r.vg_s.at[k], r.vg_r.at[t], d, turn(zh, k, 4) * 2 + c))
    start(remote(r.vg.at[t], r.vg.at[t], r.vg_s.at[0], r.vg_r.at[t], d, mate))
    for k in (1, 3, 2):
        slot = turn(y, k, 4)
        arrived(r.cap_v.at[slot], r.cv_r.at[slot])
    for q in range(4):
        r.cap_vt[q] = r.cap_v[:, q].reshape(512, 128).T
    for k in (1, 3, 2):
        slot = turn(zh, k, 4) * 2 + c
        arrived(r.vg.at[slot], r.vg_r.at[slot])
        start(remote(r.vg.at[slot], r.vg.at[slot], r.vg_s.at[4 + k], r.vg_r.at[slot], d, mate))
    arrived(r.vg.at[mate], r.vg_r.at[mate])
    for k in (1, 3, 2):
        slot = turn(zh, k, 4) * 2 + 1 - c
        arrived(r.vg.at[slot], r.vg_r.at[slot])

    predicted = r.hid_v[...] + r.vg[...].astype(F32).reshape(PADDED, 256)
    residual = predicted - jnp.concatenate([noise - clean, margin], axis=0)
    frames = jnp.full((PADDED, 1), r.motion_len[0], jnp.int32)
    live = lax.broadcasted_iota(jnp.int32, (PADDED, 1), 0) < frames
    row_weight = jnp.where(live, 1.0 / frames.astype(F32), 0.0)
    weighted = residual * row_weight
    loss_part = total(residual * weighted)
    d_vel = (2.0 * weighted).astype(BF16)
    d_att = nt(d_vel, mat_m).astype(BF16)

    heads = [d_att[:, 128 * h : 128 * h + 128] for h in (0, 1)]
    d_values = [nn(r.prob_t[h], heads[h]) for h in (0, 1)]
    r.dkx[1, zl] = jnp.concatenate(d_values, axis=1).astype(BF16)

    def dx_start(i):
        ref = r.dkx.at[i, zl]
        start(remote(ref, ref, r.dx_s.at[i], r.dx_r.at[i], other, t))

    dx_start(1)
    d_scores = []
    for h in (0, 1):
        d_prob = nt(heads[h], kv[:, 256 + 128 * h : 384 + 128 * h])
        delta = jnp.sum(probs[h] * d_prob, axis=1, keepdims=True)
        d_scores.append((probs[h] * (d_prob - delta) * SCALE).astype(BF16))
    d_keys = [tn(d_scores[h], query[:, 128 * h : 128 * h + 128]) for h in (0, 1)]
    r.dkx[0, zl] = jnp.concatenate(d_keys, axis=1).astype(BF16)
    dx_start(0)
    d_queries = [nn(d_scores[h], kv[:, 128 * h : 128 * h + 128]) for h in (0, 1)]
    d_query = jnp.concatenate(d_queries, axis=1).astype(BF16).astype(F32) * rstd
    mat_h = nn(r.blend_t[...], d_query.astype(BF16)).reshape(32, 8, 256)
    mat_g = nn(r.att_t[...], d_vel).reshape(32, 8, 256)
    r.hs[:, :, 0:256] = jnp.concatenate([mat_h, mat_g], axis=1).astype(BF16)
    frame_sum = jnp.sum(d_query, axis=0, keepdims=True)
    loss_high = loss_part.astype(BF16).astype(F32)
    which = lax.broadcasted_iota(jnp.int32, (16, 128), 0)
    extra = jnp.where(which == 2, loss_high, loss_part - loss_high)
    extra = jnp.where(which == 1, frame_sum[:, 128:256], extra)
    extra = jnp.where(which == 0, frame_sum[:, 0:128], extra)
    r.hs[:, :, 256:384] = jnp.broadcast_to(extra.astype(BF16)[None], (32, 16, 128))
    r.hr[d] = r.hs[d]

    def h_copy(k, peer):
        return remote(r.hs.at[peer], r.hr.at[d], r.hs_s.at[0], r.hs_r.at[0], peer, t)

    over_dp(lambda k, peer: h_copy(k, peer).start())

    arrived(r.dkx.at[1, 1 - zl], r.dx_r.at[1])
    r.dv[y] = r.dkx[1]
    for k in (1, 3, 2):
        start(
            remote(
                r.dv.at[y], r.dv.at[y], r.dv_s.at[k], r.dv_r.at[y], plane(x, turn(y, k, 4)), t
            )
        )
    arrived(r.dkx.at[0, 1 - zl], r.dx_r.at[0])
    r.dk[x] = r.dkx[0]
    for k in (1, 3, 2):
        start(
            remote(
                r.dk.at[x], r.dk.at[x], r.dk_s.at[k], r.dk_r.at[x], plane(turn(x, k, 4), y), t
            )
        )

    all_arrived(r.hr, r.hs_r.at[0])
    arrivals = r.hr[...].astype(F32)
    r.hg[d] = jnp.sum(arrivals[:, :, 0:256], axis=0).astype(BF16)

    def g_copy(k, peer):
        return remote(r.hg.at[d], r.hg.at[d], r.hg_s.at[0], r.hg_r.at[0], peer, t)

    over_dp(lambda k, peer: g_copy(k, peer).start())

    for k in (1, 3, 2):
        slot = turn(y, k, 4)
        arrived(r.dv.at[slot], r.dv_r.at[slot])
    all_v = r.dv[...].reshape(512, 256)
    for q in range(4):
        r.gv_send[q] = nn(r.cap_vt[q], all_v).astype(BF16)
    for k in (1, 3, 2):
        xx = turn(x, k, 4)
        start(
            remote(
                r.gv_send.at[xx], r.gv_recv.at[x], r.gv_s.at[k], r.gv_r.at[x], plane(xx, y), t
            )
        )
    r.gv_recv[x] = r.gv_send[x]
    for k in (1, 3, 2):
        slot = turn(x, k, 4)
        arrived(r.dk.at[slot], r.dk_r.at[slot])
    all_k = r.dk[...].reshape(512, 256)
    grad_k = nn(r.cap_kt[...], all_k).reshape(4, 128, 256)
    for q in range(4):
        r.gk_send[q] = grad_k[q].astype(BF16)
    for k in (1, 3, 2):
        yy = turn(y, k, 4)
        start(
            remote(
                r.gk_send.at[yy], r.gk_recv.at[y], r.gk_s.at[k], r.gk_r.at[y], plane(x, yy), t
            )
        )
    r.gk_recv[y] = r.gk_send[y]

    sums_p = jnp.concatenate([arrivals[:, 0, 256:384], arrivals[:, 1, 256:384]], axis=1)
    losses = arrivals[:, 2, 256:384] + arrivals[:, 3, 256:384]
    r.loss_out[...] = jnp.sum(losses, axis=0, keepdims=True) / 8192.0
    all_arrived(r.hg, r.hg_r.at[0])
    grads = r.hg[...].astype(F32)
    sum_h = grads[:, 0:8].reshape(256, 256)
    sum_g = grads[:, 8:16].reshape(256, 256).astype(BF16)
    r.packed_out[0:64] = nn(w_c, sum_h, HIGHEST) + tn(times_c, sums_p, HIGHEST)
    r.packed_out[320:384] = nt(r.vel[...], sum_g)
    for k in (1, 3, 2):
        slot = turn(y, k, 4)
        arrived(r.gk_recv.at[slot], r.gk_r.at[slot])
        slot = turn(x, k, 4)
        arrived(r.gv_recv.at[slot], r.gv_r.at[slot])
    r.packed_out[64:192] = jnp.sum(r.gk_recv[...].astype(F32), axis=0)
    r.packed_out[192:320] = jnp.sum(r.gv_recv[...].astype(F32), axis=0)

    for copy in pending:
        copy.wait_send()

    @pl.when(jnp.logical_not(inside))
    def _():
        cap_copy(0).wait_send()

    all_left(r.c0, r.c0_s.at[0])
    all_left(r.zrb, r.zb_s.at[0])
    all_left(r.zrf, r.zf_s.at[0])
    all_left(r.agb, r.ab_s.at[0])
    all_left(r.agf.at[c], r.af_s.at[0])
    all_left(r.hr, r.hs_s.at[0])
    all_left(r.hg, r.hg_s.at[0])


def unpack(loss, packed, loss_out, gq, gk, gv, go):
    loss_out[...] = loss[...]
    gq[...] = packed[0:64]
    gk[...] = packed[64:192]
    gv[...] = packed[192:320]
    go[...] = packed[320:384]


def rope_tables():
    inverse = 1000000.0 ** (-(np.arange(64, dtype=np.float32) * 2.0 / 128))
    angles = np.arange(64, dtype=np.float32)[:, None] * inverse[None, :].astype(np.float32)
    angles = np.concatenate([angles, angles], axis=1).astype(np.float32)
    sign = np.where(np.arange(128) < 64, -1.0, 1.0)[None, :]
    return np.cos(angles).astype(np.float32), (np.sin(angles) * sign).astype(np.float32)


def local(
    encoder_input_states,
    caption_lengths,
    encoder_input_gain,
    query_head_gain,
    key_head_gain,
    encoder_query_weight,
    encoder_key_weight,
    encoder_value_weight,
    encoder_output_weight,
    clean_motion,
    noise,
    timestep_index,
    motion_lengths,
    input_weight,
    velocity_weight,
    cross_query_weight,
    cross_key_weight,
    cross_value_weight,
    cross_output_weight,
):
    vmem = pl.BlockSpec(memory_space=pltpu.VMEM)
    hbm = pl.BlockSpec(memory_space=pl.ANY)
    smem = pl.BlockSpec(memory_space=pltpu.SMEM)
    spec = {name: vmem for name in INPUTS}
    for name in ("cap_len", "step_index", "motion_len"):
        spec[name] = smem
    for name in ("eq", "ek", "ev", "eo"):
        spec[name] = hbm
    cosine, sine = rope_tables()
    packed = pl.pallas_call(
        kernel,
        out_shape=[
            jax.ShapeDtypeStruct((1, 128), F32),
            jax.ShapeDtypeStruct((384, 256), F32),
        ],
        in_specs=[spec[name] for name in INPUTS],
        out_specs=[vmem] * 2,
        scratch_shapes=[pltpu.VMEM(shape, kind) for shape, kind in BUFFERS.values()]
        + [
            pltpu.SemaphoreType.DMA(shape if isinstance(shape, tuple) else (shape,))
            for shape in SEMAPHORES.values()
        ],
        compiler_params=pltpu.CompilerParams(
            collective_id=0, has_side_effects=True, vmem_limit_bytes=56 * 2**20
        ),
        name="motion_block",
    )(
        encoder_input_states,
        caption_lengths,
        timestep_index,
        motion_lengths,
        encoder_input_gain.reshape(8, 1, 512),
        query_head_gain.reshape(1, 128),
        key_head_gain.reshape(1, 128),
        jnp.asarray(cosine),
        jnp.asarray(sine),
        encoder_query_weight,
        encoder_key_weight,
        encoder_value_weight,
        encoder_output_weight,
        clean_motion,
        noise,
        input_weight.T,
        velocity_weight,
        cross_query_weight,
        cross_key_weight,
        cross_value_weight,
        cross_output_weight.T,
    )
    loss, gq, gk, gv, go = pl.pallas_call(
        unpack,
        out_shape=[
            jax.ShapeDtypeStruct((1, 128), F32),
            jax.ShapeDtypeStruct((64, 256), F32),
            jax.ShapeDtypeStruct((128, 256), F32),
            jax.ShapeDtypeStruct((128, 256), F32),
            jax.ShapeDtypeStruct((64, 256), F32),
        ],
        in_specs=[vmem] * 2,
        out_specs=[vmem] * 5,
        name="unpack",
    )(*packed)
    return (loss[0, 0], gq, gk, gv, go.T)


def solution(mesh):
    placed = (
        P("dp", None, "tensor"),
        P("dp"),
        P(),
        P(),
        P(),
        P(None, "tensor"),
        P(None, "tensor"),
        P(None, "tensor"),
        P("tensor", None),
        P("dp", None, None),
        P("dp", None, None),
        P("dp"),
        P("dp"),
        P(None, "dp"),
        P("dp", None),
        P("dp", "tensor"),
        P("dp", "tensor"),
        P("dp", "tensor"),
        P("tensor", "dp"),
    )
    return jax.shard_map(
        local,
        mesh=mesh,
        in_specs=placed,
        out_specs=(P(), P("dp", "tensor"), P("dp", "tensor"), P("dp", "tensor"), P("tensor", "dp")),
        check_vma=False,
    )
```

```python
import math
import types

import jax
import jax.numpy as jnp
import numpy as np
from jax import lax
from jax.experimental import pallas as pl
from jax.experimental.pallas import tpu as pltpu
from jax.sharding import PartitionSpec as P

F32 = jnp.float32
BF16 = jnp.bfloat16
MESH = pl.DeviceIdType.MESH
HIGHEST = lax.Precision.HIGHEST
EPSILON = 1e-06
STEPS = 1000
FRAMES = 360
PADDED = 384
SCALE = 1.0 / math.sqrt(128)

INPUTS = [
    "states", "cap_len", "step_index", "motion_len", "gain", "q_gain", "k_gain", "cosine", "sine",
    "eq", "ek", "ev", "eo", "clean", "noise", "w_in", "vel", "wq", "wk", "wv", "wo",
]
OUTPUTS = ["loss", "packed"]

BUFFERS = dict(
    w_qkv=((4096, 768), BF16),
    w_out=((512, 4096), BF16),
    c0=((32, 1, 384), F32),
    gx=((8, 64, 512), BF16),
    wkv=((16, 2, 64, 512), BF16),
    zsb=((32, 16, 256), BF16),
    zrb=((32, 16, 256), BF16),
    zsf=((32, 8, 384), F32),
    zrf=((32, 8, 384), F32),
    agb=((32, 16, 256), BF16),
    agf=((2, 32, 8, 256), F32),
    ra_send=((4, 64, 512), BF16),
    ra_recv=((4, 64, 512), BF16),
    rb_send=((4, 64, 512), BF16),
    rb_recv=((4, 64, 512), BF16),
    r_own=((4, 64, 512), F32),
    cap_own=((64, 512), BF16),
    caps=((4, 2, 64, 512), BF16),
    kvx_send=((64, 512), BF16),
    kvx_recv=((64, 512), BF16),
    blend=((PADDED, 256), BF16),
    query=((PADDED, 256), BF16),
    hid_v=((PADDED, 256), F32),
    va_send=((4, 48, 256), BF16),
    va_recv=((4, 48, 256), BF16),
    v_own=((4, 48, 256), F32),
    vb_send=((4, 48, 256), BF16),
    vb_recv=((4, 48, 256), BF16),
    vg=((8, 48, 256), BF16),
    dkx=((2, 2, 64, 256), BF16),
    dk=((4, 2, 64, 256), BF16),
    dv=((4, 2, 64, 256), BF16),
    cap_k=((4, 2, 64, 512), BF16),
    cap_v=((4, 4, 2, 64, 128), BF16),
    cap_kt=((512, 512), BF16),
    cap_vt=((4, 128, 512), BF16),
    blend_t=((256, PADDED), BF16),
    att_t=((256, PADDED), BF16),
    prob_t=((2, 64, PADDED), BF16),
    gk_send=((4, 128, 256), BF16),
    gk_recv=((4, 128, 256), BF16),
    gv_send=((4, 128, 256), BF16),
    gv_recv=((4, 128, 256), BF16),
    hs=((32, 16, 256), BF16),
    hr=((32, 16, 256), BF16),
    gs=((32, 16, 128), BF16),
    gr=((32, 16, 128), BF16),
    hg=((32, 16, 256), BF16),
)

SEMAPHORES = dict(
    load=4,
    c0_s=1, c0_r=1,
    gx_s=8, gx_r=8,
    wkv_s=32, wkv_r=(16, 2),
    zb_s=1, zb_r=1, zf_s=1, zf_r=1,
    ab_s=1, ab_r=1, af_s=1, af_r=1, ap_s=1, ap_r=1,
    ra_s=4, ra_r=4, rb_s=4, rb_r=4,
    cp_s=8, cp_r=(4, 2),
    kvx_s=1, kvx_r=1,
    va_s=1, va_r=1, vb_s=4, vb_r=4, vg_s=8, vg_r=8,
    dx_s=2, dx_r=2, dk_s=4, dk_r=4, dv_s=4, dv_r=4,
    ck_s=4, ck_r=4, cv_s=4, cv_r=4,
    gk_s=4, gk_r=4, gv_s=4, gv_r=4,
    hs_s=1, hs_r=1, gs_s=1, gs_r=1, hg_s=1, hg_r=1,
)


def dot(a, b, left, right, precision=None):
    return lax.dot_general(
        a, b, (((left,), (right,)), ((), ())), precision=precision, preferred_element_type=F32
    )


def nn(a, b, precision=None):
    return dot(a, b, 1, 0, precision)


def nt(a, b, precision=None):
    return dot(a, b, 1, 1, precision)


def tn(a, b, precision=None):
    return dot(a, b, 0, 0, precision)


def softmax(scores):
    top = jnp.max(scores, axis=-1, keepdims=True)
    weights = jnp.exp(scores - top)
    return weights / jnp.sum(weights, axis=-1, keepdims=True)


def remote(source, target, send, receive, dp, tensor):
    return pltpu.make_async_remote_copy(
        src_ref=source,
        dst_ref=target,
        send_sem=send,
        recv_sem=receive,
        device_id=(dp, tensor),
        device_id_type=MESH,
    )


def kernel(*refs):
    names = INPUTS + [n + "_out" for n in OUTPUTS] + list(BUFFERS) + list(SEMAPHORES)
    r = types.SimpleNamespace(**dict(zip(names, refs, strict=True)))

    d = lax.axis_index("dp")
    t = lax.axis_index("tensor")
    zl = lax.div(d, 16)
    xy = lax.rem(d, 16)
    x = lax.div(xy, 4)
    y = lax.rem(xy, 4)
    zh = lax.div(t, 2)
    c = lax.rem(t, 2)
    mate = t + 1 - 2 * c
    other = (1 - zl) * 16 + xy
    pending = []

    def start(copy):
        copy.start()
        pending.append(copy)

    def turn(base, k, size):
        return lax.rem(base + k, size)

    def plane(xx, yy):
        return zl * 16 + xx * 4 + yy

    def arrived(slot, semaphore):
        remote(slot, slot, semaphore, semaphore, other, t).wait_recv()

    def all_arrived(buffer, semaphore):
        most = buffer.at[pl.ds(0, 31)]
        remote(most, most, semaphore, semaphore, other, t).wait_recv()

    def all_left(buffer, semaphore):
        most = buffer.at[pl.ds(0, 31)]
        remote(most, most, semaphore, semaphore, other, t).wait_send()

    def over_dp(body):
        def step(k, carry):
            body(k, turn(d, k, 32))
            return carry

        lax.fori_loop(1, 32, step, 0)

    loads = [
        pltpu.make_async_copy(r.eq, r.w_qkv.at[:, pl.ds(0, 512)], r.load.at[0]),
        pltpu.make_async_copy(r.ek, r.w_qkv.at[:, pl.ds(512, 128)], r.load.at[1]),
        pltpu.make_async_copy(r.ev, r.w_qkv.at[:, pl.ds(640, 128)], r.load.at[2]),
        pltpu.make_async_copy(r.eo, r.w_out, r.load.at[3]),
    ]
    for load in loads:
        load.start()

    barrier = pltpu.get_barrier_semaphore()

    def signal(dp, tensor):
        pl.semaphore_signal(barrier, inc=1, device_id=(dp, tensor), device_id_type=MESH)

    over_dp(lambda k, peer: signal(peer, t))
    signal(d, mate)
    for k in (1, 2, 3):
        signal(d, turn(zh, k, 4) * 2 + c)
        signal(other, turn(zh, k, 4) * 2 + c)

    r.gx[t] = r.states[0]
    wk_v = r.wk[...]
    wv_v = r.wv[...]
    for half in (0, 1):
        r.wkv[xy, half, :, 0:256] = wk_v[64 * half : 64 * half + 64]
        r.wkv[xy, half, :, 256:512] = wv_v[64 * half : 64 * half + 64]
    w_in_v = r.w_in[...]
    w_in_t = w_in_v.astype(F32)
    decay = -math.log(10000.0) / 1024.0
    step_f = jnp.full((8, 128), r.step_index[0], jnp.int32).astype(F32)
    place = (
        lax.broadcasted_iota(jnp.int32, (8, 128), 0) * 128
        + lax.broadcasted_iota(jnp.int32, (8, 128), 1)
    ).astype(F32)
    all_angles = step_f * jnp.exp(decay * place)
    all_cos = jnp.cos(all_angles)
    all_sin = jnp.sin(all_angles)

    def total(tile):
        return jnp.sum(jnp.sum(tile, axis=1, keepdims=True), axis=0, keepdims=True)

    own_mean = total(all_cos + all_sin) / 2048.0
    time_square = total((all_cos - own_mean) ** 2 + (all_sin - own_mean) ** 2)
    lane = lax.broadcasted_iota(jnp.int32, (1, 128), 1)
    r.c0[d, :, 0:256] = jnp.sum(w_in_t, axis=0, keepdims=True)
    r.c0[d, :, 256:384] = jnp.where(lane == 0, step_f[0:1], own_mean)

    vel_v = r.vel[...]
    wq_v = r.wq[...]
    part_m = tn(r.wo[...], vel_v).reshape(32, 8, 256)
    part_b = tn(w_in_v, vel_v)

    pl.semaphore_wait(barrier, 38)

    for k in (2, 1, 3):
        start(remote(r.gx.at[t], r.gx.at[t], r.gx_s.at[k], r.gx_r.at[t], d, turn(zh, k, 4) * 2 + c))
    start(remote(r.gx.at[t], r.gx.at[t], r.gx_s.at[0], r.gx_r.at[t], d, mate))

    def c0_copy(k, peer):
        return remote(r.c0.at[d], r.c0.at[d], r.c0_s.at[0], r.c0_r.at[0], peer, t)

    over_dp(lambda k, peer: c0_copy(k, peer).start())

    def wkv_send(slot, half, dp, index):
        ref = r.wkv.at[slot, half]
        start(remote(ref, ref, r.wkv_s.at[index], r.wkv_r.at[slot, half], dp, t))

    for k in (1, 3, 2):
        wkv_send(xy, 0, plane(turn(x, k, 4), y), k - 1)
        wkv_send(xy, 1, plane(x, turn(y, k, 4)), 2 + k)

    for load in loads[:3]:
        load.wait()

    def project(slot, sums, square):
        chunk = r.gx[slot].astype(F32)
        square = square + jnp.sum(chunk * chunk, axis=1, keepdims=True)
        row = pl.multiple_of(slot * 512, 512)
        scaled = (chunk * r.gain[slot]).astype(BF16)
        return sums + nn(scaled, r.w_qkv[pl.ds(row, 512), :]), square

    sums, square = project(t, jnp.zeros((64, 768), F32), jnp.zeros((64, 1), F32))

    all_arrived(r.c0, r.c0_r.at[0])
    facts = r.c0[...].reshape(32, 384)
    w_mean = jnp.sum(facts[:, 0:256], axis=0, keepdims=True) / 2048.0
    steps = facts[:, 256:257]
    step_means = facts[:, 257:258]
    column = (
        lax.broadcasted_iota(jnp.int32, (1, 64), 1) + lax.rem(d, 16) * 64
    ).astype(F32)
    angles = steps * jnp.exp(decay * column)
    quarter = jnp.full((32, 64), zl, jnp.int32).astype(F32) * (math.pi / 2.0)
    times = jnp.cos(angles - quarter)
    times_c = times - step_means
    w_c = w_in_t - w_mean
    part_a = tn(w_c.astype(BF16), wq_v).reshape(32, 8, 256)
    r.zsb[...] = jnp.concatenate([part_a, part_m], axis=1).astype(BF16)
    first_core = jnp.full((256, 256), c, jnp.int32) == 0
    part_f = jnp.where(first_core, part_b, tn(w_c, w_c, HIGHEST))
    r.zsf[:, :, 0:256] = part_f.reshape(32, 8, 256)
    time_rows = jnp.concatenate(
        [
            nn(times_c, wq_v.astype(F32), HIGHEST),
            nn(times, vel_v.astype(F32), HIGHEST),
            nn(times_c, w_c, HIGHEST),
        ],
        axis=1,
    )
    for i in range(8):
        part = time_rows[:, 128 * i : 128 * i + 128] if i < 6 else jnp.zeros((32, 128), F32)
        r.zsf[:, i, 256:384] = part
    r.zrb[d] = r.zsb[d]
    r.zrf[d] = r.zsf[d]

    def z_copies(k, peer):
        return (
            remote(r.zsb.at[peer], r.zrb.at[d], r.zb_s.at[0], r.zb_r.at[0], peer, t),
            remote(r.zsf.at[peer], r.zrf.at[d], r.zf_s.at[0], r.zf_r.at[0], peer, t),
        )

    def z_start(k, peer):
        for copy in z_copies(k, peer):
            copy.start()

    def wkv_second(first, k_list):
        for k in k_list:
            if k:
                slot = turn(x, k, 4) * 4 + y
                arrived(r.wkv.at[slot, 0], r.wkv_r.at[slot, 0])
                slot = x * 4 + turn(y, k, 4)
                arrived(r.wkv.at[slot, 1], r.wkv_r.at[slot, 1])
            for j in (1, 3, 2):
                wkv_send(turn(x, k, 4) * 4 + y, 0, plane(x, turn(y, j, 4)), first + 6 * k + j - 1)
                wkv_send(
                    x * 4 + turn(y, k, 4), 1, plane(turn(x, j, 4), y), first + 6 * k + 2 + j
                )

    wkv_second(6, (0, 1, 3, 2))

    for k in (1, 3, 2):
        slot = turn(zh, k, 4) * 2 + c
        arrived(r.gx.at[slot], r.gx_r.at[slot])
        start(remote(r.gx.at[slot], r.gx.at[slot], r.gx_s.at[4 + k], r.gx_r.at[slot], d, mate))
        sums, square = project(slot, sums, square)

    over_dp(z_start)

    arrived(r.gx.at[mate], r.gx_r.at[mate])
    sums, square = project(mate, sums, square)
    for k in (1, 3, 2):
        slot = turn(zh, k, 4) * 2 + (1 - c)
        arrived(r.gx.at[slot], r.gx_r.at[slot])
        sums, square = project(slot, sums, square)

    length = r.cap_len[0]
    rms = lax.rsqrt(square / 4096.0 + EPSILON)
    sums = sums * rms
    cosine = r.cosine[...]
    sine = r.sine[...]

    def turned(vectors, scaling):
        mean = jnp.mean(vectors * vectors, axis=1, keepdims=True)
        vectors = vectors * lax.rsqrt(mean + EPSILON) * scaling
        return (vectors * cosine + pltpu.roll(vectors, 64, 1) * sine).astype(BF16)

    q_gain = r.q_gain[...]
    queries = jnp.concatenate(
        [turned(sums[:, 128 * h : 128 * h + 128], q_gain) for h in range(4)], axis=0
    )
    keys = turned(sums[:, 512:640], r.k_gain[...])
    values = sums[:, 640:768].astype(BF16)
    scores = nt(queries, keys) * SCALE
    row = lax.rem(lax.broadcasted_iota(jnp.int32, (256, 64), 0), 64)
    col = lax.broadcasted_iota(jnp.int32, (256, 64), 1)
    scores = jnp.where((col <= row) & (col < length), scores, -1e30)
    mixed = nn(softmax(scores).astype(BF16), values).astype(BF16)
    mixed = jnp.concatenate([mixed[64 * h : 64 * h + 64] for h in range(4)], axis=1)

    loads[3].wait()
    for k in (1, 3, 2, 0):
        slot = turn(zh, k, 4)
        column = pl.multiple_of((slot * 2 + 1 - c) * 512, 512)
        r.ra_send[slot] = nn(mixed, r.w_out[:, pl.ds(column, 512)]).astype(BF16)
        start(
            remote(
                r.ra_send.at[slot], r.ra_recv.at[slot], r.ra_s.at[k], r.ra_r.at[slot], d, mate
            )
        )
    for k in (1, 3, 2, 0):
        slot = turn(zh, k, 4)
        column = pl.multiple_of((slot * 2 + c) * 512, 512)
        r.r_own[slot] = nn(mixed, r.w_out[:, pl.ds(column, 512)])
    for k in (2, 1, 3):
        slot = turn(zh, k, 4)
        arrived(r.ra_recv.at[slot], r.ra_r.at[slot])
        r.rb_send[slot] = (r.r_own[slot] + r.ra_recv[slot].astype(F32)).astype(BF16)
        start(
            remote(
                r.rb_send.at[slot], r.rb_recv.at[zh], r.rb_s.at[k], r.rb_r.at[zh], d, slot * 2 + c
            )
        )

    all_arrived(r.zrb, r.zb_r.at[0])
    all_arrived(r.zrf, r.zf_r.at[0])
    r.agb[d] = jnp.sum(r.zrb[...].astype(F32), axis=0).astype(BF16)
    slabs = jnp.sum(r.zrf[...], axis=0)
    r.agf[c, d] = slabs[:, 0:256]
    time_own = jnp.concatenate([slabs[i : i + 1, 256:384] for i in range(6)], axis=1)

    def a_copies(k, peer):
        return (
            remote(r.agb.at[d], r.agb.at[d], r.ab_s.at[0], r.ab_r.at[0], peer, t),
            remote(r.agf.at[c, d], r.agf.at[c, d], r.af_s.at[0], r.af_r.at[0], peer, t),
        )

    def a_start(k, peer):
        for copy in a_copies(k, peer):
            copy.start()

    over_dp(a_start)

    slot = zh
    arrived(r.ra_recv.at[slot], r.ra_r.at[slot])
    own = r.r_own[slot] + r.ra_recv[slot].astype(F32)
    for k in (1, 3, 2):
        slot = turn(zh, k, 4)
        arrived(r.rb_recv.at[slot], r.rb_r.at[slot])
        own = own + r.rb_recv[slot].astype(F32)
    r.cap_own[...] = (r.states[0].astype(F32) + own).astype(BF16)

    target = lax.div(zh, 2)
    mine = lax.rem(t, 4)
    inside = target == zl

    def cap_copy(k):
        return remote(
            r.cap_own,
            r.caps.at[mine, zl],
            r.cp_s.at[k],
            r.cp_r.at[mine, zl],
            target * 16 + xy,
            turn(zh, k, 4) * 2 + c,
        )

    for k in (2, 1, 3):
        start(cap_copy(k))

    @pl.when(inside)
    def _():
        r.caps[mine, zl] = r.cap_own[...]

    @pl.when(jnp.logical_not(inside))
    def _():
        cap_copy(0).start()

    for k in (0, 1, 2, 3):
        for j in (1, 2, 3):
            slot = turn(x, k, 4) * 4 + turn(y, j, 4)
            arrived(r.wkv.at[slot, 0], r.wkv_r.at[slot, 0])
            slot = turn(x, j, 4) * 4 + turn(y, k, 4)
            arrived(r.wkv.at[slot, 1], r.wkv_r.at[slot, 1])

    forwards = []
    for z in (0, 1):
        for near in (0, 1):
            chunk = near * 2 + c
            ref = r.caps.at[chunk, z]
            own_slot = inside & (chunk == mine) & (z == zl)

            @pl.when(jnp.logical_not(own_slot))
            def _(ref=ref, chunk=chunk, z=z):
                arrived(ref, r.cp_r.at[chunk, z])

            start(remote(ref, ref, r.cp_s.at[4 + 2 * z + near], r.cp_r.at[chunk, z], d, mate))

    def project_caption(chunk):
        rows = r.caps[chunk].reshape(128, 512)
        weights = r.wkv[pl.ds(chunk * 4, 4)].reshape(512, 512)
        return nn(rows, weights)

    both = project_caption(c) + project_caption(2 + c)
    for near in (0, 1):
        for z in (0, 1):
            chunk = near * 2 + 1 - c
            arrived(r.caps.at[chunk, z], r.cp_r.at[chunk, z])
        both = both + project_caption(near * 2 + 1 - c)
    second = jnp.full((64, 512), zl, jnp.int32) == 1
    r.kvx_send[...] = jnp.where(second, both[0:64], both[64:128]).astype(BF16)
    start(remote(r.kvx_send, r.kvx_recv, r.kvx_s.at[0], r.kvx_r.at[0], other, t))

    r.cap_k[x] = r.caps[x]
    for q in range(4):
        column = pl.multiple_of(y * 128, 128)
        r.cap_v[y, q] = r.caps[q, :, :, pl.ds(column, 128)]
    for k in (1, 3, 2):
        xx = turn(x, k, 4)
        start(
            remote(r.caps.at[xx], r.cap_k.at[x], r.ck_s.at[k], r.ck_r.at[x], plane(xx, y), t)
        )
        yy = turn(y, k, 4)
        column = pl.multiple_of(yy * 128, 128)
        start(
            remote(
                r.caps.at[:, :, :, pl.ds(column, 128)],
                r.cap_v.at[y],
                r.cv_s.at[k],
                r.cv_r.at[y],
                plane(x, yy),
                t,
            )
        )

    clean = r.clean[0].astype(F32)
    noise = r.noise[0].astype(F32)
    tau = jnp.full((1, 256), r.step_index[0], jnp.int32).astype(F32) / STEPS
    margin = jnp.zeros((PADDED - FRAMES, 256), F32)
    blend_f = jnp.concatenate([(1.0 - tau) * clean + tau * noise, margin], axis=0)
    r.blend[...] = blend_f.astype(BF16)
    blend = r.blend[...]
    blend_f = blend.astype(F32)
    all_arrived(r.agb, r.ab_r.at[0])
    all_arrived(r.agf.at[c], r.af_r.at[0])
    start(remote(r.agf.at[c], r.agf.at[c], r.ap_s.at[0], r.ap_r.at[0], d, mate))
    matrices = r.agb[...].astype(F32)
    mat_a = matrices[:, 0:8].reshape(256, 256).astype(BF16)
    mat_m = matrices[:, 8:16].reshape(256, 256).astype(BF16)
    arrived(r.agf.at[1 - c], r.ap_r.at[0])
    mat_b = r.agf[0].reshape(256, 256)
    mat_s = r.agf[1].reshape(256, 256)
    r.hid_v[...] = nn(blend_f, mat_b, HIGHEST) + time_own[:, 256:512]
    spread = (nn(blend_f, mat_s, HIGHEST) + 2.0 * time_own[:, 512:768]) * blend_f
    variance = (jnp.sum(spread, axis=1, keepdims=True) + time_square) / 2048.0
    rstd = lax.rsqrt(jnp.maximum(variance, 0.0) + EPSILON)
    r.query[...] = ((nn(blend, mat_a) + time_own[:, 0:256]) * rstd).astype(BF16)

    kv_own = jnp.where(second, both[64:128], both[0:64])
    arrived(r.kvx_recv, r.kvx_r.at[0])
    kv = (kv_own + r.kvx_recv[...].astype(F32)).astype(BF16)

    query = r.query[...]
    allowed = lax.broadcasted_iota(jnp.int32, (PADDED, 64), 1) < length
    probs = []
    attended = []
    for h in (0, 1):
        span = slice(128 * h, 128 * h + 128)
        scores = nt(query[:, span], kv[:, span]) * SCALE
        prob = softmax(jnp.where(allowed, scores, -1e30))
        probs.append(prob)
        attended.append(nn(prob.astype(BF16), kv[:, 256 + 128 * h : 384 + 128 * h]).astype(BF16))
    attended = jnp.concatenate(attended, axis=1)
    branch = nn(attended, mat_m).reshape(8, 48, 256)

    first_half = jnp.full((48, 256), c, jnp.int32) == 0
    for q in range(4):
        r.va_send[q] = jnp.where(first_half, branch[2 * q + 1], branch[2 * q]).astype(BF16)
        r.v_own[q] = jnp.where(first_half, branch[2 * q], branch[2 * q + 1])
    start(remote(r.va_send, r.va_recv, r.va_s.at[0], r.va_r.at[0], d, mate))
    r.att_t[...] = attended.T
    for h in (0, 1):
        r.prob_t[h] = probs[h].astype(BF16).T
    arrived(r.va_recv, r.va_r.at[0])
    for k in (2, 1, 3):
        slot = turn(zh, k, 4)
        r.vb_send[slot] = (r.v_own[slot] + r.va_recv[slot].astype(F32)).astype(BF16)
        start(
            remote(
                r.vb_send.at[slot], r.vb_recv.at[zh], r.vb_s.at[k], r.vb_r.at[zh], d, slot * 2 + c
            )
        )
    r.blend_t[...] = blend.T
    for k in (1, 3, 2):
        slot = turn(x, k, 4)
        arrived(r.cap_k.at[slot], r.ck_r.at[slot])
    r.cap_kt[...] = r.cap_k[...].reshape(512, 512).T
    own = r.v_own[zh] + r.va_recv[zh].astype(F32)
    for k in (1, 3, 2):
        slot = turn(zh, k, 4)
        arrived(r.vb_recv.at[slot], r.vb_r.at[slot])
        own = own + r.vb_recv[slot].astype(F32)
    r.vg[t] = own.astype(BF16)
    for k in (2, 1, 3):
        start(remote(r.vg.at[t], r.vg.at[t], r.vg_s.at[k], r.vg_r.at[t], d, turn(zh, k, 4) * 2 + c))
    start(remote(r.vg.at[t], r.vg.at[t], r.vg_s.at[0], r.vg_r.at[t], d, mate))
    for k in (1, 3, 2):
        slot = turn(y, k, 4)
        arrived(r.cap_v.at[slot], r.cv_r.at[slot])
    for q in range(4):
        r.cap_vt[q] = r.cap_v[:, q].reshape(512, 128).T
    for k in (1, 3, 2):
        slot = turn(zh, k, 4) * 2 + c
        arrived(r.vg.at[slot], r.vg_r.at[slot])
        start(remote(r.vg.at[slot], r.vg.at[slot], r.vg_s.at[4 + k], r.vg_r.at[slot], d, mate))
    arrived(r.vg.at[mate], r.vg_r.at[mate])
    for k in (1, 3, 2):
        slot = turn(zh, k, 4) * 2 + 1 - c
        arrived(r.vg.at[slot], r.vg_r.at[slot])

    predicted = r.hid_v[...] + r.vg[...].astype(F32).reshape(PADDED, 256)
    residual = predicted - jnp.concatenate([noise - clean, margin], axis=0)
    frames = jnp.full((PADDED, 1), r.motion_len[0], jnp.int32)
    live = lax.broadcasted_iota(jnp.int32, (PADDED, 1), 0) < frames
    row_weight = jnp.where(live, 1.0 / frames.astype(F32), 0.0)
    weighted = residual * row_weight
    loss_part = total(residual * weighted)
    d_vel = (2.0 * weighted).astype(BF16)
    d_att = nt(d_vel, mat_m).astype(BF16)

    heads = [d_att[:, 128 * h : 128 * h + 128] for h in (0, 1)]
    d_values = [nn(r.prob_t[h], heads[h]) for h in (0, 1)]
    r.dkx[1, zl] = jnp.concatenate(d_values, axis=1).astype(BF16)

    def dx_start(i):
        ref = r.dkx.at[i, zl]
        start(remote(ref, ref, r.dx_s.at[i], r.dx_r.at[i], other, t))

    dx_start(1)
    d_scores = []
    for h in (0, 1):
        d_prob = nt(heads[h], kv[:, 256 + 128 * h : 384 + 128 * h])
        delta = jnp.sum(probs[h] * d_prob, axis=1, keepdims=True)
        d_scores.append((probs[h] * (d_prob - delta) * SCALE).astype(BF16))
    d_keys = [tn(d_scores[h], query[:, 128 * h : 128 * h + 128]) for h in (0, 1)]
    r.dkx[0, zl] = jnp.concatenate(d_keys, axis=1).astype(BF16)
    dx_start(0)
    mat_g = nn(r.att_t[...], d_vel).reshape(32, 8, 256)
    halves = [mat_g[:, :, 0:128], mat_g[:, :, 128:256]]
    r.gs[...] = jnp.concatenate(halves, axis=1).astype(BF16)
    r.gr[d] = r.gs[d]

    def gs_copy(k, peer):
        return remote(r.gs.at[peer], r.gr.at[d], r.gs_s.at[0], r.gs_r.at[0], peer, t)

    over_dp(lambda k, peer: gs_copy(k, peer).start())

    arrived(r.dkx.at[1, 1 - zl], r.dx_r.at[1])
    r.dv[y] = r.dkx[1]
    for k in (1, 3, 2):
        start(
            remote(
                r.dv.at[y], r.dv.at[y], r.dv_s.at[k], r.dv_r.at[y], plane(x, turn(y, k, 4)), t
            )
        )
    d_queries = [nn(d_scores[h], kv[:, 128 * h : 128 * h + 128]) for h in (0, 1)]
    arrived(r.dkx.at[0, 1 - zl], r.dx_r.at[0])
    r.dk[x] = r.dkx[0]
    for k in (1, 3, 2):
        start(
            remote(
                r.dk.at[x], r.dk.at[x], r.dk_s.at[k], r.dk_r.at[x], plane(turn(x, k, 4), y), t
            )
        )

    d_query = jnp.concatenate(d_queries, axis=1).astype(BF16).astype(F32) * rstd
    mat_h = nn(r.blend_t[...], d_query.astype(BF16)).reshape(32, 8, 256)
    halves = [mat_h[:, :, 0:128], mat_h[:, :, 128:256]]
    r.hs[:, :, 0:128] = jnp.concatenate(halves, axis=1).astype(BF16)
    frame_sum = jnp.sum(d_query, axis=0, keepdims=True)
    loss_high = loss_part.astype(BF16).astype(F32)
    which = lax.broadcasted_iota(jnp.int32, (16, 128), 0)
    extra = jnp.where(which == 2, loss_high, loss_part - loss_high)
    extra = jnp.where(which == 1, frame_sum[:, 128:256], extra)
    extra = jnp.where(which == 0, frame_sum[:, 0:128], extra)
    r.hs[:, :, 128:256] = jnp.broadcast_to(extra.astype(BF16)[None], (32, 16, 128))
    r.hr[d] = r.hs[d]

    def h_copy(k, peer):
        return remote(r.hs.at[peer], r.hr.at[d], r.hs_s.at[0], r.hs_r.at[0], peer, t)

    over_dp(lambda k, peer: h_copy(k, peer).start())

    all_arrived(r.gr, r.gs_r.at[0])
    r.hg[d, :, 128:256] = jnp.sum(r.gr[...].astype(F32), axis=0).astype(BF16)
    all_arrived(r.hr, r.hs_r.at[0])
    arrivals = r.hr[...].astype(F32)
    r.hg[d, :, 0:128] = jnp.sum(arrivals[:, :, 0:128], axis=0).astype(BF16)

    def g_copy(k, peer):
        return remote(r.hg.at[d], r.hg.at[d], r.hg_s.at[0], r.hg_r.at[0], peer, t)

    over_dp(lambda k, peer: g_copy(k, peer).start())

    for k in (1, 3, 2):
        slot = turn(y, k, 4)
        arrived(r.dv.at[slot], r.dv_r.at[slot])
    all_v = r.dv[...].reshape(512, 256)
    for q in range(4):
        r.gv_send[q] = nn(r.cap_vt[q], all_v).astype(BF16)
    for k in (1, 3, 2):
        xx = turn(x, k, 4)
        start(
            remote(
                r.gv_send.at[xx], r.gv_recv.at[x], r.gv_s.at[k], r.gv_r.at[x], plane(xx, y), t
            )
        )
    r.gv_recv[x] = r.gv_send[x]
    for k in (1, 3, 2):
        slot = turn(x, k, 4)
        arrived(r.dk.at[slot], r.dk_r.at[slot])
    all_k = r.dk[...].reshape(512, 256)
    grad_k = nn(r.cap_kt[...], all_k).reshape(4, 128, 256)
    for q in range(4):
        r.gk_send[q] = grad_k[q].astype(BF16)
    for k in (1, 3, 2):
        yy = turn(y, k, 4)
        start(
            remote(
                r.gk_send.at[yy], r.gk_recv.at[y], r.gk_s.at[k], r.gk_r.at[y], plane(x, yy), t
            )
        )
    r.gk_recv[y] = r.gk_send[y]

    sums_p = jnp.concatenate([arrivals[:, 0, 128:256], arrivals[:, 1, 128:256]], axis=1)
    losses = arrivals[:, 2, 128:256] + arrivals[:, 3, 128:256]
    r.loss_out[...] = jnp.sum(losses, axis=0, keepdims=True) / 8192.0
    all_arrived(r.hg, r.hg_r.at[0])
    grads = r.hg[...].astype(F32)

    def matrix(slabs):
        left = slabs[:, 0:8].reshape(256, 128)
        right = slabs[:, 8:16].reshape(256, 128)
        return jnp.concatenate([left, right], axis=1)

    sum_h = matrix(grads[:, :, 0:128])
    sum_g = matrix(grads[:, :, 128:256]).astype(BF16)
    r.packed_out[0:64] = nn(w_c, sum_h, HIGHEST) + tn(times_c, sums_p, HIGHEST)
    r.packed_out[320:384] = nt(r.vel[...], sum_g)
    for k in (1, 3, 2):
        slot = turn(y, k, 4)
        arrived(r.gk_recv.at[slot], r.gk_r.at[slot])
        slot = turn(x, k, 4)
        arrived(r.gv_recv.at[slot], r.gv_r.at[slot])
    r.packed_out[64:192] = jnp.sum(r.gk_recv[...].astype(F32), axis=0)
    r.packed_out[192:320] = jnp.sum(r.gv_recv[...].astype(F32), axis=0)

    for copy in pending:
        copy.wait_send()

    @pl.when(jnp.logical_not(inside))
    def _():
        cap_copy(0).wait_send()

    all_left(r.c0, r.c0_s.at[0])
    all_left(r.zrb, r.zb_s.at[0])
    all_left(r.zrf, r.zf_s.at[0])
    all_left(r.agb, r.ab_s.at[0])
    all_left(r.agf.at[c], r.af_s.at[0])
    all_left(r.hr, r.hs_s.at[0])
    all_left(r.gr, r.gs_s.at[0])
    all_left(r.hg, r.hg_s.at[0])


def unpack(loss, packed, loss_out, gq, gk, gv, go):
    loss_out[...] = loss[...]
    gq[...] = packed[0:64]
    gk[...] = packed[64:192]
    gv[...] = packed[192:320]
    go[...] = packed[320:384]


def rope_tables():
    inverse = 1000000.0 ** (-(np.arange(64, dtype=np.float32) * 2.0 / 128))
    angles = np.arange(64, dtype=np.float32)[:, None] * inverse[None, :].astype(np.float32)
    angles = np.concatenate([angles, angles], axis=1).astype(np.float32)
    sign = np.where(np.arange(128) < 64, -1.0, 1.0)[None, :]
    return np.cos(angles).astype(np.float32), (np.sin(angles) * sign).astype(np.float32)


def local(
    encoder_input_states,
    caption_lengths,
    encoder_input_gain,
    query_head_gain,
    key_head_gain,
    encoder_query_weight,
    encoder_key_weight,
    encoder_value_weight,
    encoder_output_weight,
    clean_motion,
    noise,
    timestep_index,
    motion_lengths,
    input_weight,
    velocity_weight,
    cross_query_weight,
    cross_key_weight,
    cross_value_weight,
    cross_output_weight,
):
    vmem = pl.BlockSpec(memory_space=pltpu.VMEM)
    hbm = pl.BlockSpec(memory_space=pl.ANY)
    smem = pl.BlockSpec(memory_space=pltpu.SMEM)
    spec = {name: vmem for name in INPUTS}
    for name in ("cap_len", "step_index", "motion_len"):
        spec[name] = smem
    for name in ("eq", "ek", "ev", "eo"):
        spec[name] = hbm
    cosine, sine = rope_tables()
    packed = pl.pallas_call(
        kernel,
        out_shape=[
            jax.ShapeDtypeStruct((1, 128), F32),
            jax.ShapeDtypeStruct((384, 256), F32),
        ],
        in_specs=[spec[name] for name in INPUTS],
        out_specs=[vmem] * 2,
        scratch_shapes=[pltpu.VMEM(shape, kind) for shape, kind in BUFFERS.values()]
        + [
            pltpu.SemaphoreType.DMA(shape if isinstance(shape, tuple) else (shape,))
            for shape in SEMAPHORES.values()
        ],
        compiler_params=pltpu.CompilerParams(
            collective_id=0, has_side_effects=True, vmem_limit_bytes=56 * 2**20
        ),
        name="motion_block",
    )(
        encoder_input_states,
        caption_lengths,
        timestep_index,
        motion_lengths,
        encoder_input_gain.reshape(8, 1, 512),
        query_head_gain.reshape(1, 128),
        key_head_gain.reshape(1, 128),
        jnp.asarray(cosine),
        jnp.asarray(sine),
        encoder_query_weight,
        encoder_key_weight,
        encoder_value_weight,
        encoder_output_weight,
        clean_motion,
        noise,
        input_weight.T,
        velocity_weight,
        cross_query_weight,
        cross_key_weight,
        cross_value_weight,
        cross_output_weight.T,
    )
    loss, gq, gk, gv, go = pl.pallas_call(
        unpack,
        out_shape=[
            jax.ShapeDtypeStruct((1, 128), F32),
            jax.ShapeDtypeStruct((64, 256), F32),
            jax.ShapeDtypeStruct((128, 256), F32),
            jax.ShapeDtypeStruct((128, 256), F32),
            jax.ShapeDtypeStruct((64, 256), F32),
        ],
        in_specs=[vmem] * 2,
        out_specs=[vmem] * 5,
        name="unpack",
    )(*packed)
    return (loss[0, 0], gq, gk, gv, go.T)


def solution(mesh):
    placed = (
        P("dp", None, "tensor"),
        P("dp"),
        P(),
        P(),
        P(),
        P(None, "tensor"),
        P(None, "tensor"),
        P(None, "tensor"),
        P("tensor", None),
        P("dp", None, None),
        P("dp", None, None),
        P("dp"),
        P("dp"),
        P(None, "dp"),
        P("dp", None),
        P("dp", "tensor"),
        P("dp", "tensor"),
        P("dp", "tensor"),
        P("tensor", "dp"),
    )
    return jax.shard_map(
        local,
        mesh=mesh,
        in_specs=placed,
        out_specs=(P(), P("dp", "tensor"), P("dp", "tensor"), P("dp", "tensor"), P("tensor", "dp")),
        check_vma=False,
    )
```

```python
import math
import types

import jax
import jax.numpy as jnp
import numpy as np
from jax import lax
from jax.experimental import pallas as pl
from jax.experimental.pallas import tpu as pltpu
from jax.sharding import PartitionSpec as P

F32 = jnp.float32
BF16 = jnp.bfloat16
MESH = pl.DeviceIdType.MESH
HIGHEST = lax.Precision.HIGHEST
EPSILON = 1e-06
STEPS = 1000
FRAMES = 360
PADDED = 384
SCALE = 1.0 / math.sqrt(128)

INPUTS = [
    "states", "cap_len", "step_index", "motion_len", "gain", "q_gain", "k_gain", "cosine", "sine",
    "eq", "ek", "ev", "eo", "clean", "noise", "w_in", "vel", "wq", "wk", "wv", "wo",
]
OUTPUTS = ["loss", "packed"]

BUFFERS = dict(
    w_qkv=((4096, 768), BF16),
    w_out=((512, 4096), BF16),
    c0=((32, 1, 384), F32),
    gx=((8, 64, 512), BF16),
    wkv=((16, 2, 64, 512), BF16),
    zsb=((32, 16, 256), BF16),
    zrb=((32, 16, 256), BF16),
    zsf=((32, 8, 384), F32),
    zrf=((32, 8, 384), F32),
    agb=((32, 16, 256), BF16),
    agf=((2, 32, 8, 256), F32),
    ra_send=((4, 64, 512), BF16),
    ra_recv=((4, 64, 512), BF16),
    rb_send=((4, 64, 512), BF16),
    rb_recv=((4, 64, 512), BF16),
    r_own=((4, 64, 512), F32),
    cap_own=((64, 512), BF16),
    caps=((4, 2, 64, 512), BF16),
    kvx_send=((64, 512), BF16),
    kvx_recv=((64, 512), BF16),
    blend=((PADDED, 256), BF16),
    query=((PADDED, 256), BF16),
    hid_v=((PADDED, 256), F32),
    va_send=((4, 48, 256), BF16),
    va_recv=((4, 48, 256), BF16),
    v_own=((4, 48, 256), F32),
    vb_send=((4, 48, 256), BF16),
    vb_recv=((4, 48, 256), BF16),
    vg=((8, 48, 256), BF16),
    dkx=((2, 2, 64, 256), BF16),
    dk=((4, 2, 64, 256), BF16),
    dv=((4, 2, 64, 256), BF16),
    cap_k=((4, 2, 64, 512), BF16),
    cap_v=((4, 4, 2, 64, 128), BF16),
    cap_kt=((512, 512), BF16),
    cap_vt=((4, 128, 512), BF16),
    blend_t=((256, PADDED), BF16),
    att_t=((256, PADDED), BF16),
    prob_t=((2, 64, PADDED), BF16),
    gk_send=((4, 128, 256), BF16),
    gk_recv=((4, 128, 256), BF16),
    gv_send=((4, 128, 256), BF16),
    gv_recv=((4, 128, 256), BF16),
    hs=((32, 16, 384), BF16),
    hr=((32, 16, 384), BF16),
    hg=((32, 16, 256), BF16),
)

SEMAPHORES = dict(
    load=4,
    c0_s=1, c0_r=1,
    gx_s=8, gx_r=8,
    wkv_s=32, wkv_r=(16, 2),
    zb_s=1, zb_r=1, zf_s=1, zf_r=1,
    ab_s=1, ab_r=1, af_s=1, af_r=1, ap_s=1, ap_r=1,
    ra_s=4, ra_r=4, rb_s=4, rb_r=4,
    cp_s=8, cp_r=(4, 2),
    kvx_s=1, kvx_r=1,
    va_s=1, va_r=1, vb_s=4, vb_r=4, vg_s=8, vg_r=8,
    dx_s=2, dx_r=2, dk_s=4, dk_r=4, dv_s=4, dv_r=4,
    ck_s=4, ck_r=4, cv_s=4, cv_r=4,
    gk_s=4, gk_r=4, gv_s=4, gv_r=4,
    hs_s=1, hs_r=1, hg_s=1, hg_r=1,
)


def dot(a, b, left, right, precision=None):
    return lax.dot_general(
        a, b, (((left,), (right,)), ((), ())), precision=precision, preferred_element_type=F32
    )


def nn(a, b, precision=None):
    return dot(a, b, 1, 0, precision)


def nt(a, b, precision=None):
    return dot(a, b, 1, 1, precision)


def tn(a, b, precision=None):
    return dot(a, b, 0, 0, precision)


def softmax(scores):
    top = jnp.max(scores, axis=-1, keepdims=True)
    weights = jnp.exp(scores - top)
    return weights / jnp.sum(weights, axis=-1, keepdims=True)


def remote(source, target, send, receive, dp, tensor):
    return pltpu.make_async_remote_copy(
        src_ref=source,
        dst_ref=target,
        send_sem=send,
        recv_sem=receive,
        device_id=(dp, tensor),
        device_id_type=MESH,
    )


def kernel(*refs):
    names = INPUTS + [n + "_out" for n in OUTPUTS] + list(BUFFERS) + list(SEMAPHORES)
    r = types.SimpleNamespace(**dict(zip(names, refs, strict=True)))

    d = lax.axis_index("dp")
    t = lax.axis_index("tensor")
    zl = lax.div(d, 16)
    xy = lax.rem(d, 16)
    x = lax.div(xy, 4)
    y = lax.rem(xy, 4)
    zh = lax.div(t, 2)
    c = lax.rem(t, 2)
    mate = t + 1 - 2 * c
    other = (1 - zl) * 16 + xy
    pending = []

    def start(copy):
        copy.start()
        pending.append(copy)

    def turn(base, k, size):
        return lax.rem(base + k, size)

    def plane(xx, yy):
        return zl * 16 + xx * 4 + yy

    def arrived(slot, semaphore):
        remote(slot, slot, semaphore, semaphore, other, t).wait_recv()

    def all_arrived(buffer, semaphore):
        most = buffer.at[pl.ds(0, 31)]
        remote(most, most, semaphore, semaphore, other, t).wait_recv()

    def all_left(buffer, semaphore):
        most = buffer.at[pl.ds(0, 31)]
        remote(most, most, semaphore, semaphore, other, t).wait_send()

    def over_dp(body):
        def step(k, carry):
            body(k, turn(d, k, 32))
            return carry

        lax.fori_loop(1, 32, step, 0)

    loads = [
        pltpu.make_async_copy(r.eq, r.w_qkv.at[:, pl.ds(0, 512)], r.load.at[0]),
        pltpu.make_async_copy(r.ek, r.w_qkv.at[:, pl.ds(512, 128)], r.load.at[1]),
        pltpu.make_async_copy(r.ev, r.w_qkv.at[:, pl.ds(640, 128)], r.load.at[2]),
        pltpu.make_async_copy(r.eo, r.w_out, r.load.at[3]),
    ]
    for load in loads:
        load.start()

    barrier = pltpu.get_barrier_semaphore()

    def signal(dp, tensor):
        pl.semaphore_signal(barrier, inc=1, device_id=(dp, tensor), device_id_type=MESH)

    over_dp(lambda k, peer: signal(peer, t))
    signal(d, mate)
    for k in (1, 2, 3):
        signal(d, turn(zh, k, 4) * 2 + c)
        signal(other, turn(zh, k, 4) * 2 + c)

    r.gx[t] = r.states[0]
    wk_v = r.wk[...]
    wv_v = r.wv[...]
    for half in (0, 1):
        r.wkv[xy, half, :, 0:256] = wk_v[64 * half : 64 * half + 64]
        r.wkv[xy, half, :, 256:512] = wv_v[64 * half : 64 * half + 64]
    w_in_v = r.w_in[...]
    w_in_t = w_in_v.astype(F32)
    decay = -math.log(10000.0) / 1024.0
    step_f = jnp.full((8, 128), r.step_index[0], jnp.int32).astype(F32)
    place = (
        lax.broadcasted_iota(jnp.int32, (8, 128), 0) * 128
        + lax.broadcasted_iota(jnp.int32, (8, 128), 1)
    ).astype(F32)
    all_angles = step_f * jnp.exp(decay * place)
    all_cos = jnp.cos(all_angles)
    all_sin = jnp.sin(all_angles)

    def total(tile):
        return jnp.sum(jnp.sum(tile, axis=1, keepdims=True), axis=0, keepdims=True)

    own_mean = total(all_cos + all_sin) / 2048.0
    time_square = total((all_cos - own_mean) ** 2 + (all_sin - own_mean) ** 2)
    lane = lax.broadcasted_iota(jnp.int32, (1, 128), 1)
    r.c0[d, :, 0:256] = jnp.sum(w_in_t, axis=0, keepdims=True)
    r.c0[d, :, 256:384] = jnp.where(lane == 0, step_f[0:1], own_mean)

    vel_v = r.vel[...]
    wq_v = r.wq[...]
    part_m = tn(r.wo[...], vel_v).reshape(32, 8, 256)
    part_b = tn(w_in_v, vel_v)

    pl.semaphore_wait(barrier, 38)

    for k in (2, 1, 3):
        start(remote(r.gx.at[t], r.gx.at[t], r.gx_s.at[k], r.gx_r.at[t], d, turn(zh, k, 4) * 2 + c))
    start(remote(r.gx.at[t], r.gx.at[t], r.gx_s.at[0], r.gx_r.at[t], d, mate))

    def wkv_send(slot, half, dp, index):
        ref = r.wkv.at[slot, half]
        start(remote(ref, ref, r.wkv_s.at[index], r.wkv_r.at[slot, half], dp, t))

    for k in (1, 3, 2):
        wkv_send(xy, 0, plane(turn(x, k, 4), y), k - 1)
        wkv_send(xy, 1, plane(x, turn(y, k, 4)), 2 + k)

    def c0_copy(k, peer):
        return remote(r.c0.at[d], r.c0.at[d], r.c0_s.at[0], r.c0_r.at[0], peer, t)

    over_dp(lambda k, peer: c0_copy(k, peer).start())

    def wkv_second(first, k_list):
        for k in k_list:
            if k:
                slot = turn(x, k, 4) * 4 + y
                arrived(r.wkv.at[slot, 0], r.wkv_r.at[slot, 0])
                slot = x * 4 + turn(y, k, 4)
                arrived(r.wkv.at[slot, 1], r.wkv_r.at[slot, 1])
            for j in (1, 3, 2):
                wkv_send(turn(x, k, 4) * 4 + y, 0, plane(x, turn(y, j, 4)), first + 6 * k + j - 1)
                wkv_send(
                    x * 4 + turn(y, k, 4), 1, plane(turn(x, j, 4), y), first + 6 * k + 2 + j
                )

    wkv_second(6, (0, 1, 3, 2))

    for load in loads[:3]:
        load.wait()

    def project(slot, sums, square):
        chunk = r.gx[slot].astype(F32)
        square = square + jnp.sum(chunk * chunk, axis=1, keepdims=True)
        row = pl.multiple_of(slot * 512, 512)
        scaled = (chunk * r.gain[slot]).astype(BF16)
        return sums + nn(scaled, r.w_qkv[pl.ds(row, 512), :]), square

    sums, square = project(t, jnp.zeros((64, 768), F32), jnp.zeros((64, 1), F32))

    all_arrived(r.c0, r.c0_r.at[0])
    facts = r.c0[...].reshape(32, 384)
    w_mean = jnp.sum(facts[:, 0:256], axis=0, keepdims=True) / 2048.0
    steps = facts[:, 256:257]
    step_means = facts[:, 257:258]
    column = (
        lax.broadcasted_iota(jnp.int32, (1, 64), 1) + lax.rem(d, 16) * 64
    ).astype(F32)
    angles = steps * jnp.exp(decay * column)
    quarter = jnp.full((32, 64), zl, jnp.int32).astype(F32) * (math.pi / 2.0)
    times = jnp.cos(angles - quarter)
    times_c = times - step_means
    w_c = w_in_t - w_mean
    part_a = tn(w_c.astype(BF16), wq_v).reshape(32, 8, 256)
    r.zsb[...] = jnp.concatenate([part_a, part_m], axis=1).astype(BF16)
    first_core = jnp.full((256, 256), c, jnp.int32) == 0
    part_f = jnp.where(first_core, part_b, tn(w_c, w_c, HIGHEST))
    r.zsf[:, :, 0:256] = part_f.reshape(32, 8, 256)
    time_rows = jnp.concatenate(
        [
            nn(times_c, wq_v.astype(F32), HIGHEST),
            nn(times, vel_v.astype(F32), HIGHEST),
            nn(times_c, w_c, HIGHEST),
        ],
        axis=1,
    )
    for i in range(8):
        part = time_rows[:, 128 * i : 128 * i + 128] if i < 6 else jnp.zeros((32, 128), F32)
        r.zsf[:, i, 256:384] = part
    r.zrb[d] = r.zsb[d]
    r.zrf[d] = r.zsf[d]

    def z_copies(k, peer):
        return (
            remote(r.zsb.at[peer], r.zrb.at[d], r.zb_s.at[0], r.zb_r.at[0], peer, t),
            remote(r.zsf.at[peer], r.zrf.at[d], r.zf_s.at[0], r.zf_r.at[0], peer, t),
        )

    def z_start(k, peer):
        for copy in z_copies(k, peer):
            copy.start()

    for k in (1, 3, 2):
        slot = turn(zh, k, 4) * 2 + c
        arrived(r.gx.at[slot], r.gx_r.at[slot])
        start(remote(r.gx.at[slot], r.gx.at[slot], r.gx_s.at[4 + k], r.gx_r.at[slot], d, mate))
        sums, square = project(slot, sums, square)

    over_dp(z_start)

    arrived(r.gx.at[mate], r.gx_r.at[mate])
    sums, square = project(mate, sums, square)
    for k in (1, 3, 2):
        slot = turn(zh, k, 4) * 2 + (1 - c)
        arrived(r.gx.at[slot], r.gx_r.at[slot])
        sums, square = project(slot, sums, square)

    length = r.cap_len[0]
    rms = lax.rsqrt(square / 4096.0 + EPSILON)
    sums = sums * rms
    cosine = r.cosine[...]
    sine = r.sine[...]

    def turned(vectors, scaling):
        mean = jnp.mean(vectors * vectors, axis=1, keepdims=True)
        vectors = vectors * lax.rsqrt(mean + EPSILON) * scaling
        return (vectors * cosine + pltpu.roll(vectors, 64, 1) * sine).astype(BF16)

    q_gain = r.q_gain[...]
    queries = jnp.concatenate(
        [turned(sums[:, 128 * h : 128 * h + 128], q_gain) for h in range(4)], axis=0
    )
    keys = turned(sums[:, 512:640], r.k_gain[...])
    values = sums[:, 640:768].astype(BF16)
    scores = nt(queries, keys) * SCALE
    row = lax.rem(lax.broadcasted_iota(jnp.int32, (256, 64), 0), 64)
    col = lax.broadcasted_iota(jnp.int32, (256, 64), 1)
    scores = jnp.where((col <= row) & (col < length), scores, -1e30)
    mixed = nn(softmax(scores).astype(BF16), values).astype(BF16)
    mixed = jnp.concatenate([mixed[64 * h : 64 * h + 64] for h in range(4)], axis=1)

    loads[3].wait()
    for k in (1, 3, 2, 0):
        slot = turn(zh, k, 4)
        column = pl.multiple_of((slot * 2 + 1 - c) * 512, 512)
        r.ra_send[slot] = nn(mixed, r.w_out[:, pl.ds(column, 512)]).astype(BF16)
        start(
            remote(
                r.ra_send.at[slot], r.ra_recv.at[slot], r.ra_s.at[k], r.ra_r.at[slot], d, mate
            )
        )
    for k in (1, 3, 2, 0):
        slot = turn(zh, k, 4)
        column = pl.multiple_of((slot * 2 + c) * 512, 512)
        r.r_own[slot] = nn(mixed, r.w_out[:, pl.ds(column, 512)])
    for k in (2, 1, 3):
        slot = turn(zh, k, 4)
        arrived(r.ra_recv.at[slot], r.ra_r.at[slot])
        r.rb_send[slot] = (r.r_own[slot] + r.ra_recv[slot].astype(F32)).astype(BF16)
        start(
            remote(
                r.rb_send.at[slot], r.rb_recv.at[zh], r.rb_s.at[k], r.rb_r.at[zh], d, slot * 2 + c
            )
        )

    slot = zh
    arrived(r.ra_recv.at[slot], r.ra_r.at[slot])
    own = r.r_own[slot] + r.ra_recv[slot].astype(F32)
    for k in (1, 3, 2):
        slot = turn(zh, k, 4)
        arrived(r.rb_recv.at[slot], r.rb_r.at[slot])
        own = own + r.rb_recv[slot].astype(F32)
    r.cap_own[...] = (r.states[0].astype(F32) + own).astype(BF16)

    target = lax.div(zh, 2)
    mine = lax.rem(t, 4)
    inside = target == zl

    def cap_copy(k):
        return remote(
            r.cap_own,
            r.caps.at[mine, zl],
            r.cp_s.at[k],
            r.cp_r.at[mine, zl],
            target * 16 + xy,
            turn(zh, k, 4) * 2 + c,
        )

    for k in (2, 1, 3):
        start(cap_copy(k))

    @pl.when(inside)
    def _():
        r.caps[mine, zl] = r.cap_own[...]

    @pl.when(jnp.logical_not(inside))
    def _():
        cap_copy(0).start()

    all_arrived(r.zrb, r.zb_r.at[0])
    all_arrived(r.zrf, r.zf_r.at[0])
    r.agb[d] = jnp.sum(r.zrb[...].astype(F32), axis=0).astype(BF16)
    slabs = jnp.sum(r.zrf[...], axis=0)
    r.agf[c, d] = slabs[:, 0:256]
    time_own = jnp.concatenate([slabs[i : i + 1, 256:384] for i in range(6)], axis=1)

    def a_copies(k, peer):
        return (
            remote(r.agb.at[d], r.agb.at[d], r.ab_s.at[0], r.ab_r.at[0], peer, t),
            remote(r.agf.at[c, d], r.agf.at[c, d], r.af_s.at[0], r.af_r.at[0], peer, t),
        )

    def a_start(k, peer):
        for copy in a_copies(k, peer):
            copy.start()

    over_dp(a_start)

    for k in (0, 1, 2, 3):
        for j in (1, 2, 3):
            slot = turn(x, k, 4) * 4 + turn(y, j, 4)
            arrived(r.wkv.at[slot, 0], r.wkv_r.at[slot, 0])
            slot = turn(x, j, 4) * 4 + turn(y, k, 4)
            arrived(r.wkv.at[slot, 1], r.wkv_r.at[slot, 1])

    forwards = []
    for z in (0, 1):
        for near in (0, 1):
            chunk = near * 2 + c
            ref = r.caps.at[chunk, z]
            own_slot = inside & (chunk == mine) & (z == zl)

            @pl.when(jnp.logical_not(own_slot))
            def _(ref=ref, chunk=chunk, z=z):
                arrived(ref, r.cp_r.at[chunk, z])

            start(remote(ref, ref, r.cp_s.at[4 + 2 * z + near], r.cp_r.at[chunk, z], d, mate))

    def project_caption(chunk):
        rows = r.caps[chunk].reshape(128, 512)
        weights = r.wkv[pl.ds(chunk * 4, 4)].reshape(512, 512)
        return nn(rows, weights)

    both = project_caption(c) + project_caption(2 + c)
    for near in (0, 1):
        for z in (0, 1):
            chunk = near * 2 + 1 - c
            arrived(r.caps.at[chunk, z], r.cp_r.at[chunk, z])
        both = both + project_caption(near * 2 + 1 - c)
    second = jnp.full((64, 512), zl, jnp.int32) == 1
    r.kvx_send[...] = jnp.where(second, both[0:64], both[64:128]).astype(BF16)
    start(remote(r.kvx_send, r.kvx_recv, r.kvx_s.at[0], r.kvx_r.at[0], other, t))

    r.cap_k[x] = r.caps[x]
    for q in range(4):
        column = pl.multiple_of(y * 128, 128)
        r.cap_v[y, q] = r.caps[q, :, :, pl.ds(column, 128)]
    for k in (1, 3, 2):
        xx = turn(x, k, 4)
        start(
            remote(r.caps.at[xx], r.cap_k.at[x], r.ck_s.at[k], r.ck_r.at[x], plane(xx, y), t)
        )
        yy = turn(y, k, 4)
        column = pl.multiple_of(yy * 128, 128)
        start(
            remote(
                r.caps.at[:, :, :, pl.ds(column, 128)],
                r.cap_v.at[y],
                r.cv_s.at[k],
                r.cv_r.at[y],
                plane(x, yy),
                t,
            )
        )

    clean = r.clean[0].astype(F32)
    noise = r.noise[0].astype(F32)
    tau = jnp.full((1, 256), r.step_index[0], jnp.int32).astype(F32) / STEPS
    margin = jnp.zeros((PADDED - FRAMES, 256), F32)
    blend_f = jnp.concatenate([(1.0 - tau) * clean + tau * noise, margin], axis=0)
    r.blend[...] = blend_f.astype(BF16)
    blend = r.blend[...]
    blend_f = blend.astype(F32)
    all_arrived(r.agb, r.ab_r.at[0])
    all_arrived(r.agf.at[c], r.af_r.at[0])
    start(remote(r.agf.at[c], r.agf.at[c], r.ap_s.at[0], r.ap_r.at[0], d, mate))
    matrices = r.agb[...].astype(F32)
    mat_a = matrices[:, 0:8].reshape(256, 256).astype(BF16)
    mat_m = matrices[:, 8:16].reshape(256, 256).astype(BF16)
    arrived(r.agf.at[1 - c], r.ap_r.at[0])
    mat_b = r.agf[0].reshape(256, 256)
    mat_s = r.agf[1].reshape(256, 256)
    r.hid_v[...] = nn(blend_f, mat_b, HIGHEST) + time_own[:, 256:512]
    spread = (nn(blend_f, mat_s, HIGHEST) + 2.0 * time_own[:, 512:768]) * blend_f
    variance = (jnp.sum(spread, axis=1, keepdims=True) + time_square) / 2048.0
    rstd = lax.rsqrt(jnp.maximum(variance, 0.0) + EPSILON)
    r.query[...] = ((nn(blend, mat_a) + time_own[:, 0:256]) * rstd).astype(BF16)

    kv_own = jnp.where(second, both[64:128], both[0:64])
    arrived(r.kvx_recv, r.kvx_r.at[0])
    kv = (kv_own + r.kvx_recv[...].astype(F32)).astype(BF16)

    query = r.query[...]
    allowed = lax.broadcasted_iota(jnp.int32, (PADDED, 64), 1) < length
    probs = []
    attended = []
    for h in (0, 1):
        span = slice(128 * h, 128 * h + 128)
        scores = nt(query[:, span], kv[:, span]) * SCALE
        prob = softmax(jnp.where(allowed, scores, -1e30))
        probs.append(prob)
        attended.append(nn(prob.astype(BF16), kv[:, 256 + 128 * h : 384 + 128 * h]).astype(BF16))
    attended = jnp.concatenate(attended, axis=1)
    branch = nn(attended, mat_m).reshape(8, 48, 256)

    first_half = jnp.full((48, 256), c, jnp.int32) == 0
    for q in range(4):
        r.va_send[q] = jnp.where(first_half, branch[2 * q + 1], branch[2 * q]).astype(BF16)
        r.v_own[q] = jnp.where(first_half, branch[2 * q], branch[2 * q + 1])
    start(remote(r.va_send, r.va_recv, r.va_s.at[0], r.va_r.at[0], d, mate))
    r.att_t[...] = attended.T
    for h in (0, 1):
        r.prob_t[h] = probs[h].astype(BF16).T
    arrived(r.va_recv, r.va_r.at[0])
    for k in (2, 1, 3):
        slot = turn(zh, k, 4)
        r.vb_send[slot] = (r.v_own[slot] + r.va_recv[slot].astype(F32)).astype(BF16)
        start(
            remote(
                r.vb_send.at[slot], r.vb_recv.at[zh], r.vb_s.at[k], r.vb_r.at[zh], d, slot * 2 + c
            )
        )
    r.blend_t[...] = blend.T
    for k in (1, 3, 2):
        slot = turn(x, k, 4)
        arrived(r.cap_k.at[slot], r.ck_r.at[slot])
    r.cap_kt[...] = r.cap_k[...].reshape(512, 512).T
    own = r.v_own[zh] + r.va_recv[zh].astype(F32)
    for k in (1, 3, 2):
        slot = turn(zh, k, 4)
        arrived(r.vb_recv.at[slot], r.vb_r.at[slot])
        own = own + r.vb_recv[slot].astype(F32)
    r.vg[t] = own.astype(BF16)
    for k in (2, 1, 3):
        start(remote(r.vg.at[t], r.vg.at[t], r.vg_s.at[k], r.vg_r.at[t], d, turn(zh, k, 4) * 2 + c))
    start(remote(r.vg.at[t], r.vg.at[t], r.vg_s.at[0], r.vg_r.at[t], d, mate))
    for k in (1, 3, 2):
        slot = turn(y, k, 4)
        arrived(r.cap_v.at[slot], r.cv_r.at[slot])
    for q in range(4):
        r.cap_vt[q] = r.cap_v[:, q].reshape(512, 128).T
    for k in (1, 3, 2):
        slot = turn(zh, k, 4) * 2 + c
        arrived(r.vg.at[slot], r.vg_r.at[slot])
        start(remote(r.vg.at[slot], r.vg.at[slot], r.vg_s.at[4 + k], r.vg_r.at[slot], d, mate))
    arrived(r.vg.at[mate], r.vg_r.at[mate])
    for k in (1, 3, 2):
        slot = turn(zh, k, 4) * 2 + 1 - c
        arrived(r.vg.at[slot], r.vg_r.at[slot])

    predicted = r.hid_v[...] + r.vg[...].astype(F32).reshape(PADDED, 256)
    residual = predicted - jnp.concatenate([noise - clean, margin], axis=0)
    frames = jnp.full((PADDED, 1), r.motion_len[0], jnp.int32)
    live = lax.broadcasted_iota(jnp.int32, (PADDED, 1), 0) < frames
    row_weight = jnp.where(live, 1.0 / frames.astype(F32), 0.0)
    weighted = residual * row_weight
    loss_part = total(residual * weighted)
    d_vel = (2.0 * weighted).astype(BF16)
    d_att = nt(d_vel, mat_m).astype(BF16)

    heads = [d_att[:, 128 * h : 128 * h + 128] for h in (0, 1)]
    d_values = [nn(r.prob_t[h], heads[h]) for h in (0, 1)]
    r.dkx[1, zl] = jnp.concatenate(d_values, axis=1).astype(BF16)

    def dx_start(i):
        ref = r.dkx.at[i, zl]
        start(remote(ref, ref, r.dx_s.at[i], r.dx_r.at[i], other, t))

    dx_start(1)
    d_scores = []
    for h in (0, 1):
        d_prob = nt(heads[h], kv[:, 256 + 128 * h : 384 + 128 * h])
        delta = jnp.sum(probs[h] * d_prob, axis=1, keepdims=True)
        d_scores.append((probs[h] * (d_prob - delta) * SCALE).astype(BF16))
    d_keys = [tn(d_scores[h], query[:, 128 * h : 128 * h + 128]) for h in (0, 1)]
    r.dkx[0, zl] = jnp.concatenate(d_keys, axis=1).astype(BF16)
    dx_start(0)
    mat_g = nn(r.att_t[...], d_vel).reshape(32, 8, 256)
    d_queries = [nn(d_scores[h], kv[:, 128 * h : 128 * h + 128]) for h in (0, 1)]
    arrived(r.dkx.at[1, 1 - zl], r.dx_r.at[1])
    r.dv[y] = r.dkx[1]
    for k in (1, 3, 2):
        start(
            remote(
                r.dv.at[y], r.dv.at[y], r.dv_s.at[k], r.dv_r.at[y], plane(x, turn(y, k, 4)), t
            )
        )
    d_query = jnp.concatenate(d_queries, axis=1).astype(BF16).astype(F32) * rstd
    mat_h = nn(r.blend_t[...], d_query.astype(BF16)).reshape(32, 8, 256)
    arrived(r.dkx.at[0, 1 - zl], r.dx_r.at[0])
    r.dk[x] = r.dkx[0]
    for k in (1, 3, 2):
        start(
            remote(
                r.dk.at[x], r.dk.at[x], r.dk_s.at[k], r.dk_r.at[x], plane(turn(x, k, 4), y), t
            )
        )

    r.hs[:, :, 0:256] = jnp.concatenate([mat_h, mat_g], axis=1).astype(BF16)
    frame_sum = jnp.sum(d_query, axis=0, keepdims=True)
    loss_high = loss_part.astype(BF16).astype(F32)
    which = lax.broadcasted_iota(jnp.int32, (16, 128), 0)
    extra = jnp.where(which == 2, loss_high, loss_part - loss_high)
    extra = jnp.where(which == 1, frame_sum[:, 128:256], extra)
    extra = jnp.where(which == 0, frame_sum[:, 0:128], extra)
    r.hs[:, :, 256:384] = jnp.broadcast_to(extra.astype(BF16)[None], (32, 16, 128))
    r.hr[d] = r.hs[d]

    def h_copy(k, peer):
        return remote(r.hs.at[peer], r.hr.at[d], r.hs_s.at[0], r.hs_r.at[0], peer, t)

    over_dp(lambda k, peer: h_copy(k, peer).start())

    for k in (1, 3, 2):
        slot = turn(y, k, 4)
        arrived(r.dv.at[slot], r.dv_r.at[slot])
    all_v = r.dv[...].reshape(512, 256)
    for q in range(4):
        r.gv_send[q] = nn(r.cap_vt[q], all_v).astype(BF16)
    for k in (1, 3, 2):
        xx = turn(x, k, 4)
        start(
            remote(
                r.gv_send.at[xx], r.gv_recv.at[x], r.gv_s.at[k], r.gv_r.at[x], plane(xx, y), t
            )
        )
    r.gv_recv[x] = r.gv_send[x]
    for k in (1, 3, 2):
        slot = turn(x, k, 4)
        arrived(r.dk.at[slot], r.dk_r.at[slot])
    all_k = r.dk[...].reshape(512, 256)
    grad_k = nn(r.cap_kt[...], all_k).reshape(4, 128, 256)
    for q in range(4):
        r.gk_send[q] = grad_k[q].astype(BF16)
    for k in (1, 3, 2):
        yy = turn(y, k, 4)
        start(
            remote(
                r.gk_send.at[yy], r.gk_recv.at[y], r.gk_s.at[k], r.gk_r.at[y], plane(x, yy), t
            )
        )
    r.gk_recv[y] = r.gk_send[y]

    all_arrived(r.hr, r.hs_r.at[0])
    arrivals = r.hr[...].astype(F32)
    r.hg[d] = jnp.sum(arrivals[:, :, 0:256], axis=0).astype(BF16)

    def g_copy(k, peer):
        return remote(r.hg.at[d], r.hg.at[d], r.hg_s.at[0], r.hg_r.at[0], peer, t)

    over_dp(lambda k, peer: g_copy(k, peer).start())

    sums_p = jnp.concatenate([arrivals[:, 0, 256:384], arrivals[:, 1, 256:384]], axis=1)
    losses = arrivals[:, 2, 256:384] + arrivals[:, 3, 256:384]
    r.loss_out[...] = jnp.sum(losses, axis=0, keepdims=True) / 8192.0
    for k in (1, 3, 2):
        slot = turn(y, k, 4)
        arrived(r.gk_recv.at[slot], r.gk_r.at[slot])
        slot = turn(x, k, 4)
        arrived(r.gv_recv.at[slot], r.gv_r.at[slot])
    r.packed_out[64:192] = jnp.sum(r.gk_recv[...].astype(F32), axis=0)
    r.packed_out[192:320] = jnp.sum(r.gv_recv[...].astype(F32), axis=0)
    all_arrived(r.hg, r.hg_r.at[0])
    grads = r.hg[...].astype(F32)
    sum_h = grads[:, 0:8].reshape(256, 256)
    sum_g = grads[:, 8:16].reshape(256, 256).astype(BF16)
    r.packed_out[0:64] = nn(w_c, sum_h, HIGHEST) + tn(times_c, sums_p, HIGHEST)
    r.packed_out[320:384] = nt(r.vel[...], sum_g)

    for copy in pending:
        copy.wait_send()

    @pl.when(jnp.logical_not(inside))
    def _():
        cap_copy(0).wait_send()

    all_left(r.c0, r.c0_s.at[0])
    all_left(r.zrb, r.zb_s.at[0])
    all_left(r.zrf, r.zf_s.at[0])
    all_left(r.agb, r.ab_s.at[0])
    all_left(r.agf.at[c], r.af_s.at[0])
    all_left(r.hr, r.hs_s.at[0])
    all_left(r.hg, r.hg_s.at[0])


def unpack(loss, packed, loss_out, gq, gk, gv, go):
    loss_out[...] = loss[...]
    gq[...] = packed[0:64]
    gk[...] = packed[64:192]
    gv[...] = packed[192:320]
    go[...] = packed[320:384]


def rope_tables():
    inverse = 1000000.0 ** (-(np.arange(64, dtype=np.float32) * 2.0 / 128))
    angles = np.arange(64, dtype=np.float32)[:, None] * inverse[None, :].astype(np.float32)
    angles = np.concatenate([angles, angles], axis=1).astype(np.float32)
    sign = np.where(np.arange(128) < 64, -1.0, 1.0)[None, :]
    return np.cos(angles).astype(np.float32), (np.sin(angles) * sign).astype(np.float32)


def local(
    encoder_input_states,
    caption_lengths,
    encoder_input_gain,
    query_head_gain,
    key_head_gain,
    encoder_query_weight,
    encoder_key_weight,
    encoder_value_weight,
    encoder_output_weight,
    clean_motion,
    noise,
    timestep_index,
    motion_lengths,
    input_weight,
    velocity_weight,
    cross_query_weight,
    cross_key_weight,
    cross_value_weight,
    cross_output_weight,
):
    vmem = pl.BlockSpec(memory_space=pltpu.VMEM)
    hbm = pl.BlockSpec(memory_space=pl.ANY)
    smem = pl.BlockSpec(memory_space=pltpu.SMEM)
    spec = {name: vmem for name in INPUTS}
    for name in ("cap_len", "step_index", "motion_len"):
        spec[name] = smem
    for name in ("eq", "ek", "ev", "eo"):
        spec[name] = hbm
    cosine, sine = rope_tables()
    packed = pl.pallas_call(
        kernel,
        out_shape=[
            jax.ShapeDtypeStruct((1, 128), F32),
            jax.ShapeDtypeStruct((384, 256), F32),
        ],
        in_specs=[spec[name] for name in INPUTS],
        out_specs=[vmem] * 2,
        scratch_shapes=[pltpu.VMEM(shape, kind) for shape, kind in BUFFERS.values()]
        + [
            pltpu.SemaphoreType.DMA(shape if isinstance(shape, tuple) else (shape,))
            for shape in SEMAPHORES.values()
        ],
        compiler_params=pltpu.CompilerParams(
            collective_id=0, has_side_effects=True, vmem_limit_bytes=56 * 2**20
        ),
        name="motion_block",
    )(
        encoder_input_states,
        caption_lengths,
        timestep_index,
        motion_lengths,
        encoder_input_gain.reshape(8, 1, 512),
        query_head_gain.reshape(1, 128),
        key_head_gain.reshape(1, 128),
        jnp.asarray(cosine),
        jnp.asarray(sine),
        encoder_query_weight,
        encoder_key_weight,
        encoder_value_weight,
        encoder_output_weight,
        clean_motion,
        noise,
        input_weight.T,
        velocity_weight,
        cross_query_weight,
        cross_key_weight,
        cross_value_weight,
        cross_output_weight.T,
    )
    loss, gq, gk, gv, go = pl.pallas_call(
        unpack,
        out_shape=[
            jax.ShapeDtypeStruct((1, 128), F32),
            jax.ShapeDtypeStruct((64, 256), F32),
            jax.ShapeDtypeStruct((128, 256), F32),
            jax.ShapeDtypeStruct((128, 256), F32),
            jax.ShapeDtypeStruct((64, 256), F32),
        ],
        in_specs=[vmem] * 2,
        out_specs=[vmem] * 5,
        name="unpack",
    )(*packed)
    return (loss[0, 0], gq, gk, gv, go.T)


def solution(mesh):
    placed = (
        P("dp", None, "tensor"),
        P("dp"),
        P(),
        P(),
        P(),
        P(None, "tensor"),
        P(None, "tensor"),
        P(None, "tensor"),
        P("tensor", None),
        P("dp", None, None),
        P("dp", None, None),
        P("dp"),
        P("dp"),
        P(None, "dp"),
        P("dp", None),
        P("dp", "tensor"),
        P("dp", "tensor"),
        P("dp", "tensor"),
        P("tensor", "dp"),
    )
    return jax.shard_map(
        local,
        mesh=mesh,
        in_specs=placed,
        out_specs=(P(), P("dp", "tensor"), P("dp", "tensor"), P("dp", "tensor"), P("tensor", "dp")),
        check_vma=False,
    )
```

```python
import math
import types

import jax
import jax.numpy as jnp
import numpy as np
from jax import lax
from jax.experimental import pallas as pl
from jax.experimental.pallas import tpu as pltpu
from jax.sharding import PartitionSpec as P

F32 = jnp.float32
BF16 = jnp.bfloat16
MESH = pl.DeviceIdType.MESH
HIGHEST = lax.Precision.HIGHEST
EPSILON = 1e-06
STEPS = 1000
FRAMES = 360
PADDED = 384
SCALE = 1.0 / math.sqrt(128)

INPUTS = [
    "states", "cap_len", "step_index", "motion_len", "gain", "q_gain", "k_gain", "cosine", "sine",
    "eq", "ek", "ev", "eo", "clean", "noise", "w_in", "vel", "wq", "wk", "wv", "wo",
]
OUTPUTS = ["loss", "packed"]

BUFFERS = dict(
    w_qkv=((4096, 768), BF16),
    w_out=((512, 4096), BF16),
    c0=((32, 1, 384), F32),
    gx=((8, 64, 512), BF16),
    wkv=((16, 2, 64, 512), BF16),
    zsb=((16, 2, 16, 256), BF16),
    zrb=((16, 2, 16, 256), BF16),
    zsf=((16, 2, 8, 384), F32),
    zrf=((16, 2, 8, 384), F32),
    pzb=((2, 2, 16, 256), BF16),
    pzf=((2, 2, 8, 384), F32),
    agb=((16, 2, 16, 256), BF16),
    agf=((2, 16, 2, 8, 256), F32),
    ra_send=((4, 64, 512), BF16),
    ra_recv=((4, 64, 512), BF16),
    rb_send=((4, 64, 512), BF16),
    rb_recv=((4, 64, 512), BF16),
    r_own=((4, 64, 512), F32),
    cap_own=((64, 512), BF16),
    caps=((4, 2, 64, 512), BF16),
    kvx_send=((64, 512), BF16),
    kvx_recv=((64, 512), BF16),
    blend=((PADDED, 256), BF16),
    query=((PADDED, 256), BF16),
    hid_v=((PADDED, 256), F32),
    va_send=((4, 48, 256), BF16),
    va_recv=((4, 48, 256), BF16),
    v_own=((4, 48, 256), F32),
    vb_send=((4, 48, 256), BF16),
    vb_recv=((4, 48, 256), BF16),
    vg=((8, 48, 256), BF16),
    dkx=((2, 2, 64, 256), BF16),
    dk=((4, 2, 64, 256), BF16),
    dv=((4, 2, 64, 256), BF16),
    cap_k=((4, 2, 64, 512), BF16),
    cap_v=((4, 4, 2, 64, 128), BF16),
    cap_kt=((512, 512), BF16),
    cap_vt=((4, 128, 512), BF16),
    blend_t=((256, PADDED), BF16),
    att_t=((256, PADDED), BF16),
    prob_t=((2, 64, PADDED), BF16),
    gk_send=((4, 128, 256), BF16),
    gk_recv=((4, 128, 256), BF16),
    gv_send=((4, 128, 256), BF16),
    gv_recv=((4, 128, 256), BF16),
    hs=((32, 16, 384), BF16),
    hr=((32, 16, 384), BF16),
    hg=((32, 16, 256), BF16),
)

SEMAPHORES = dict(
    load=4,
    c0_s=1, c0_r=1,
    gx_s=8, gx_r=8,
    wkv_s=32, wkv_r=(16, 2),
    zb_s=1, zb_r=1, zf_s=1, zf_r=1, pb_s=1, pb_r=1, pf_s=1, pf_r=1,
    ab_s=1, ab_r=1, af_s=1, af_r=1, ap_s=1, ap_r=1,
    ra_s=4, ra_r=4, rb_s=4, rb_r=4,
    cp_s=8, cp_r=(4, 2),
    kvx_s=1, kvx_r=1,
    va_s=1, va_r=1, vb_s=4, vb_r=4, vg_s=8, vg_r=8,
    dx_s=2, dx_r=2, dk_s=4, dk_r=4, dv_s=4, dv_r=4,
    ck_s=4, ck_r=4, cv_s=4, cv_r=4,
    gk_s=4, gk_r=4, gv_s=4, gv_r=4,
    hs_s=1, hs_r=1, hg_s=1, hg_r=1,
)


def dot(a, b, left, right, precision=None):
    return lax.dot_general(
        a, b, (((left,), (right,)), ((), ())), precision=precision, preferred_element_type=F32
    )


def nn(a, b, precision=None):
    return dot(a, b, 1, 0, precision)


def nt(a, b, precision=None):
    return dot(a, b, 1, 1, precision)


def tn(a, b, precision=None):
    return dot(a, b, 0, 0, precision)


def softmax(scores):
    top = jnp.max(scores, axis=-1, keepdims=True)
    weights = jnp.exp(scores - top)
    return weights / jnp.sum(weights, axis=-1, keepdims=True)


def remote(source, target, send, receive, dp, tensor):
    return pltpu.make_async_remote_copy(
        src_ref=source,
        dst_ref=target,
        send_sem=send,
        recv_sem=receive,
        device_id=(dp, tensor),
        device_id_type=MESH,
    )


def kernel(*refs):
    names = INPUTS + [n + "_out" for n in OUTPUTS] + list(BUFFERS) + list(SEMAPHORES)
    r = types.SimpleNamespace(**dict(zip(names, refs, strict=True)))

    d = lax.axis_index("dp")
    t = lax.axis_index("tensor")
    zl = lax.div(d, 16)
    xy = lax.rem(d, 16)
    x = lax.div(xy, 4)
    y = lax.rem(xy, 4)
    zh = lax.div(t, 2)
    c = lax.rem(t, 2)
    mate = t + 1 - 2 * c
    other = (1 - zl) * 16 + xy
    pending = []

    def start(copy):
        copy.start()
        pending.append(copy)

    def turn(base, k, size):
        return lax.rem(base + k, size)

    def plane(xx, yy):
        return zl * 16 + xx * 4 + yy

    def arrived(slot, semaphore):
        remote(slot, slot, semaphore, semaphore, other, t).wait_recv()

    def all_arrived(buffer, semaphore):
        most = buffer.at[pl.ds(0, 31)]
        remote(most, most, semaphore, semaphore, other, t).wait_recv()

    def all_left(buffer, semaphore):
        most = buffer.at[pl.ds(0, 31)]
        remote(most, most, semaphore, semaphore, other, t).wait_send()

    def plane_arrived(buffer, semaphore):
        most = buffer.at[pl.ds(0, 15)]
        remote(most, most, semaphore, semaphore, other, t).wait_recv()

    def plane_left(buffer, semaphore):
        most = buffer.at[pl.ds(0, 15)]
        remote(most, most, semaphore, semaphore, other, t).wait_send()

    def over_plane(body):
        def step(k, carry):
            body(turn(xy, k, 16))
            return carry

        lax.fori_loop(1, 16, step, 0)

    def over_dp(body):
        def step(k, carry):
            body(k, turn(d, k, 32))
            return carry

        lax.fori_loop(1, 32, step, 0)

    loads = [
        pltpu.make_async_copy(r.eq, r.w_qkv.at[:, pl.ds(0, 512)], r.load.at[0]),
        pltpu.make_async_copy(r.ek, r.w_qkv.at[:, pl.ds(512, 128)], r.load.at[1]),
        pltpu.make_async_copy(r.ev, r.w_qkv.at[:, pl.ds(640, 128)], r.load.at[2]),
        pltpu.make_async_copy(r.eo, r.w_out, r.load.at[3]),
    ]
    for load in loads:
        load.start()

    barrier = pltpu.get_barrier_semaphore()

    def signal(dp, tensor):
        pl.semaphore_signal(barrier, inc=1, device_id=(dp, tensor), device_id_type=MESH)

    over_dp(lambda k, peer: signal(peer, t))
    signal(d, mate)
    for k in (1, 2, 3):
        signal(d, turn(zh, k, 4) * 2 + c)
        signal(other, turn(zh, k, 4) * 2 + c)

    r.gx[t] = r.states[0]
    wk_v = r.wk[...]
    wv_v = r.wv[...]
    for half in (0, 1):
        r.wkv[xy, half, :, 0:256] = wk_v[64 * half : 64 * half + 64]
        r.wkv[xy, half, :, 256:512] = wv_v[64 * half : 64 * half + 64]
    w_in_v = r.w_in[...]
    w_in_t = w_in_v.astype(F32)
    decay = -math.log(10000.0) / 1024.0
    step_f = jnp.full((8, 128), r.step_index[0], jnp.int32).astype(F32)
    place = (
        lax.broadcasted_iota(jnp.int32, (8, 128), 0) * 128
        + lax.broadcasted_iota(jnp.int32, (8, 128), 1)
    ).astype(F32)
    all_angles = step_f * jnp.exp(decay * place)
    all_cos = jnp.cos(all_angles)
    all_sin = jnp.sin(all_angles)

    def total(tile):
        return jnp.sum(jnp.sum(tile, axis=1, keepdims=True), axis=0, keepdims=True)

    own_mean = total(all_cos + all_sin) / 2048.0
    time_square = total((all_cos - own_mean) ** 2 + (all_sin - own_mean) ** 2)
    lane = lax.broadcasted_iota(jnp.int32, (1, 128), 1)
    r.c0[d, :, 0:256] = jnp.sum(w_in_t, axis=0, keepdims=True)
    r.c0[d, :, 256:384] = jnp.where(lane == 0, step_f[0:1], own_mean)

    vel_v = r.vel[...]
    wq_v = r.wq[...]
    part_m = tn(r.wo[...], vel_v).reshape(32, 8, 256)
    part_b = tn(w_in_v, vel_v)

    pl.semaphore_wait(barrier, 38)

    for k in (2, 1, 3):
        start(remote(r.gx.at[t], r.gx.at[t], r.gx_s.at[k], r.gx_r.at[t], d, turn(zh, k, 4) * 2 + c))
    start(remote(r.gx.at[t], r.gx.at[t], r.gx_s.at[0], r.gx_r.at[t], d, mate))

    def wkv_send(slot, half, dp, index):
        ref = r.wkv.at[slot, half]
        start(remote(ref, ref, r.wkv_s.at[index], r.wkv_r.at[slot, half], dp, t))

    for k in (1, 3, 2):
        wkv_send(xy, 0, plane(turn(x, k, 4), y), k - 1)
        wkv_send(xy, 1, plane(x, turn(y, k, 4)), 2 + k)

    def c0_copy(k, peer):
        return remote(r.c0.at[d], r.c0.at[d], r.c0_s.at[0], r.c0_r.at[0], peer, t)

    over_dp(lambda k, peer: c0_copy(k, peer).start())

    def wkv_second(first, k_list):
        for k in k_list:
            if k:
                slot = turn(x, k, 4) * 4 + y
                arrived(r.wkv.at[slot, 0], r.wkv_r.at[slot, 0])
                slot = x * 4 + turn(y, k, 4)
                arrived(r.wkv.at[slot, 1], r.wkv_r.at[slot, 1])
            for j in (1, 3, 2):
                wkv_send(turn(x, k, 4) * 4 + y, 0, plane(x, turn(y, j, 4)), first + 6 * k + j - 1)
                wkv_send(
                    x * 4 + turn(y, k, 4), 1, plane(turn(x, j, 4), y), first + 6 * k + 2 + j
                )

    wkv_second(6, (0, 1, 3, 2))

    for load in loads[:3]:
        load.wait()

    def project(slot, sums, square):
        chunk = r.gx[slot].astype(F32)
        square = square + jnp.sum(chunk * chunk, axis=1, keepdims=True)
        row = pl.multiple_of(slot * 512, 512)
        scaled = (chunk * r.gain[slot]).astype(BF16)
        return sums + nn(scaled, r.w_qkv[pl.ds(row, 512), :]), square

    sums, square = project(t, jnp.zeros((64, 768), F32), jnp.zeros((64, 1), F32))

    all_arrived(r.c0, r.c0_r.at[0])
    facts = r.c0[...].reshape(32, 384)
    w_mean = jnp.sum(facts[:, 0:256], axis=0, keepdims=True) / 2048.0
    steps = facts[:, 256:257]
    step_means = facts[:, 257:258]
    column = (
        lax.broadcasted_iota(jnp.int32, (1, 64), 1) + lax.rem(d, 16) * 64
    ).astype(F32)
    angles = steps * jnp.exp(decay * column)
    quarter = jnp.full((32, 64), zl, jnp.int32).astype(F32) * (math.pi / 2.0)
    times = jnp.cos(angles - quarter)
    times_c = times - step_means
    w_c = w_in_t - w_mean
    part_a = tn(w_c.astype(BF16), wq_v).reshape(32, 8, 256)
    slabs_b = jnp.concatenate([part_a, part_m], axis=1).astype(BF16)
    first_core = jnp.full((256, 256), c, jnp.int32) == 0
    part_f = jnp.where(first_core, part_b, tn(w_c, w_c, HIGHEST))
    slabs_f = part_f.reshape(32, 8, 256)
    time_rows = jnp.concatenate(
        [
            nn(times_c, wq_v.astype(F32), HIGHEST),
            nn(times, vel_v.astype(F32), HIGHEST),
            nn(times_c, w_c, HIGHEST),
        ],
        axis=1,
    )
    for z in (0, 1):
        here = slice(16 * z, 16 * z + 16)
        r.zsb[:, z] = slabs_b[here]
        r.zsf[:, z, :, 0:256] = slabs_f[here]
        for i in range(8):
            part = time_rows[here, 128 * i : 128 * i + 128] if i < 6 else jnp.zeros((16, 128), F32)
            r.zsf[:, z, i, 256:384] = part
    r.zrb[xy] = r.zsb[xy]
    r.zrf[xy] = r.zsf[xy]

    def z_start(peer):
        dp = zl * 16 + peer
        remote(r.zsb.at[peer], r.zrb.at[xy], r.zb_s.at[0], r.zb_r.at[0], dp, t).start()
        remote(r.zsf.at[peer], r.zrf.at[xy], r.zf_s.at[0], r.zf_r.at[0], dp, t).start()

    for k in (1, 3, 2):
        slot = turn(zh, k, 4) * 2 + c
        arrived(r.gx.at[slot], r.gx_r.at[slot])
        start(remote(r.gx.at[slot], r.gx.at[slot], r.gx_s.at[4 + k], r.gx_r.at[slot], d, mate))
        sums, square = project(slot, sums, square)

    over_plane(z_start)

    arrived(r.gx.at[mate], r.gx_r.at[mate])
    sums, square = project(mate, sums, square)
    for k in (1, 3, 2):
        slot = turn(zh, k, 4) * 2 + (1 - c)
        arrived(r.gx.at[slot], r.gx_r.at[slot])
        sums, square = project(slot, sums, square)

    length = r.cap_len[0]
    rms = lax.rsqrt(square / 4096.0 + EPSILON)
    sums = sums * rms
    cosine = r.cosine[...]
    sine = r.sine[...]

    def turned(vectors, scaling):
        mean = jnp.mean(vectors * vectors, axis=1, keepdims=True)
        vectors = vectors * lax.rsqrt(mean + EPSILON) * scaling
        return (vectors * cosine + pltpu.roll(vectors, 64, 1) * sine).astype(BF16)

    q_gain = r.q_gain[...]
    queries = jnp.concatenate(
        [turned(sums[:, 128 * h : 128 * h + 128], q_gain) for h in range(4)], axis=0
    )
    keys = turned(sums[:, 512:640], r.k_gain[...])
    values = sums[:, 640:768].astype(BF16)
    scores = nt(queries, keys) * SCALE
    row = lax.rem(lax.broadcasted_iota(jnp.int32, (256, 64), 0), 64)
    col = lax.broadcasted_iota(jnp.int32, (256, 64), 1)
    scores = jnp.where((col <= row) & (col < length), scores, -1e30)
    mixed = nn(softmax(scores).astype(BF16), values).astype(BF16)
    mixed = jnp.concatenate([mixed[64 * h : 64 * h + 64] for h in range(4)], axis=1)

    loads[3].wait()
    for k in (1, 3, 2, 0):
        slot = turn(zh, k, 4)
        column = pl.multiple_of((slot * 2 + 1 - c) * 512, 512)
        r.ra_send[slot] = nn(mixed, r.w_out[:, pl.ds(column, 512)]).astype(BF16)
        start(
            remote(
                r.ra_send.at[slot], r.ra_recv.at[slot], r.ra_s.at[k], r.ra_r.at[slot], d, mate
            )
        )
    for k in (1, 3, 2, 0):
        slot = turn(zh, k, 4)
        column = pl.multiple_of((slot * 2 + c) * 512, 512)
        r.r_own[slot] = nn(mixed, r.w_out[:, pl.ds(column, 512)])
    for k in (2, 1, 3):
        slot = turn(zh, k, 4)
        arrived(r.ra_recv.at[slot], r.ra_r.at[slot])
        r.rb_send[slot] = (r.r_own[slot] + r.ra_recv[slot].astype(F32)).astype(BF16)
        start(
            remote(
                r.rb_send.at[slot], r.rb_recv.at[zh], r.rb_s.at[k], r.rb_r.at[zh], d, slot * 2 + c
            )
        )

    slot = zh
    arrived(r.ra_recv.at[slot], r.ra_r.at[slot])
    own = r.r_own[slot] + r.ra_recv[slot].astype(F32)
    for k in (1, 3, 2):
        slot = turn(zh, k, 4)
        arrived(r.rb_recv.at[slot], r.rb_r.at[slot])
        own = own + r.rb_recv[slot].astype(F32)
    r.cap_own[...] = (r.states[0].astype(F32) + own).astype(BF16)

    target = lax.div(zh, 2)
    mine = lax.rem(t, 4)
    inside = target == zl

    def cap_copy(k):
        return remote(
            r.cap_own,
            r.caps.at[mine, zl],
            r.cp_s.at[k],
            r.cp_r.at[mine, zl],
            target * 16 + xy,
            turn(zh, k, 4) * 2 + c,
        )

    for k in (2, 1, 3):
        start(cap_copy(k))

    @pl.when(inside)
    def _():
        r.caps[mine, zl] = r.cap_own[...]

    @pl.when(jnp.logical_not(inside))
    def _():
        cap_copy(0).start()

    plane_arrived(r.zrb, r.zb_r.at[0])
    plane_arrived(r.zrf, r.zf_r.at[0])
    plane_b = jnp.sum(r.zrb[...].astype(F32), axis=0)
    plane_f = jnp.sum(r.zrf[...], axis=0)
    r.pzb[zl] = plane_b.astype(BF16)
    r.pzf[zl] = plane_f
    start(remote(r.pzb.at[zl], r.pzb.at[zl], r.pb_s.at[0], r.pb_r.at[0], other, t))
    start(remote(r.pzf.at[zl], r.pzf.at[zl], r.pf_s.at[0], r.pf_r.at[0], other, t))

    for k in (0, 1, 2, 3):
        for j in (1, 2, 3):
            slot = turn(x, k, 4) * 4 + turn(y, j, 4)
            arrived(r.wkv.at[slot, 0], r.wkv_r.at[slot, 0])
            slot = turn(x, j, 4) * 4 + turn(y, k, 4)
            arrived(r.wkv.at[slot, 1], r.wkv_r.at[slot, 1])

    forwards = []
    for z in (0, 1):
        for near in (0, 1):
            chunk = near * 2 + c
            ref = r.caps.at[chunk, z]
            own_slot = inside & (chunk == mine) & (z == zl)

            @pl.when(jnp.logical_not(own_slot))
            def _(ref=ref, chunk=chunk, z=z):
                arrived(ref, r.cp_r.at[chunk, z])

            start(remote(ref, ref, r.cp_s.at[4 + 2 * z + near], r.cp_r.at[chunk, z], d, mate))

    arrived(r.pzb.at[1 - zl], r.pb_r.at[0])
    arrived(r.pzf.at[1 - zl], r.pf_r.at[0])
    r.agb[xy] = (plane_b + r.pzb[1 - zl].astype(F32)).astype(BF16)
    slabs = plane_f + r.pzf[1 - zl]
    r.agf[c, xy] = slabs[:, :, 0:256]
    late = jnp.full((8, 128), zl, jnp.int32) == 1
    rows = jnp.where(late, slabs[1, :, 256:384], slabs[0, :, 256:384])
    time_own = jnp.concatenate([rows[i : i + 1] for i in range(6)], axis=1)

    def a_start(peer):
        dp = zl * 16 + peer
        remote(r.agb.at[xy], r.agb.at[xy], r.ab_s.at[0], r.ab_r.at[0], dp, t).start()
        remote(r.agf.at[c, xy], r.agf.at[c, xy], r.af_s.at[0], r.af_r.at[0], dp, t).start()

    over_plane(a_start)

    def project_caption(chunk):
        rows = r.caps[chunk].reshape(128, 512)
        weights = r.wkv[pl.ds(chunk * 4, 4)].reshape(512, 512)
        return nn(rows, weights)

    both = project_caption(c) + project_caption(2 + c)
    for near in (0, 1):
        for z in (0, 1):
            chunk = near * 2 + 1 - c
            arrived(r.caps.at[chunk, z], r.cp_r.at[chunk, z])
        both = both + project_caption(near * 2 + 1 - c)
    second = jnp.full((64, 512), zl, jnp.int32) == 1
    r.kvx_send[...] = jnp.where(second, both[0:64], both[64:128]).astype(BF16)
    start(remote(r.kvx_send, r.kvx_recv, r.kvx_s.at[0], r.kvx_r.at[0], other, t))

    r.cap_k[x] = r.caps[x]
    for q in range(4):
        column = pl.multiple_of(y * 128, 128)
        r.cap_v[y, q] = r.caps[q, :, :, pl.ds(column, 128)]
    for k in (1, 3, 2):
        xx = turn(x, k, 4)
        start(
            remote(r.caps.at[xx], r.cap_k.at[x], r.ck_s.at[k], r.ck_r.at[x], plane(xx, y), t)
        )
        yy = turn(y, k, 4)
        column = pl.multiple_of(yy * 128, 128)
        start(
            remote(
                r.caps.at[:, :, :, pl.ds(column, 128)],
                r.cap_v.at[y],
                r.cv_s.at[k],
                r.cv_r.at[y],
                plane(x, yy),
                t,
            )
        )

    clean = r.clean[0].astype(F32)
    noise = r.noise[0].astype(F32)
    tau = jnp.full((1, 256), r.step_index[0], jnp.int32).astype(F32) / STEPS
    margin = jnp.zeros((PADDED - FRAMES, 256), F32)
    blend_f = jnp.concatenate([(1.0 - tau) * clean + tau * noise, margin], axis=0)
    r.blend[...] = blend_f.astype(BF16)
    blend = r.blend[...]
    blend_f = blend.astype(F32)
    plane_arrived(r.agb, r.ab_r.at[0])
    plane_arrived(r.agf.at[c], r.af_r.at[0])
    start(remote(r.agf.at[c], r.agf.at[c], r.ap_s.at[0], r.ap_r.at[0], d, mate))
    matrices = r.agb[...].astype(F32)

    def planes(slabs):
        return jnp.concatenate([slabs[:, z].reshape(128, 256) for z in (0, 1)], axis=0)

    mat_a = planes(matrices[:, :, 0:8]).astype(BF16)
    mat_m = planes(matrices[:, :, 8:16]).astype(BF16)
    arrived(r.agf.at[1 - c], r.ap_r.at[0])
    mat_b = planes(r.agf[0])
    mat_s = planes(r.agf[1])
    r.hid_v[...] = nn(blend_f, mat_b, HIGHEST) + time_own[:, 256:512]
    spread = (nn(blend_f, mat_s, HIGHEST) + 2.0 * time_own[:, 512:768]) * blend_f
    variance = (jnp.sum(spread, axis=1, keepdims=True) + time_square) / 2048.0
    rstd = lax.rsqrt(jnp.maximum(variance, 0.0) + EPSILON)
    r.query[...] = ((nn(blend, mat_a) + time_own[:, 0:256]) * rstd).astype(BF16)

    kv_own = jnp.where(second, both[64:128], both[0:64])
    arrived(r.kvx_recv, r.kvx_r.at[0])
    kv = (kv_own + r.kvx_recv[...].astype(F32)).astype(BF16)

    query = r.query[...]
    allowed = lax.broadcasted_iota(jnp.int32, (PADDED, 64), 1) < length
    probs = []
    attended = []
    for h in (0, 1):
        span = slice(128 * h, 128 * h + 128)
        scores = nt(query[:, span], kv[:, span]) * SCALE
        prob = softmax(jnp.where(allowed, scores, -1e30))
        probs.append(prob)
        attended.append(nn(prob.astype(BF16), kv[:, 256 + 128 * h : 384 + 128 * h]).astype(BF16))
    attended = jnp.concatenate(attended, axis=1)
    branch = nn(attended, mat_m).reshape(8, 48, 256)

    first_half = jnp.full((48, 256), c, jnp.int32) == 0
    for q in range(4):
        r.va_send[q] = jnp.where(first_half, branch[2 * q + 1], branch[2 * q]).astype(BF16)
        r.v_own[q] = jnp.where(first_half, branch[2 * q], branch[2 * q + 1])
    start(remote(r.va_send, r.va_recv, r.va_s.at[0], r.va_r.at[0], d, mate))
    r.att_t[...] = attended.T
    for h in (0, 1):
        r.prob_t[h] = probs[h].astype(BF16).T
    arrived(r.va_recv, r.va_r.at[0])
    for k in (2, 1, 3):
        slot = turn(zh, k, 4)
        r.vb_send[slot] = (r.v_own[slot] + r.va_recv[slot].astype(F32)).astype(BF16)
        start(
            remote(
                r.vb_send.at[slot], r.vb_recv.at[zh], r.vb_s.at[k], r.vb_r.at[zh], d, slot * 2 + c
            )
        )
    r.blend_t[...] = blend.T
    for k in (1, 3, 2):
        slot = turn(x, k, 4)
        arrived(r.cap_k.at[slot], r.ck_r.at[slot])
    r.cap_kt[...] = r.cap_k[...].reshape(512, 512).T
    own = r.v_own[zh] + r.va_recv[zh].astype(F32)
    for k in (1, 3, 2):
        slot = turn(zh, k, 4)
        arrived(r.vb_recv.at[slot], r.vb_r.at[slot])
        own = own + r.vb_recv[slot].astype(F32)
    r.vg[t] = own.astype(BF16)
    for k in (2, 1, 3):
        start(remote(r.vg.at[t], r.vg.at[t], r.vg_s.at[k], r.vg_r.at[t], d, turn(zh, k, 4) * 2 + c))
    start(remote(r.vg.at[t], r.vg.at[t], r.vg_s.at[0], r.vg_r.at[t], d, mate))
    for k in (1, 3, 2):
        slot = turn(y, k, 4)
        arrived(r.cap_v.at[slot], r.cv_r.at[slot])
    for q in range(4):
        r.cap_vt[q] = r.cap_v[:, q].reshape(512, 128).T
    for k in (1, 3, 2):
        slot = turn(zh, k, 4) * 2 + c
        arrived(r.vg.at[slot], r.vg_r.at[slot])
        start(remote(r.vg.at[slot], r.vg.at[slot], r.vg_s.at[4 + k], r.vg_r.at[slot], d, mate))
    arrived(r.vg.at[mate], r.vg_r.at[mate])
    for k in (1, 3, 2):
        slot = turn(zh, k, 4) * 2 + 1 - c
        arrived(r.vg.at[slot], r.vg_r.at[slot])

    predicted = r.hid_v[...] + r.vg[...].astype(F32).reshape(PADDED, 256)
    residual = predicted - jnp.concatenate([noise - clean, margin], axis=0)
    frames = jnp.full((PADDED, 1), r.motion_len[0], jnp.int32)
    live = lax.broadcasted_iota(jnp.int32, (PADDED, 1), 0) < frames
    row_weight = jnp.where(live, 1.0 / frames.astype(F32), 0.0)
    weighted = residual * row_weight
    loss_part = total(residual * weighted)
    d_vel = (2.0 * weighted).astype(BF16)
    d_att = nt(d_vel, mat_m).astype(BF16)

    heads = [d_att[:, 128 * h : 128 * h + 128] for h in (0, 1)]
    d_values = [nn(r.prob_t[h], heads[h]) for h in (0, 1)]
    r.dkx[1, zl] = jnp.concatenate(d_values, axis=1).astype(BF16)

    def dx_start(i):
        ref = r.dkx.at[i, zl]
        start(remote(ref, ref, r.dx_s.at[i], r.dx_r.at[i], other, t))

    dx_start(1)
    d_scores = []
    for h in (0, 1):
        d_prob = nt(heads[h], kv[:, 256 + 128 * h : 384 + 128 * h])
        delta = jnp.sum(probs[h] * d_prob, axis=1, keepdims=True)
        d_scores.append((probs[h] * (d_prob - delta) * SCALE).astype(BF16))
    d_keys = [tn(d_scores[h], query[:, 128 * h : 128 * h + 128]) for h in (0, 1)]
    r.dkx[0, zl] = jnp.concatenate(d_keys, axis=1).astype(BF16)
    dx_start(0)
    d_queries = [nn(d_scores[h], kv[:, 128 * h : 128 * h + 128]) for h in (0, 1)]
    d_query = jnp.concatenate(d_queries, axis=1).astype(BF16).astype(F32) * rstd
    mat_h = nn(r.blend_t[...], d_query.astype(BF16)).reshape(32, 8, 256)
    mat_g = nn(r.att_t[...], d_vel).reshape(32, 8, 256)
    r.hs[:, :, 0:256] = jnp.concatenate([mat_h, mat_g], axis=1).astype(BF16)
    frame_sum = jnp.sum(d_query, axis=0, keepdims=True)
    loss_high = loss_part.astype(BF16).astype(F32)
    which = lax.broadcasted_iota(jnp.int32, (16, 128), 0)
    extra = jnp.where(which == 2, loss_high, loss_part - loss_high)
    extra = jnp.where(which == 1, frame_sum[:, 128:256], extra)
    extra = jnp.where(which == 0, frame_sum[:, 0:128], extra)
    r.hs[:, :, 256:384] = jnp.broadcast_to(extra.astype(BF16)[None], (32, 16, 128))
    r.hr[d] = r.hs[d]

    def h_copy(k, peer):
        return remote(r.hs.at[peer], r.hr.at[d], r.hs_s.at[0], r.hs_r.at[0], peer, t)

    over_dp(lambda k, peer: h_copy(k, peer).start())

    arrived(r.dkx.at[1, 1 - zl], r.dx_r.at[1])
    r.dv[y] = r.dkx[1]
    for k in (1, 3, 2):
        start(
            remote(
                r.dv.at[y], r.dv.at[y], r.dv_s.at[k], r.dv_r.at[y], plane(x, turn(y, k, 4)), t
            )
        )
    arrived(r.dkx.at[0, 1 - zl], r.dx_r.at[0])
    r.dk[x] = r.dkx[0]
    for k in (1, 3, 2):
        start(
            remote(
                r.dk.at[x], r.dk.at[x], r.dk_s.at[k], r.dk_r.at[x], plane(turn(x, k, 4), y), t
            )
        )

    all_arrived(r.hr, r.hs_r.at[0])
    arrivals = r.hr[...].astype(F32)
    r.hg[d] = jnp.sum(arrivals[:, :, 0:256], axis=0).astype(BF16)

    def g_copy(k, peer):
        return remote(r.hg.at[d], r.hg.at[d], r.hg_s.at[0], r.hg_r.at[0], peer, t)

    over_dp(lambda k, peer: g_copy(k, peer).start())

    for k in (1, 3, 2):
        slot = turn(y, k, 4)
        arrived(r.dv.at[slot], r.dv_r.at[slot])
    all_v = r.dv[...].reshape(512, 256)
    for q in range(4):
        r.gv_send[q] = nn(r.cap_vt[q], all_v).astype(BF16)
    for k in (1, 3, 2):
        xx = turn(x, k, 4)
        start(
            remote(
                r.gv_send.at[xx], r.gv_recv.at[x], r.gv_s.at[k], r.gv_r.at[x], plane(xx, y), t
            )
        )
    r.gv_recv[x] = r.gv_send[x]
    for k in (1, 3, 2):
        slot = turn(x, k, 4)
        arrived(r.dk.at[slot], r.dk_r.at[slot])
    all_k = r.dk[...].reshape(512, 256)
    grad_k = nn(r.cap_kt[...], all_k).reshape(4, 128, 256)
    for q in range(4):
        r.gk_send[q] = grad_k[q].astype(BF16)
    for k in (1, 3, 2):
        yy = turn(y, k, 4)
        start(
            remote(
                r.gk_send.at[yy], r.gk_recv.at[y], r.gk_s.at[k], r.gk_r.at[y], plane(x, yy), t
            )
        )
    r.gk_recv[y] = r.gk_send[y]

    sums_p = jnp.concatenate([arrivals[:, 0, 256:384], arrivals[:, 1, 256:384]], axis=1)
    losses = arrivals[:, 2, 256:384] + arrivals[:, 3, 256:384]
    r.loss_out[...] = jnp.sum(losses, axis=0, keepdims=True) / 8192.0
    all_arrived(r.hg, r.hg_r.at[0])
    grads = r.hg[...].astype(F32)
    sum_h = grads[:, 0:8].reshape(256, 256)
    sum_g = grads[:, 8:16].reshape(256, 256).astype(BF16)
    r.packed_out[0:64] = nn(w_c, sum_h, HIGHEST) + tn(times_c, sums_p, HIGHEST)
    r.packed_out[320:384] = nt(r.vel[...], sum_g)
    for k in (1, 3, 2):
        slot = turn(y, k, 4)
        arrived(r.gk_recv.at[slot], r.gk_r.at[slot])
        slot = turn(x, k, 4)
        arrived(r.gv_recv.at[slot], r.gv_r.at[slot])
    r.packed_out[64:192] = jnp.sum(r.gk_recv[...].astype(F32), axis=0)
    r.packed_out[192:320] = jnp.sum(r.gv_recv[...].astype(F32), axis=0)

    for copy in pending:
        copy.wait_send()

    @pl.when(jnp.logical_not(inside))
    def _():
        cap_copy(0).wait_send()

    all_left(r.c0, r.c0_s.at[0])
    plane_left(r.zrb, r.zb_s.at[0])
    plane_left(r.zrf, r.zf_s.at[0])
    plane_left(r.agb, r.ab_s.at[0])
    plane_left(r.agf.at[c], r.af_s.at[0])
    all_left(r.hr, r.hs_s.at[0])
    all_left(r.hg, r.hg_s.at[0])


def unpack(loss, packed, loss_out, gq, gk, gv, go):
    loss_out[...] = loss[...]
    gq[...] = packed[0:64]
    gk[...] = packed[64:192]
    gv[...] = packed[192:320]
    go[...] = packed[320:384]


def rope_tables():
    inverse = 1000000.0 ** (-(np.arange(64, dtype=np.float32) * 2.0 / 128))
    angles = np.arange(64, dtype=np.float32)[:, None] * inverse[None, :].astype(np.float32)
    angles = np.concatenate([angles, angles], axis=1).astype(np.float32)
    sign = np.where(np.arange(128) < 64, -1.0, 1.0)[None, :]
    return np.cos(angles).astype(np.float32), (np.sin(angles) * sign).astype(np.float32)


def local(
    encoder_input_states,
    caption_lengths,
    encoder_input_gain,
    query_head_gain,
    key_head_gain,
    encoder_query_weight,
    encoder_key_weight,
    encoder_value_weight,
    encoder_output_weight,
    clean_motion,
    noise,
    timestep_index,
    motion_lengths,
    input_weight,
    velocity_weight,
    cross_query_weight,
    cross_key_weight,
    cross_value_weight,
    cross_output_weight,
):
    vmem = pl.BlockSpec(memory_space=pltpu.VMEM)
    hbm = pl.BlockSpec(memory_space=pl.ANY)
    smem = pl.BlockSpec(memory_space=pltpu.SMEM)
    spec = {name: vmem for name in INPUTS}
    for name in ("cap_len", "step_index", "motion_len"):
        spec[name] = smem
    for name in ("eq", "ek", "ev", "eo"):
        spec[name] = hbm
    cosine, sine = rope_tables()
    packed = pl.pallas_call(
        kernel,
        out_shape=[
            jax.ShapeDtypeStruct((1, 128), F32),
            jax.ShapeDtypeStruct((384, 256), F32),
        ],
        in_specs=[spec[name] for name in INPUTS],
        out_specs=[vmem] * 2,
        scratch_shapes=[pltpu.VMEM(shape, kind) for shape, kind in BUFFERS.values()]
        + [
            pltpu.SemaphoreType.DMA(shape if isinstance(shape, tuple) else (shape,))
            for shape in SEMAPHORES.values()
        ],
        compiler_params=pltpu.CompilerParams(
            collective_id=0, has_side_effects=True, vmem_limit_bytes=56 * 2**20
        ),
        name="motion_block",
    )(
        encoder_input_states,
        caption_lengths,
        timestep_index,
        motion_lengths,
        encoder_input_gain.reshape(8, 1, 512),
        query_head_gain.reshape(1, 128),
        key_head_gain.reshape(1, 128),
        jnp.asarray(cosine),
        jnp.asarray(sine),
        encoder_query_weight,
        encoder_key_weight,
        encoder_value_weight,
        encoder_output_weight,
        clean_motion,
        noise,
        input_weight.T,
        velocity_weight,
        cross_query_weight,
        cross_key_weight,
        cross_value_weight,
        cross_output_weight.T,
    )
    loss, gq, gk, gv, go = pl.pallas_call(
        unpack,
        out_shape=[
            jax.ShapeDtypeStruct((1, 128), F32),
            jax.ShapeDtypeStruct((64, 256), F32),
            jax.ShapeDtypeStruct((128, 256), F32),
            jax.ShapeDtypeStruct((128, 256), F32),
            jax.ShapeDtypeStruct((64, 256), F32),
        ],
        in_specs=[vmem] * 2,
        out_specs=[vmem] * 5,
        name="unpack",
    )(*packed)
    return (loss[0, 0], gq, gk, gv, go.T)


def solution(mesh):
    placed = (
        P("dp", None, "tensor"),
        P("dp"),
        P(),
        P(),
        P(),
        P(None, "tensor"),
        P(None, "tensor"),
        P(None, "tensor"),
        P("tensor", None),
        P("dp", None, None),
        P("dp", None, None),
        P("dp"),
        P("dp"),
        P(None, "dp"),
        P("dp", None),
        P("dp", "tensor"),
        P("dp", "tensor"),
        P("dp", "tensor"),
        P("tensor", "dp"),
    )
    return jax.shard_map(
        local,
        mesh=mesh,
        in_specs=placed,
        out_specs=(P(), P("dp", "tensor"), P("dp", "tensor"), P("dp", "tensor"), P("tensor", "dp")),
        check_vma=False,
    )
```

```python
import math
import types

import jax
import jax.numpy as jnp
import numpy as np
from jax import lax
from jax.experimental import pallas as pl
from jax.experimental.pallas import tpu as pltpu
from jax.sharding import PartitionSpec as P

F32 = jnp.float32
BF16 = jnp.bfloat16
MESH = pl.DeviceIdType.MESH
HIGHEST = lax.Precision.HIGHEST
EPSILON = 1e-06
STEPS = 1000
FRAMES = 360
PADDED = 384
SCALE = 1.0 / math.sqrt(128)

INPUTS = [
    "states", "cap_len", "step_index", "motion_len", "gain", "q_gain", "k_gain", "cosine", "sine",
    "eq", "ek", "ev", "eo", "clean", "noise", "w_in", "vel", "wq", "wk", "wv", "wo",
]
OUTPUTS = ["loss", "packed"]

BUFFERS = dict(
    w_qkv=((4096, 768), BF16),
    w_out=((512, 4096), BF16),
    c0=((32, 1, 384), F32),
    gx=((8, 64, 512), BF16),
    wkv=((16, 2, 64, 512), BF16),
    zsb=((16, 2, 16, 256), BF16),
    zrb=((16, 2, 16, 256), BF16),
    zsf=((16, 2, 8, 384), F32),
    zrf=((16, 2, 8, 384), F32),
    pzb=((2, 2, 16, 256), BF16),
    pzf=((2, 2, 8, 384), F32),
    agb=((16, 2, 16, 256), BF16),
    agf=((2, 16, 2, 8, 256), F32),
    ra_send=((4, 64, 512), BF16),
    ra_recv=((4, 64, 512), BF16),
    rb_send=((4, 64, 512), BF16),
    rb_recv=((4, 64, 512), BF16),
    r_own=((4, 64, 512), F32),
    cap_own=((64, 512), BF16),
    caps=((4, 2, 64, 512), BF16),
    kvx_send=((64, 512), BF16),
    kvx_recv=((64, 512), BF16),
    blend=((PADDED, 256), BF16),
    query=((PADDED, 256), BF16),
    hid_v=((PADDED, 256), F32),
    va_send=((4, 48, 256), BF16),
    va_recv=((4, 48, 256), BF16),
    v_own=((4, 48, 256), F32),
    vb_send=((4, 48, 256), BF16),
    vb_recv=((4, 48, 256), BF16),
    vg=((8, 48, 256), BF16),
    dkx=((2, 2, 64, 256), BF16),
    dk=((4, 2, 64, 256), BF16),
    dv=((4, 2, 64, 256), BF16),
    cap_k=((4, 2, 64, 512), BF16),
    cap_v=((4, 4, 2, 64, 128), BF16),
    cap_kt=((512, 512), BF16),
    cap_vt=((4, 128, 512), BF16),
    blend_t=((256, PADDED), BF16),
    att_t=((256, PADDED), BF16),
    prob_t=((2, 64, PADDED), BF16),
    gk_send=((4, 128, 256), BF16),
    gk_recv=((4, 128, 256), BF16),
    gv_send=((4, 128, 256), BF16),
    gv_recv=((4, 128, 256), BF16),
    hs=((32, 16, 384), BF16),
    hr=((32, 16, 384), BF16),
    hg=((32, 16, 256), BF16),
)

SEMAPHORES = dict(
    load=4,
    c0_s=1, c0_r=1,
    gx_s=8, gx_r=8,
    wkv_s=32, wkv_r=(16, 2),
    zb_s=1, zb_r=1, zf_s=1, zf_r=1, pb_s=1, pb_r=1, pf_s=1, pf_r=1,
    ab_s=1, ab_r=1, af_s=1, af_r=1, ap_s=1, ap_r=1,
    ra_s=4, ra_r=4, rb_s=4, rb_r=4,
    cp_s=8, cp_r=(4, 2),
    kvx_s=1, kvx_r=1,
    va_s=1, va_r=1, vb_s=4, vb_r=4, vg_s=8, vg_r=8,
    dx_s=2, dx_r=2, dk_s=4, dk_r=4, dv_s=4, dv_r=4,
    ck_s=4, ck_r=4, cv_s=4, cv_r=4,
    gk_s=4, gk_r=4, gv_s=4, gv_r=4,
    hs_s=1, hs_r=1, hg_s=1, hg_r=1,
)


def dot(a, b, left, right, precision=None):
    return lax.dot_general(
        a, b, (((left,), (right,)), ((), ())), precision=precision, preferred_element_type=F32
    )


def nn(a, b, precision=None):
    return dot(a, b, 1, 0, precision)


def nt(a, b, precision=None):
    return dot(a, b, 1, 1, precision)


def tn(a, b, precision=None):
    return dot(a, b, 0, 0, precision)


def softmax(scores):
    top = jnp.max(scores, axis=-1, keepdims=True)
    weights = jnp.exp(scores - top)
    return weights / jnp.sum(weights, axis=-1, keepdims=True)


def remote(source, target, send, receive, dp, tensor):
    return pltpu.make_async_remote_copy(
        src_ref=source,
        dst_ref=target,
        send_sem=send,
        recv_sem=receive,
        device_id=(dp, tensor),
        device_id_type=MESH,
    )


def kernel(*refs):
    names = INPUTS + [n + "_out" for n in OUTPUTS] + list(BUFFERS) + list(SEMAPHORES)
    r = types.SimpleNamespace(**dict(zip(names, refs, strict=True)))

    d = lax.axis_index("dp")
    t = lax.axis_index("tensor")
    zl = lax.div(d, 16)
    xy = lax.rem(d, 16)
    x = lax.div(xy, 4)
    y = lax.rem(xy, 4)
    zh = lax.div(t, 2)
    c = lax.rem(t, 2)
    mate = t + 1 - 2 * c
    other = (1 - zl) * 16 + xy
    pending = []

    def start(copy):
        copy.start()
        pending.append(copy)

    def turn(base, k, size):
        return lax.rem(base + k, size)

    def plane(xx, yy):
        return zl * 16 + xx * 4 + yy

    def arrived(slot, semaphore):
        remote(slot, slot, semaphore, semaphore, other, t).wait_recv()

    def all_arrived(buffer, semaphore):
        most = buffer.at[pl.ds(0, 31)]
        remote(most, most, semaphore, semaphore, other, t).wait_recv()

    def all_left(buffer, semaphore):
        most = buffer.at[pl.ds(0, 31)]
        remote(most, most, semaphore, semaphore, other, t).wait_send()

    def plane_arrived(buffer, semaphore):
        most = buffer.at[pl.ds(0, 15)]
        remote(most, most, semaphore, semaphore, other, t).wait_recv()

    def plane_left(buffer, semaphore):
        most = buffer.at[pl.ds(0, 15)]
        remote(most, most, semaphore, semaphore, other, t).wait_send()

    def over_plane(body):
        def step(k, carry):
            body(turn(xy, k, 16))
            return carry

        lax.fori_loop(1, 16, step, 0)

    def over_dp(body):
        def step(k, carry):
            body(k, turn(d, k, 32))
            return carry

        lax.fori_loop(1, 32, step, 0)

    loads = [
        pltpu.make_async_copy(r.eq, r.w_qkv.at[:, pl.ds(0, 512)], r.load.at[0]),
        pltpu.make_async_copy(r.ek, r.w_qkv.at[:, pl.ds(512, 128)], r.load.at[1]),
        pltpu.make_async_copy(r.ev, r.w_qkv.at[:, pl.ds(640, 128)], r.load.at[2]),
        pltpu.make_async_copy(r.eo, r.w_out, r.load.at[3]),
    ]
    for load in loads:
        load.start()

    barrier = pltpu.get_barrier_semaphore()

    def signal(dp, tensor):
        pl.semaphore_signal(barrier, inc=1, device_id=(dp, tensor), device_id_type=MESH)

    over_dp(lambda k, peer: signal(peer, t))
    signal(d, mate)
    for k in (1, 2, 3):
        signal(d, turn(zh, k, 4) * 2 + c)
        signal(other, turn(zh, k, 4) * 2 + c)

    r.gx[t] = r.states[0]
    wk_v = r.wk[...]
    wv_v = r.wv[...]
    for half in (0, 1):
        r.wkv[xy, half, :, 0:256] = wk_v[64 * half : 64 * half + 64]
        r.wkv[xy, half, :, 256:512] = wv_v[64 * half : 64 * half + 64]
    w_in_v = r.w_in[...]
    w_in_t = w_in_v.astype(F32)
    decay = -math.log(10000.0) / 1024.0
    step_f = jnp.full((8, 128), r.step_index[0], jnp.int32).astype(F32)
    place = (
        lax.broadcasted_iota(jnp.int32, (8, 128), 0) * 128
        + lax.broadcasted_iota(jnp.int32, (8, 128), 1)
    ).astype(F32)
    all_angles = step_f * jnp.exp(decay * place)
    all_cos = jnp.cos(all_angles)
    all_sin = jnp.sin(all_angles)

    def total(tile):
        return jnp.sum(jnp.sum(tile, axis=1, keepdims=True), axis=0, keepdims=True)

    own_mean = total(all_cos + all_sin) / 2048.0
    time_square = total((all_cos - own_mean) ** 2 + (all_sin - own_mean) ** 2)
    lane = lax.broadcasted_iota(jnp.int32, (1, 128), 1)
    r.c0[d, :, 0:256] = jnp.sum(w_in_t, axis=0, keepdims=True)
    r.c0[d, :, 256:384] = jnp.where(lane == 0, step_f[0:1], own_mean)

    vel_v = r.vel[...]
    wq_v = r.wq[...]
    part_m = tn(r.wo[...], vel_v).reshape(32, 8, 256)
    part_b = tn(w_in_v, vel_v)

    pl.semaphore_wait(barrier, 38)

    for k in (2, 1, 3):
        start(remote(r.gx.at[t], r.gx.at[t], r.gx_s.at[k], r.gx_r.at[t], d, turn(zh, k, 4) * 2 + c))
    start(remote(r.gx.at[t], r.gx.at[t], r.gx_s.at[0], r.gx_r.at[t], d, mate))

    def wkv_send(slot, half, dp, index):
        ref = r.wkv.at[slot, half]
        start(remote(ref, ref, r.wkv_s.at[index], r.wkv_r.at[slot, half], dp, t))

    for k in (1, 3, 2):
        wkv_send(xy, 0, plane(turn(x, k, 4), y), k - 1)
        wkv_send(xy, 1, plane(x, turn(y, k, 4)), 2 + k)

    def c0_copy(k, peer):
        return remote(r.c0.at[d], r.c0.at[d], r.c0_s.at[0], r.c0_r.at[0], peer, t)

    over_dp(lambda k, peer: c0_copy(k, peer).start())

    def wkv_second(first, k_list):
        for k in k_list:
            if k:
                slot = turn(x, k, 4) * 4 + y
                arrived(r.wkv.at[slot, 0], r.wkv_r.at[slot, 0])
                slot = x * 4 + turn(y, k, 4)
                arrived(r.wkv.at[slot, 1], r.wkv_r.at[slot, 1])
            for j in (1, 3, 2):
                wkv_send(turn(x, k, 4) * 4 + y, 0, plane(x, turn(y, j, 4)), first + 6 * k + j - 1)
                wkv_send(
                    x * 4 + turn(y, k, 4), 1, plane(turn(x, j, 4), y), first + 6 * k + 2 + j
                )

    wkv_second(6, (0, 1, 3, 2))

    for load in loads[:3]:
        load.wait()

    def project(slot, sums, square):
        chunk = r.gx[slot].astype(F32)
        square = square + jnp.sum(chunk * chunk, axis=1, keepdims=True)
        row = pl.multiple_of(slot * 512, 512)
        scaled = (chunk * r.gain[slot]).astype(BF16)
        return sums + nn(scaled, r.w_qkv[pl.ds(row, 512), :]), square

    sums, square = project(t, jnp.zeros((64, 768), F32), jnp.zeros((64, 1), F32))

    for k in (1, 3, 2):
        slot = turn(zh, k, 4) * 2 + c
        arrived(r.gx.at[slot], r.gx_r.at[slot])
        start(remote(r.gx.at[slot], r.gx.at[slot], r.gx_s.at[4 + k], r.gx_r.at[slot], d, mate))
        sums, square = project(slot, sums, square)

    arrived(r.gx.at[mate], r.gx_r.at[mate])
    sums, square = project(mate, sums, square)
    for k in (1, 3, 2):
        slot = turn(zh, k, 4) * 2 + (1 - c)
        arrived(r.gx.at[slot], r.gx_r.at[slot])
        sums, square = project(slot, sums, square)

    length = r.cap_len[0]
    rms = lax.rsqrt(square / 4096.0 + EPSILON)
    sums = sums * rms
    cosine = r.cosine[...]
    sine = r.sine[...]

    def turned(vectors, scaling):
        mean = jnp.mean(vectors * vectors, axis=1, keepdims=True)
        vectors = vectors * lax.rsqrt(mean + EPSILON) * scaling
        return (vectors * cosine + pltpu.roll(vectors, 64, 1) * sine).astype(BF16)

    q_gain = r.q_gain[...]
    queries = jnp.concatenate(
        [turned(sums[:, 128 * h : 128 * h + 128], q_gain) for h in range(4)], axis=0
    )
    keys = turned(sums[:, 512:640], r.k_gain[...])
    values = sums[:, 640:768].astype(BF16)
    scores = nt(queries, keys) * SCALE
    row = lax.rem(lax.broadcasted_iota(jnp.int32, (256, 64), 0), 64)
    col = lax.broadcasted_iota(jnp.int32, (256, 64), 1)
    scores = jnp.where((col <= row) & (col < length), scores, -1e30)
    mixed = nn(softmax(scores).astype(BF16), values).astype(BF16)
    mixed = jnp.concatenate([mixed[64 * h : 64 * h + 64] for h in range(4)], axis=1)

    loads[3].wait()
    for k in (1, 3, 2, 0):
        slot = turn(zh, k, 4)
        column = pl.multiple_of((slot * 2 + 1 - c) * 512, 512)
        r.ra_send[slot] = nn(mixed, r.w_out[:, pl.ds(column, 512)]).astype(BF16)
        start(
            remote(
                r.ra_send.at[slot], r.ra_recv.at[slot], r.ra_s.at[k], r.ra_r.at[slot], d, mate
            )
        )
    for k in (1, 3, 2, 0):
        slot = turn(zh, k, 4)
        column = pl.multiple_of((slot * 2 + c) * 512, 512)
        r.r_own[slot] = nn(mixed, r.w_out[:, pl.ds(column, 512)])
    for k in (2, 1, 3):
        slot = turn(zh, k, 4)
        arrived(r.ra_recv.at[slot], r.ra_r.at[slot])
        r.rb_send[slot] = (r.r_own[slot] + r.ra_recv[slot].astype(F32)).astype(BF16)
        start(
            remote(
                r.rb_send.at[slot], r.rb_recv.at[zh], r.rb_s.at[k], r.rb_r.at[zh], d, slot * 2 + c
            )
        )

    all_arrived(r.c0, r.c0_r.at[0])
    facts = r.c0[...].reshape(32, 384)
    w_mean = jnp.sum(facts[:, 0:256], axis=0, keepdims=True) / 2048.0
    steps = facts[:, 256:257]
    step_means = facts[:, 257:258]
    column = (
        lax.broadcasted_iota(jnp.int32, (1, 64), 1) + lax.rem(d, 16) * 64
    ).astype(F32)
    angles = steps * jnp.exp(decay * column)
    quarter = jnp.full((32, 64), zl, jnp.int32).astype(F32) * (math.pi / 2.0)
    times = jnp.cos(angles - quarter)
    times_c = times - step_means
    w_c = w_in_t - w_mean
    part_a = tn(w_c.astype(BF16), wq_v).reshape(32, 8, 256)
    slabs_b = jnp.concatenate([part_a, part_m], axis=1).astype(BF16)
    first_core = jnp.full((256, 256), c, jnp.int32) == 0
    part_f = jnp.where(first_core, part_b, tn(w_c, w_c, HIGHEST))
    slabs_f = part_f.reshape(32, 8, 256)
    time_rows = jnp.concatenate(
        [
            nn(times_c, wq_v.astype(F32), HIGHEST),
            nn(times, vel_v.astype(F32), HIGHEST),
            nn(times_c, w_c, HIGHEST),
        ],
        axis=1,
    )
    for z in (0, 1):
        here = slice(16 * z, 16 * z + 16)
        r.zsb[:, z] = slabs_b[here]
        r.zsf[:, z, :, 0:256] = slabs_f[here]
        for i in range(8):
            part = time_rows[here, 128 * i : 128 * i + 128] if i < 6 else jnp.zeros((16, 128), F32)
            r.zsf[:, z, i, 256:384] = part
    r.zrb[xy] = r.zsb[xy]
    r.zrf[xy] = r.zsf[xy]

    def z_start(peer):
        dp = zl * 16 + peer
        remote(r.zsb.at[peer], r.zrb.at[xy], r.zb_s.at[0], r.zb_r.at[0], dp, t).start()
        remote(r.zsf.at[peer], r.zrf.at[xy], r.zf_s.at[0], r.zf_r.at[0], dp, t).start()

    over_plane(z_start)

    slot = zh
    arrived(r.ra_recv.at[slot], r.ra_r.at[slot])
    own = r.r_own[slot] + r.ra_recv[slot].astype(F32)
    for k in (1, 3, 2):
        slot = turn(zh, k, 4)
        arrived(r.rb_recv.at[slot], r.rb_r.at[slot])
        own = own + r.rb_recv[slot].astype(F32)
    r.cap_own[...] = (r.states[0].astype(F32) + own).astype(BF16)

    target = lax.div(zh, 2)
    mine = lax.rem(t, 4)
    inside = target == zl

    def cap_copy(k):
        return remote(
            r.cap_own,
            r.caps.at[mine, zl],
            r.cp_s.at[k],
            r.cp_r.at[mine, zl],
            target * 16 + xy,
            turn(zh, k, 4) * 2 + c,
        )

    for k in (2, 1, 3):
        start(cap_copy(k))

    @pl.when(inside)
    def _():
        r.caps[mine, zl] = r.cap_own[...]

    @pl.when(jnp.logical_not(inside))
    def _():
        cap_copy(0).start()

    plane_arrived(r.zrb, r.zb_r.at[0])
    plane_arrived(r.zrf, r.zf_r.at[0])
    plane_b = jnp.sum(r.zrb[...].astype(F32), axis=0)
    plane_f = jnp.sum(r.zrf[...], axis=0)
    r.pzb[zl] = plane_b.astype(BF16)
    r.pzf[zl] = plane_f
    start(remote(r.pzb.at[zl], r.pzb.at[zl], r.pb_s.at[0], r.pb_r.at[0], other, t))
    start(remote(r.pzf.at[zl], r.pzf.at[zl], r.pf_s.at[0], r.pf_r.at[0], other, t))

    for k in (0, 1, 2, 3):
        for j in (1, 2, 3):
            slot = turn(x, k, 4) * 4 + turn(y, j, 4)
            arrived(r.wkv.at[slot, 0], r.wkv_r.at[slot, 0])
            slot = turn(x, j, 4) * 4 + turn(y, k, 4)
            arrived(r.wkv.at[slot, 1], r.wkv_r.at[slot, 1])

    forwards = []
    for z in (0, 1):
        for near in (0, 1):
            chunk = near * 2 + c
            ref = r.caps.at[chunk, z]
            own_slot = inside & (chunk == mine) & (z == zl)

            @pl.when(jnp.logical_not(own_slot))
            def _(ref=ref, chunk=chunk, z=z):
                arrived(ref, r.cp_r.at[chunk, z])

            start(remote(ref, ref, r.cp_s.at[4 + 2 * z + near], r.cp_r.at[chunk, z], d, mate))

    arrived(r.pzb.at[1 - zl], r.pb_r.at[0])
    arrived(r.pzf.at[1 - zl], r.pf_r.at[0])
    r.agb[xy] = (plane_b + r.pzb[1 - zl].astype(F32)).astype(BF16)
    slabs = plane_f + r.pzf[1 - zl]
    r.agf[c, xy] = slabs[:, :, 0:256]
    late = jnp.full((8, 128), zl, jnp.int32) == 1
    rows = jnp.where(late, slabs[1, :, 256:384], slabs[0, :, 256:384])
    time_own = jnp.concatenate([rows[i : i + 1] for i in range(6)], axis=1)

    def a_start(peer):
        dp = zl * 16 + peer
        remote(r.agb.at[xy], r.agb.at[xy], r.ab_s.at[0], r.ab_r.at[0], dp, t).start()
        remote(r.agf.at[c, xy], r.agf.at[c, xy], r.af_s.at[0], r.af_r.at[0], dp, t).start()

    over_plane(a_start)

    def project_caption(chunk):
        rows = r.caps[chunk].reshape(128, 512)
        weights = r.wkv[pl.ds(chunk * 4, 4)].reshape(512, 512)
        return nn(rows, weights)

    both = project_caption(c) + project_caption(2 + c)
    for near in (0, 1):
        for z in (0, 1):
            chunk = near * 2 + 1 - c
            arrived(r.caps.at[chunk, z], r.cp_r.at[chunk, z])
        both = both + project_caption(near * 2 + 1 - c)
    second = jnp.full((64, 512), zl, jnp.int32) == 1
    r.kvx_send[...] = jnp.where(second, both[0:64], both[64:128]).astype(BF16)
    start(remote(r.kvx_send, r.kvx_recv, r.kvx_s.at[0], r.kvx_r.at[0], other, t))

    r.cap_k[x] = r.caps[x]
    for q in range(4):
        column = pl.multiple_of(y * 128, 128)
        r.cap_v[y, q] = r.caps[q, :, :, pl.ds(column, 128)]
    for k in (1, 3, 2):
        xx = turn(x, k, 4)
        start(
            remote(r.caps.at[xx], r.cap_k.at[x], r.ck_s.at[k], r.ck_r.at[x], plane(xx, y), t)
        )
        yy = turn(y, k, 4)
        column = pl.multiple_of(yy * 128, 128)
        start(
            remote(
                r.caps.at[:, :, :, pl.ds(column, 128)],
                r.cap_v.at[y],
                r.cv_s.at[k],
                r.cv_r.at[y],
                plane(x, yy),
                t,
            )
        )

    clean = r.clean[0].astype(F32)
    noise = r.noise[0].astype(F32)
    tau = jnp.full((1, 256), r.step_index[0], jnp.int32).astype(F32) / STEPS
    margin = jnp.zeros((PADDED - FRAMES, 256), F32)
    blend_f = jnp.concatenate([(1.0 - tau) * clean + tau * noise, margin], axis=0)
    r.blend[...] = blend_f.astype(BF16)
    blend = r.blend[...]
    blend_f = blend.astype(F32)
    plane_arrived(r.agb, r.ab_r.at[0])
    plane_arrived(r.agf.at[c], r.af_r.at[0])
    start(remote(r.agf.at[c], r.agf.at[c], r.ap_s.at[0], r.ap_r.at[0], d, mate))
    matrices = r.agb[...].astype(F32)

    def planes(slabs):
        return jnp.concatenate([slabs[:, z].reshape(128, 256) for z in (0, 1)], axis=0)

    mat_a = planes(matrices[:, :, 0:8]).astype(BF16)
    mat_m = planes(matrices[:, :, 8:16]).astype(BF16)
    arrived(r.agf.at[1 - c], r.ap_r.at[0])
    mat_b = planes(r.agf[0])
    mat_s = planes(r.agf[1])
    r.hid_v[...] = nn(blend_f, mat_b, HIGHEST) + time_own[:, 256:512]
    spread = (nn(blend_f, mat_s, HIGHEST) + 2.0 * time_own[:, 512:768]) * blend_f
    variance = (jnp.sum(spread, axis=1, keepdims=True) + time_square) / 2048.0
    rstd = lax.rsqrt(jnp.maximum(variance, 0.0) + EPSILON)
    r.query[...] = ((nn(blend, mat_a) + time_own[:, 0:256]) * rstd).astype(BF16)

    kv_own = jnp.where(second, both[64:128], both[0:64])
    arrived(r.kvx_recv, r.kvx_r.at[0])
    kv = (kv_own + r.kvx_recv[...].astype(F32)).astype(BF16)

    query = r.query[...]
    allowed = lax.broadcasted_iota(jnp.int32, (PADDED, 64), 1) < length
    probs = []
    attended = []
    for h in (0, 1):
        span = slice(128 * h, 128 * h + 128)
        scores = nt(query[:, span], kv[:, span]) * SCALE
        prob = softmax(jnp.where(allowed, scores, -1e30))
        probs.append(prob)
        attended.append(nn(prob.astype(BF16), kv[:, 256 + 128 * h : 384 + 128 * h]).astype(BF16))
    attended = jnp.concatenate(attended, axis=1)
    branch = nn(attended, mat_m).reshape(8, 48, 256)

    first_half = jnp.full((48, 256), c, jnp.int32) == 0
    for q in range(4):
        r.va_send[q] = jnp.where(first_half, branch[2 * q + 1], branch[2 * q]).astype(BF16)
        r.v_own[q] = jnp.where(first_half, branch[2 * q], branch[2 * q + 1])
    start(remote(r.va_send, r.va_recv, r.va_s.at[0], r.va_r.at[0], d, mate))
    r.att_t[...] = attended.T
    for h in (0, 1):
        r.prob_t[h] = probs[h].astype(BF16).T
    arrived(r.va_recv, r.va_r.at[0])
    for k in (2, 1, 3):
        slot = turn(zh, k, 4)
        r.vb_send[slot] = (r.v_own[slot] + r.va_recv[slot].astype(F32)).astype(BF16)
        start(
            remote(
                r.vb_send.at[slot], r.vb_recv.at[zh], r.vb_s.at[k], r.vb_r.at[zh], d, slot * 2 + c
            )
        )
    r.blend_t[...] = blend.T
    for k in (1, 3, 2):
        slot = turn(x, k, 4)
        arrived(r.cap_k.at[slot], r.ck_r.at[slot])
    r.cap_kt[...] = r.cap_k[...].reshape(512, 512).T
    own = r.v_own[zh] + r.va_recv[zh].astype(F32)
    for k in (1, 3, 2):
        slot = turn(zh, k, 4)
        arrived(r.vb_recv.at[slot], r.vb_r.at[slot])
        own = own + r.vb_recv[slot].astype(F32)
    r.vg[t] = own.astype(BF16)
    for k in (2, 1, 3):
        start(remote(r.vg.at[t], r.vg.at[t], r.vg_s.at[k], r.vg_r.at[t], d, turn(zh, k, 4) * 2 + c))
    start(remote(r.vg.at[t], r.vg.at[t], r.vg_s.at[0], r.vg_r.at[t], d, mate))
    for k in (1, 3, 2):
        slot = turn(y, k, 4)
        arrived(r.cap_v.at[slot], r.cv_r.at[slot])
    for q in range(4):
        r.cap_vt[q] = r.cap_v[:, q].reshape(512, 128).T
    for k in (1, 3, 2):
        slot = turn(zh, k, 4) * 2 + c
        arrived(r.vg.at[slot], r.vg_r.at[slot])
        start(remote(r.vg.at[slot], r.vg.at[slot], r.vg_s.at[4 + k], r.vg_r.at[slot], d, mate))
    arrived(r.vg.at[mate], r.vg_r.at[mate])
    for k in (1, 3, 2):
        slot = turn(zh, k, 4) * 2 + 1 - c
        arrived(r.vg.at[slot], r.vg_r.at[slot])

    predicted = r.hid_v[...] + r.vg[...].astype(F32).reshape(PADDED, 256)
    residual = predicted - jnp.concatenate([noise - clean, margin], axis=0)
    frames = jnp.full((PADDED, 1), r.motion_len[0], jnp.int32)
    live = lax.broadcasted_iota(jnp.int32, (PADDED, 1), 0) < frames
    row_weight = jnp.where(live, 1.0 / frames.astype(F32), 0.0)
    weighted = residual * row_weight
    loss_part = total(residual * weighted)
    d_vel = (2.0 * weighted).astype(BF16)
    d_att = nt(d_vel, mat_m).astype(BF16)

    heads = [d_att[:, 128 * h : 128 * h + 128] for h in (0, 1)]
    d_values = [nn(r.prob_t[h], heads[h]) for h in (0, 1)]
    r.dkx[1, zl] = jnp.concatenate(d_values, axis=1).astype(BF16)

    def dx_start(i):
        ref = r.dkx.at[i, zl]
        start(remote(ref, ref, r.dx_s.at[i], r.dx_r.at[i], other, t))

    dx_start(1)
    d_scores = []
    for h in (0, 1):
        d_prob = nt(heads[h], kv[:, 256 + 128 * h : 384 + 128 * h])
        delta = jnp.sum(probs[h] * d_prob, axis=1, keepdims=True)
        d_scores.append((probs[h] * (d_prob - delta) * SCALE).astype(BF16))
    d_keys = [tn(d_scores[h], query[:, 128 * h : 128 * h + 128]) for h in (0, 1)]
    r.dkx[0, zl] = jnp.concatenate(d_keys, axis=1).astype(BF16)
    dx_start(0)
    d_queries = [nn(d_scores[h], kv[:, 128 * h : 128 * h + 128]) for h in (0, 1)]
    d_query = jnp.concatenate(d_queries, axis=1).astype(BF16).astype(F32) * rstd
    mat_h = nn(r.blend_t[...], d_query.astype(BF16)).reshape(32, 8, 256)
    mat_g = nn(r.att_t[...], d_vel).reshape(32, 8, 256)
    r.hs[:, :, 0:256] = jnp.concatenate([mat_h, mat_g], axis=1).astype(BF16)
    frame_sum = jnp.sum(d_query, axis=0, keepdims=True)
    loss_high = loss_part.astype(BF16).astype(F32)
    which = lax.broadcasted_iota(jnp.int32, (16, 128), 0)
    extra = jnp.where(which == 2, loss_high, loss_part - loss_high)
    extra = jnp.where(which == 1, frame_sum[:, 128:256], extra)
    extra = jnp.where(which == 0, frame_sum[:, 0:128], extra)
    r.hs[:, :, 256:384] = jnp.broadcast_to(extra.astype(BF16)[None], (32, 16, 128))
    r.hr[d] = r.hs[d]

    def h_copy(k, peer):
        return remote(r.hs.at[peer], r.hr.at[d], r.hs_s.at[0], r.hs_r.at[0], peer, t)

    over_dp(lambda k, peer: h_copy(k, peer).start())

    arrived(r.dkx.at[1, 1 - zl], r.dx_r.at[1])
    r.dv[y] = r.dkx[1]
    for k in (1, 3, 2):
        start(
            remote(
                r.dv.at[y], r.dv.at[y], r.dv_s.at[k], r.dv_r.at[y], plane(x, turn(y, k, 4)), t
            )
        )
    arrived(r.dkx.at[0, 1 - zl], r.dx_r.at[0])
    r.dk[x] = r.dkx[0]
    for k in (1, 3, 2):
        start(
            remote(
                r.dk.at[x], r.dk.at[x], r.dk_s.at[k], r.dk_r.at[x], plane(turn(x, k, 4), y), t
            )
        )

    all_arrived(r.hr, r.hs_r.at[0])
    arrivals = r.hr[...].astype(F32)
    r.hg[d] = jnp.sum(arrivals[:, :, 0:256], axis=0).astype(BF16)

    def g_copy(k, peer):
        return remote(r.hg.at[d], r.hg.at[d], r.hg_s.at[0], r.hg_r.at[0], peer, t)

    over_dp(lambda k, peer: g_copy(k, peer).start())

    for k in (1, 3, 2):
        slot = turn(y, k, 4)
        arrived(r.dv.at[slot], r.dv_r.at[slot])
    all_v = r.dv[...].reshape(512, 256)
    for q in range(4):
        r.gv_send[q] = nn(r.cap_vt[q], all_v).astype(BF16)
    for k in (1, 3, 2):
        xx = turn(x, k, 4)
        start(
            remote(
                r.gv_send.at[xx], r.gv_recv.at[x], r.gv_s.at[k], r.gv_r.at[x], plane(xx, y), t
            )
        )
    r.gv_recv[x] = r.gv_send[x]
    for k in (1, 3, 2):
        slot = turn(x, k, 4)
        arrived(r.dk.at[slot], r.dk_r.at[slot])
    all_k = r.dk[...].reshape(512, 256)
    grad_k = nn(r.cap_kt[...], all_k).reshape(4, 128, 256)
    for q in range(4):
        r.gk_send[q] = grad_k[q].astype(BF16)
    for k in (1, 3, 2):
        yy = turn(y, k, 4)
        start(
            remote(
                r.gk_send.at[yy], r.gk_recv.at[y], r.gk_s.at[k], r.gk_r.at[y], plane(x, yy), t
            )
        )
    r.gk_recv[y] = r.gk_send[y]

    sums_p = jnp.concatenate([arrivals[:, 0, 256:384], arrivals[:, 1, 256:384]], axis=1)
    losses = arrivals[:, 2, 256:384] + arrivals[:, 3, 256:384]
    r.loss_out[...] = jnp.sum(losses, axis=0, keepdims=True) / 8192.0
    all_arrived(r.hg, r.hg_r.at[0])
    grads = r.hg[...].astype(F32)
    sum_h = grads[:, 0:8].reshape(256, 256)
    sum_g = grads[:, 8:16].reshape(256, 256).astype(BF16)
    r.packed_out[0:64] = nn(w_c, sum_h, HIGHEST) + tn(times_c, sums_p, HIGHEST)
    r.packed_out[320:384] = nt(r.vel[...], sum_g)
    for k in (1, 3, 2):
        slot = turn(y, k, 4)
        arrived(r.gk_recv.at[slot], r.gk_r.at[slot])
        slot = turn(x, k, 4)
        arrived(r.gv_recv.at[slot], r.gv_r.at[slot])
    r.packed_out[64:192] = jnp.sum(r.gk_recv[...].astype(F32), axis=0)
    r.packed_out[192:320] = jnp.sum(r.gv_recv[...].astype(F32), axis=0)

    for copy in pending:
        copy.wait_send()

    @pl.when(jnp.logical_not(inside))
    def _():
        cap_copy(0).wait_send()

    all_left(r.c0, r.c0_s.at[0])
    plane_left(r.zrb, r.zb_s.at[0])
    plane_left(r.zrf, r.zf_s.at[0])
    plane_left(r.agb, r.ab_s.at[0])
    plane_left(r.agf.at[c], r.af_s.at[0])
    all_left(r.hr, r.hs_s.at[0])
    all_left(r.hg, r.hg_s.at[0])


def unpack(loss, packed, loss_out, gq, gk, gv, go):
    loss_out[...] = loss[...]
    gq[...] = packed[0:64]
    gk[...] = packed[64:192]
    gv[...] = packed[192:320]
    go[...] = packed[320:384]


def rope_tables():
    inverse = 1000000.0 ** (-(np.arange(64, dtype=np.float32) * 2.0 / 128))
    angles = np.arange(64, dtype=np.float32)[:, None] * inverse[None, :].astype(np.float32)
    angles = np.concatenate([angles, angles], axis=1).astype(np.float32)
    sign = np.where(np.arange(128) < 64, -1.0, 1.0)[None, :]
    return np.cos(angles).astype(np.float32), (np.sin(angles) * sign).astype(np.float32)


def local(
    encoder_input_states,
    caption_lengths,
    encoder_input_gain,
    query_head_gain,
    key_head_gain,
    encoder_query_weight,
    encoder_key_weight,
    encoder_value_weight,
    encoder_output_weight,
    clean_motion,
    noise,
    timestep_index,
    motion_lengths,
    input_weight,
    velocity_weight,
    cross_query_weight,
    cross_key_weight,
    cross_value_weight,
    cross_output_weight,
):
    vmem = pl.BlockSpec(memory_space=pltpu.VMEM)
    hbm = pl.BlockSpec(memory_space=pl.ANY)
    smem = pl.BlockSpec(memory_space=pltpu.SMEM)
    spec = {name: vmem for name in INPUTS}
    for name in ("cap_len", "step_index", "motion_len"):
        spec[name] = smem
    for name in ("eq", "ek", "ev", "eo"):
        spec[name] = hbm
    cosine, sine = rope_tables()
    packed = pl.pallas_call(
        kernel,
        out_shape=[
            jax.ShapeDtypeStruct((1, 128), F32),
            jax.ShapeDtypeStruct((384, 256), F32),
        ],
        in_specs=[spec[name] for name in INPUTS],
        out_specs=[vmem] * 2,
        scratch_shapes=[pltpu.VMEM(shape, kind) for shape, kind in BUFFERS.values()]
        + [
            pltpu.SemaphoreType.DMA(shape if isinstance(shape, tuple) else (shape,))
            for shape in SEMAPHORES.values()
        ],
        compiler_params=pltpu.CompilerParams(
            collective_id=0, has_side_effects=True, vmem_limit_bytes=56 * 2**20
        ),
        name="motion_block",
    )(
        encoder_input_states,
        caption_lengths,
        timestep_index,
        motion_lengths,
        encoder_input_gain.reshape(8, 1, 512),
        query_head_gain.reshape(1, 128),
        key_head_gain.reshape(1, 128),
        jnp.asarray(cosine),
        jnp.asarray(sine),
        encoder_query_weight,
        encoder_key_weight,
        encoder_value_weight,
        encoder_output_weight,
        clean_motion,
        noise,
        input_weight.T,
        velocity_weight,
        cross_query_weight,
        cross_key_weight,
        cross_value_weight,
        cross_output_weight.T,
    )
    loss, gq, gk, gv, go = pl.pallas_call(
        unpack,
        out_shape=[
            jax.ShapeDtypeStruct((1, 128), F32),
            jax.ShapeDtypeStruct((64, 256), F32),
            jax.ShapeDtypeStruct((128, 256), F32),
            jax.ShapeDtypeStruct((128, 256), F32),
            jax.ShapeDtypeStruct((64, 256), F32),
        ],
        in_specs=[vmem] * 2,
        out_specs=[vmem] * 5,
        name="unpack",
    )(*packed)
    return (loss[0, 0], gq, gk, gv, go.T)


def solution(mesh):
    placed = (
        P("dp", None, "tensor"),
        P("dp"),
        P(),
        P(),
        P(),
        P(None, "tensor"),
        P(None, "tensor"),
        P(None, "tensor"),
        P("tensor", None),
        P("dp", None, None),
        P("dp", None, None),
        P("dp"),
        P("dp"),
        P(None, "dp"),
        P("dp", None),
        P("dp", "tensor"),
        P("dp", "tensor"),
        P("dp", "tensor"),
        P("tensor", "dp"),
    )
    return jax.shard_map(
        local,
        mesh=mesh,
        in_specs=placed,
        out_specs=(P(), P("dp", "tensor"), P("dp", "tensor"), P("dp", "tensor"), P("tensor", "dp")),
        check_vma=False,
    )
```

```python
import math
import types

import jax
import jax.numpy as jnp
import numpy as np
from jax import lax
from jax.experimental import pallas as pl
from jax.experimental.pallas import tpu as pltpu
from jax.sharding import PartitionSpec as P

F32 = jnp.float32
BF16 = jnp.bfloat16
MESH = pl.DeviceIdType.MESH
HIGHEST = lax.Precision.HIGHEST
EPSILON = 1e-06
STEPS = 1000
FRAMES = 360
PADDED = 384
SCALE = 1.0 / math.sqrt(128)

INPUTS = [
    "states", "cap_len", "step_index", "motion_len", "gain", "q_gain", "k_gain", "cosine", "sine",
    "eq", "ek", "ev", "eo", "clean", "noise", "w_in", "vel", "wq", "wk", "wv", "wo",
]
OUTPUTS = ["loss", "packed"]

BUFFERS = dict(
    w_qkv=((4096, 768), BF16),
    w_out=((512, 4096), BF16),
    c0=((32, 1, 384), F32),
    gx=((8, 64, 512), BF16),
    wkv=((16, 2, 64, 512), BF16),
    zsb=((16, 2, 16, 256), BF16),
    zrb=((16, 2, 16, 256), BF16),
    zsf=((16, 2, 8, 384), F32),
    zrf=((16, 2, 8, 384), F32),
    pzb=((2, 2, 16, 256), BF16),
    pzf=((2, 2, 8, 384), F32),
    agb=((16, 2, 16, 256), BF16),
    agf=((2, 16, 2, 8, 256), F32),
    ra_send=((4, 64, 512), BF16),
    ra_recv=((4, 64, 512), BF16),
    rb_send=((4, 64, 512), BF16),
    rb_recv=((4, 64, 512), BF16),
    r_own=((4, 64, 512), F32),
    cap_own=((64, 512), BF16),
    caps=((4, 2, 64, 512), BF16),
    kvx_send=((64, 512), BF16),
    kvx_recv=((64, 512), BF16),
    blend=((PADDED, 256), BF16),
    query=((PADDED, 256), BF16),
    hid_v=((PADDED, 256), F32),
    va_send=((4, 48, 256), BF16),
    va_recv=((4, 48, 256), BF16),
    v_own=((4, 48, 256), F32),
    vb_send=((4, 48, 256), BF16),
    vb_recv=((4, 48, 256), BF16),
    vg=((8, 48, 256), BF16),
    dkx=((2, 2, 64, 256), BF16),
    dk=((4, 2, 64, 256), BF16),
    dv=((4, 2, 64, 256), BF16),
    cap_k=((4, 2, 64, 512), BF16),
    cap_v=((4, 4, 2, 64, 128), BF16),
    cap_kt=((512, 512), BF16),
    cap_vt=((4, 128, 512), BF16),
    blend_t=((256, PADDED), BF16),
    att_t=((256, PADDED), BF16),
    prob_t=((2, 64, PADDED), BF16),
    gk_send=((4, 128, 256), BF16),
    gk_recv=((4, 128, 256), BF16),
    gv_send=((4, 128, 256), BF16),
    gv_recv=((4, 128, 256), BF16),
    hs=((32, 16, 384), BF16),
    hr=((32, 16, 384), BF16),
    hg=((32, 16, 256), BF16),
)

SEMAPHORES = dict(
    load=4,
    c0_s=1, c0_r=1,
    gx_s=12, gx_r=(8, 2),
    wkv_s=32, wkv_r=(16, 2),
    zb_s=1, zb_r=1, zf_s=1, zf_r=1, pb_s=1, pb_r=1, pf_s=1, pf_r=1,
    ab_s=1, ab_r=1, af_s=1, af_r=1, ap_s=1, ap_r=1,
    ra_s=4, ra_r=4, rb_s=4, rb_r=4,
    cp_s=8, cp_r=(4, 2),
    kvx_s=1, kvx_r=1,
    va_s=1, va_r=1, vb_s=4, vb_r=4, vg_s=8, vg_r=8,
    dx_s=2, dx_r=2, dk_s=4, dk_r=4, dv_s=4, dv_r=4,
    ck_s=4, ck_r=4, cv_s=4, cv_r=4,
    gk_s=4, gk_r=4, gv_s=4, gv_r=4,
    hs_s=1, hs_r=1, hg_s=1, hg_r=1,
)


def dot(a, b, left, right, precision=None):
    return lax.dot_general(
        a, b, (((left,), (right,)), ((), ())), precision=precision, preferred_element_type=F32
    )


def nn(a, b, precision=None):
    return dot(a, b, 1, 0, precision)


def nt(a, b, precision=None):
    return dot(a, b, 1, 1, precision)


def tn(a, b, precision=None):
    return dot(a, b, 0, 0, precision)


def softmax(scores):
    top = jnp.max(scores, axis=-1, keepdims=True)
    weights = jnp.exp(scores - top)
    return weights / jnp.sum(weights, axis=-1, keepdims=True)


def remote(source, target, send, receive, dp, tensor):
    return pltpu.make_async_remote_copy(
        src_ref=source,
        dst_ref=target,
        send_sem=send,
        recv_sem=receive,
        device_id=(dp, tensor),
        device_id_type=MESH,
    )


def kernel(*refs):
    names = INPUTS + [n + "_out" for n in OUTPUTS] + list(BUFFERS) + list(SEMAPHORES)
    r = types.SimpleNamespace(**dict(zip(names, refs, strict=True)))

    d = lax.axis_index("dp")
    t = lax.axis_index("tensor")
    zl = lax.div(d, 16)
    xy = lax.rem(d, 16)
    x = lax.div(xy, 4)
    y = lax.rem(xy, 4)
    zh = lax.div(t, 2)
    c = lax.rem(t, 2)
    mate = t + 1 - 2 * c
    other = (1 - zl) * 16 + xy
    pending = []

    def start(copy):
        copy.start()
        pending.append(copy)

    def turn(base, k, size):
        return lax.rem(base + k, size)

    def plane(xx, yy):
        return zl * 16 + xx * 4 + yy

    def arrived(slot, semaphore):
        remote(slot, slot, semaphore, semaphore, other, t).wait_recv()

    def all_arrived(buffer, semaphore):
        most = buffer.at[pl.ds(0, 31)]
        remote(most, most, semaphore, semaphore, other, t).wait_recv()

    def all_left(buffer, semaphore):
        most = buffer.at[pl.ds(0, 31)]
        remote(most, most, semaphore, semaphore, other, t).wait_send()

    def plane_arrived(buffer, semaphore):
        most = buffer.at[pl.ds(0, 15)]
        remote(most, most, semaphore, semaphore, other, t).wait_recv()

    def plane_left(buffer, semaphore):
        most = buffer.at[pl.ds(0, 15)]
        remote(most, most, semaphore, semaphore, other, t).wait_send()

    def over_plane(body):
        def step(k, carry):
            body(turn(xy, k, 16))
            return carry

        lax.fori_loop(1, 16, step, 0)

    def over_dp(body):
        def step(k, carry):
            body(k, turn(d, k, 32))
            return carry

        lax.fori_loop(1, 32, step, 0)

    loads = [
        pltpu.make_async_copy(r.eq, r.w_qkv.at[:, pl.ds(0, 512)], r.load.at[0]),
        pltpu.make_async_copy(r.ek, r.w_qkv.at[:, pl.ds(512, 128)], r.load.at[1]),
        pltpu.make_async_copy(r.ev, r.w_qkv.at[:, pl.ds(640, 128)], r.load.at[2]),
        pltpu.make_async_copy(r.eo, r.w_out, r.load.at[3]),
    ]
    for load in loads:
        load.start()

    barrier = pltpu.get_barrier_semaphore()

    def signal(dp, tensor):
        pl.semaphore_signal(barrier, inc=1, device_id=(dp, tensor), device_id_type=MESH)

    over_dp(lambda k, peer: signal(peer, t))
    signal(d, mate)
    for k in (1, 2, 3):
        signal(d, turn(zh, k, 4) * 2 + c)
        signal(other, turn(zh, k, 4) * 2 + c)

    r.gx[t] = r.states[0]
    wk_v = r.wk[...]
    wv_v = r.wv[...]
    for half in (0, 1):
        r.wkv[xy, half, :, 0:256] = wk_v[64 * half : 64 * half + 64]
        r.wkv[xy, half, :, 256:512] = wv_v[64 * half : 64 * half + 64]
    w_in_v = r.w_in[...]
    w_in_t = w_in_v.astype(F32)
    decay = -math.log(10000.0) / 1024.0
    step_f = jnp.full((8, 128), r.step_index[0], jnp.int32).astype(F32)
    place = (
        lax.broadcasted_iota(jnp.int32, (8, 128), 0) * 128
        + lax.broadcasted_iota(jnp.int32, (8, 128), 1)
    ).astype(F32)
    all_angles = step_f * jnp.exp(decay * place)
    all_cos = jnp.cos(all_angles)
    all_sin = jnp.sin(all_angles)

    def total(tile):
        return jnp.sum(jnp.sum(tile, axis=1, keepdims=True), axis=0, keepdims=True)

    own_mean = total(all_cos + all_sin) / 2048.0
    time_square = total((all_cos - own_mean) ** 2 + (all_sin - own_mean) ** 2)
    lane = lax.broadcasted_iota(jnp.int32, (1, 128), 1)
    r.c0[d, :, 0:256] = jnp.sum(w_in_t, axis=0, keepdims=True)
    r.c0[d, :, 256:384] = jnp.where(lane == 0, step_f[0:1], own_mean)

    vel_v = r.vel[...]
    wq_v = r.wq[...]
    part_m = tn(r.wo[...], vel_v).reshape(32, 8, 256)
    part_b = tn(w_in_v, vel_v)

    pl.semaphore_wait(barrier, 38)

    def gx_half(slot, half):
        return r.gx.at[slot, pl.ds(32 * half, 32)]

    def gx_send(slot, half, step, index):
        ref = gx_half(slot, half)
        peer = turn(zh, step, 4) * 2 + c
        start(remote(ref, ref, r.gx_s.at[index], r.gx_r.at[slot, half], d, peer))

    def gx_arrived(slot, half):
        arrived(gx_half(slot, half), r.gx_r.at[slot, half])

    gx_send(t, 0, 1, 1)
    gx_send(t, 1, 3, 2)
    gx_send(t, 1, 1, 3)
    gx_send(t, 0, 3, 8)
    start(remote(r.gx.at[t], r.gx.at[t], r.gx_s.at[0], r.gx_r.at[t, 0], d, mate))

    def wkv_send(slot, half, dp, index):
        ref = r.wkv.at[slot, half]
        start(remote(ref, ref, r.wkv_s.at[index], r.wkv_r.at[slot, half], dp, t))

    for k in (1, 3, 2):
        wkv_send(xy, 0, plane(turn(x, k, 4), y), k - 1)
        wkv_send(xy, 1, plane(x, turn(y, k, 4)), 2 + k)

    def c0_copy(k, peer):
        return remote(r.c0.at[d], r.c0.at[d], r.c0_s.at[0], r.c0_r.at[0], peer, t)

    over_dp(lambda k, peer: c0_copy(k, peer).start())

    before = turn(zh, 3, 4) * 2 + c
    after = turn(zh, 1, 4) * 2 + c
    gx_arrived(before, 0)
    gx_send(before, 0, 1, 9)
    gx_arrived(after, 1)
    gx_send(after, 1, 3, 10)

    def wkv_second(first, k_list):
        for k in k_list:
            if k:
                slot = turn(x, k, 4) * 4 + y
                arrived(r.wkv.at[slot, 0], r.wkv_r.at[slot, 0])
                slot = x * 4 + turn(y, k, 4)
                arrived(r.wkv.at[slot, 1], r.wkv_r.at[slot, 1])
            for j in (1, 3, 2):
                wkv_send(turn(x, k, 4) * 4 + y, 0, plane(x, turn(y, j, 4)), first + 6 * k + j - 1)
                wkv_send(
                    x * 4 + turn(y, k, 4), 1, plane(turn(x, j, 4), y), first + 6 * k + 2 + j
                )

    wkv_second(6, (0, 1, 3, 2))

    for load in loads[:3]:
        load.wait()

    def project(slot, sums, square):
        chunk = r.gx[slot].astype(F32)
        square = square + jnp.sum(chunk * chunk, axis=1, keepdims=True)
        row = pl.multiple_of(slot * 512, 512)
        scaled = (chunk * r.gain[slot]).astype(BF16)
        return sums + nn(scaled, r.w_qkv[pl.ds(row, 512), :]), square

    sums, square = project(t, jnp.zeros((64, 768), F32), jnp.zeros((64, 1), F32))

    for k, halves in ((1, (0,)), (3, (1,)), (2, (0, 1))):
        slot = turn(zh, k, 4) * 2 + c
        for half in halves:
            gx_arrived(slot, half)
        ref = r.gx.at[slot]
        start(remote(ref, ref, r.gx_s.at[4 + k], r.gx_r.at[slot, 0], d, mate))
        sums, square = project(slot, sums, square)

    arrived(r.gx.at[mate], r.gx_r.at[mate, 0])
    sums, square = project(mate, sums, square)
    for k in (1, 3, 2):
        slot = turn(zh, k, 4) * 2 + (1 - c)
        arrived(r.gx.at[slot], r.gx_r.at[slot, 0])
        sums, square = project(slot, sums, square)

    length = r.cap_len[0]
    rms = lax.rsqrt(square / 4096.0 + EPSILON)
    sums = sums * rms
    cosine = r.cosine[...]
    sine = r.sine[...]

    def turned(vectors, scaling):
        mean = jnp.mean(vectors * vectors, axis=1, keepdims=True)
        vectors = vectors * lax.rsqrt(mean + EPSILON) * scaling
        return (vectors * cosine + pltpu.roll(vectors, 64, 1) * sine).astype(BF16)

    q_gain = r.q_gain[...]
    queries = jnp.concatenate(
        [turned(sums[:, 128 * h : 128 * h + 128], q_gain) for h in range(4)], axis=0
    )
    keys = turned(sums[:, 512:640], r.k_gain[...])
    values = sums[:, 640:768].astype(BF16)
    scores = nt(queries, keys) * SCALE
    row = lax.rem(lax.broadcasted_iota(jnp.int32, (256, 64), 0), 64)
    col = lax.broadcasted_iota(jnp.int32, (256, 64), 1)
    scores = jnp.where((col <= row) & (col < length), scores, -1e30)
    mixed = nn(softmax(scores).astype(BF16), values).astype(BF16)
    mixed = jnp.concatenate([mixed[64 * h : 64 * h + 64] for h in range(4)], axis=1)

    loads[3].wait()
    for k in (1, 3, 2, 0):
        slot = turn(zh, k, 4)
        column = pl.multiple_of((slot * 2 + 1 - c) * 512, 512)
        r.ra_send[slot] = nn(mixed, r.w_out[:, pl.ds(column, 512)]).astype(BF16)
        start(
            remote(
                r.ra_send.at[slot], r.ra_recv.at[slot], r.ra_s.at[k], r.ra_r.at[slot], d, mate
            )
        )
    for k in (1, 3, 2, 0):
        slot = turn(zh, k, 4)
        column = pl.multiple_of((slot * 2 + c) * 512, 512)
        r.r_own[slot] = nn(mixed, r.w_out[:, pl.ds(column, 512)])
    for k in (2, 1, 3):
        slot = turn(zh, k, 4)
        arrived(r.ra_recv.at[slot], r.ra_r.at[slot])
        r.rb_send[slot] = (r.r_own[slot] + r.ra_recv[slot].astype(F32)).astype(BF16)
        start(
            remote(
                r.rb_send.at[slot], r.rb_recv.at[zh], r.rb_s.at[k], r.rb_r.at[zh], d, slot * 2 + c
            )
        )

    all_arrived(r.c0, r.c0_r.at[0])
    facts = r.c0[...].reshape(32, 384)
    w_mean = jnp.sum(facts[:, 0:256], axis=0, keepdims=True) / 2048.0
    steps = facts[:, 256:257]
    step_means = facts[:, 257:258]
    column = (
        lax.broadcasted_iota(jnp.int32, (1, 64), 1) + lax.rem(d, 16) * 64
    ).astype(F32)
    angles = steps * jnp.exp(decay * column)
    quarter = jnp.full((32, 64), zl, jnp.int32).astype(F32) * (math.pi / 2.0)
    times = jnp.cos(angles - quarter)
    times_c = times - step_means
    w_c = w_in_t - w_mean
    part_a = tn(w_c.astype(BF16), wq_v).reshape(32, 8, 256)
    slabs_b = jnp.concatenate([part_a, part_m], axis=1).astype(BF16)
    first_core = jnp.full((256, 256), c, jnp.int32) == 0
    part_f = jnp.where(first_core, part_b, tn(w_c, w_c, HIGHEST))
    slabs_f = part_f.reshape(32, 8, 256)
    time_rows = jnp.concatenate(
        [
            nn(times_c, wq_v.astype(F32), HIGHEST),
            nn(times, vel_v.astype(F32), HIGHEST),
            nn(times_c, w_c, HIGHEST),
        ],
        axis=1,
    )
    for z in (0, 1):
        here = slice(16 * z, 16 * z + 16)
        r.zsb[:, z] = slabs_b[here]
        r.zsf[:, z, :, 0:256] = slabs_f[here]
        for i in range(8):
            part = time_rows[here, 128 * i : 128 * i + 128] if i < 6 else jnp.zeros((16, 128), F32)
            r.zsf[:, z, i, 256:384] = part
    r.zrb[xy] = r.zsb[xy]
    r.zrf[xy] = r.zsf[xy]

    def z_start(peer):
        dp = zl * 16 + peer
        remote(r.zsb.at[peer], r.zrb.at[xy], r.zb_s.at[0], r.zb_r.at[0], dp, t).start()
        remote(r.zsf.at[peer], r.zrf.at[xy], r.zf_s.at[0], r.zf_r.at[0], dp, t).start()

    over_plane(z_start)

    slot = zh
    arrived(r.ra_recv.at[slot], r.ra_r.at[slot])
    own = r.r_own[slot] + r.ra_recv[slot].astype(F32)
    for k in (1, 3, 2):
        slot = turn(zh, k, 4)
        arrived(r.rb_recv.at[slot], r.rb_r.at[slot])
        own = own + r.rb_recv[slot].astype(F32)
    r.cap_own[...] = (r.states[0].astype(F32) + own).astype(BF16)

    target = lax.div(zh, 2)
    mine = lax.rem(t, 4)
    inside = target == zl

    def cap_copy(k):
        return remote(
            r.cap_own,
            r.caps.at[mine, zl],
            r.cp_s.at[k],
            r.cp_r.at[mine, zl],
            target * 16 + xy,
            turn(zh, k, 4) * 2 + c,
        )

    for k in (2, 1, 3):
        start(cap_copy(k))

    @pl.when(inside)
    def _():
        r.caps[mine, zl] = r.cap_own[...]

    @pl.when(jnp.logical_not(inside))
    def _():
        cap_copy(0).start()

    plane_arrived(r.zrb, r.zb_r.at[0])
    plane_arrived(r.zrf, r.zf_r.at[0])
    plane_b = jnp.sum(r.zrb[...].astype(F32), axis=0)
    plane_f = jnp.sum(r.zrf[...], axis=0)
    r.pzb[zl] = plane_b.astype(BF16)
    r.pzf[zl] = plane_f
    start(remote(r.pzb.at[zl], r.pzb.at[zl], r.pb_s.at[0], r.pb_r.at[0], other, t))
    start(remote(r.pzf.at[zl], r.pzf.at[zl], r.pf_s.at[0], r.pf_r.at[0], other, t))

    for k in (0, 1, 2, 3):
        for j in (1, 2, 3):
            slot = turn(x, k, 4) * 4 + turn(y, j, 4)
            arrived(r.wkv.at[slot, 0], r.wkv_r.at[slot, 0])
            slot = turn(x, j, 4) * 4 + turn(y, k, 4)
            arrived(r.wkv.at[slot, 1], r.wkv_r.at[slot, 1])

    forwards = []
    for z in (0, 1):
        for near in (0, 1):
            chunk = near * 2 + c
            ref = r.caps.at[chunk, z]
            own_slot = inside & (chunk == mine) & (z == zl)

            @pl.when(jnp.logical_not(own_slot))
            def _(ref=ref, chunk=chunk, z=z):
                arrived(ref, r.cp_r.at[chunk, z])

            start(remote(ref, ref, r.cp_s.at[4 + 2 * z + near], r.cp_r.at[chunk, z], d, mate))

    arrived(r.pzb.at[1 - zl], r.pb_r.at[0])
    arrived(r.pzf.at[1 - zl], r.pf_r.at[0])
    r.agb[xy] = (plane_b + r.pzb[1 - zl].astype(F32)).astype(BF16)
    slabs = plane_f + r.pzf[1 - zl]
    r.agf[c, xy] = slabs[:, :, 0:256]
    late = jnp.full((8, 128), zl, jnp.int32) == 1
    rows = jnp.where(late, slabs[1, :, 256:384], slabs[0, :, 256:384])
    time_own = jnp.concatenate([rows[i : i + 1] for i in range(6)], axis=1)

    def a_start(peer):
        dp = zl * 16 + peer
        remote(r.agb.at[xy], r.agb.at[xy], r.ab_s.at[0], r.ab_r.at[0], dp, t).start()
        remote(r.agf.at[c, xy], r.agf.at[c, xy], r.af_s.at[0], r.af_r.at[0], dp, t).start()

    over_plane(a_start)

    def project_caption(chunk):
        rows = r.caps[chunk].reshape(128, 512)
        weights = r.wkv[pl.ds(chunk * 4, 4)].reshape(512, 512)
        return nn(rows, weights)

    both = project_caption(c) + project_caption(2 + c)
    for near in (0, 1):
        for z in (0, 1):
            chunk = near * 2 + 1 - c
            arrived(r.caps.at[chunk, z], r.cp_r.at[chunk, z])
        both = both + project_caption(near * 2 + 1 - c)
    second = jnp.full((64, 512), zl, jnp.int32) == 1
    r.kvx_send[...] = jnp.where(second, both[0:64], both[64:128]).astype(BF16)
    start(remote(r.kvx_send, r.kvx_recv, r.kvx_s.at[0], r.kvx_r.at[0], other, t))

    r.cap_k[x] = r.caps[x]
    for q in range(4):
        column = pl.multiple_of(y * 128, 128)
        r.cap_v[y, q] = r.caps[q, :, :, pl.ds(column, 128)]
    for k in (1, 3, 2):
        xx = turn(x, k, 4)
        start(
            remote(r.caps.at[xx], r.cap_k.at[x], r.ck_s.at[k], r.ck_r.at[x], plane(xx, y), t)
        )
        yy = turn(y, k, 4)
        column = pl.multiple_of(yy * 128, 128)
        start(
            remote(
                r.caps.at[:, :, :, pl.ds(column, 128)],
                r.cap_v.at[y],
                r.cv_s.at[k],
                r.cv_r.at[y],
                plane(x, yy),
                t,
            )
        )

    clean = r.clean[0].astype(F32)
    noise = r.noise[0].astype(F32)
    tau = jnp.full((1, 256), r.step_index[0], jnp.int32).astype(F32) / STEPS
    margin = jnp.zeros((PADDED - FRAMES, 256), F32)
    blend_f = jnp.concatenate([(1.0 - tau) * clean + tau * noise, margin], axis=0)
    r.blend[...] = blend_f.astype(BF16)
    blend = r.blend[...]
    blend_f = blend.astype(F32)
    plane_arrived(r.agb, r.ab_r.at[0])
    plane_arrived(r.agf.at[c], r.af_r.at[0])
    start(remote(r.agf.at[c], r.agf.at[c], r.ap_s.at[0], r.ap_r.at[0], d, mate))
    matrices = r.agb[...].astype(F32)

    def planes(slabs):
        return jnp.concatenate([slabs[:, z].reshape(128, 256) for z in (0, 1)], axis=0)

    mat_a = planes(matrices[:, :, 0:8]).astype(BF16)
    mat_m = planes(matrices[:, :, 8:16]).astype(BF16)
    arrived(r.agf.at[1 - c], r.ap_r.at[0])
    mat_b = planes(r.agf[0])
    mat_s = planes(r.agf[1])
    r.hid_v[...] = nn(blend_f, mat_b, HIGHEST) + time_own[:, 256:512]
    spread = (nn(blend_f, mat_s, HIGHEST) + 2.0 * time_own[:, 512:768]) * blend_f
    variance = (jnp.sum(spread, axis=1, keepdims=True) + time_square) / 2048.0
    rstd = lax.rsqrt(jnp.maximum(variance, 0.0) + EPSILON)
    r.query[...] = ((nn(blend, mat_a) + time_own[:, 0:256]) * rstd).astype(BF16)

    kv_own = jnp.where(second, both[64:128], both[0:64])
    arrived(r.kvx_recv, r.kvx_r.at[0])
    kv = (kv_own + r.kvx_recv[...].astype(F32)).astype(BF16)

    query = r.query[...]
    allowed = lax.broadcasted_iota(jnp.int32, (PADDED, 64), 1) < length
    probs = []
    attended = []
    for h in (0, 1):
        span = slice(128 * h, 128 * h + 128)
        scores = nt(query[:, span], kv[:, span]) * SCALE
        prob = softmax(jnp.where(allowed, scores, -1e30))
        probs.append(prob)
        attended.append(nn(prob.astype(BF16), kv[:, 256 + 128 * h : 384 + 128 * h]).astype(BF16))
    attended = jnp.concatenate(attended, axis=1)
    branch = nn(attended, mat_m).reshape(8, 48, 256)

    first_half = jnp.full((48, 256), c, jnp.int32) == 0
    for q in range(4):
        r.va_send[q] = jnp.where(first_half, branch[2 * q + 1], branch[2 * q]).astype(BF16)
        r.v_own[q] = jnp.where(first_half, branch[2 * q], branch[2 * q + 1])
    start(remote(r.va_send, r.va_recv, r.va_s.at[0], r.va_r.at[0], d, mate))
    r.att_t[...] = attended.T
    for h in (0, 1):
        r.prob_t[h] = probs[h].astype(BF16).T
    arrived(r.va_recv, r.va_r.at[0])
    for k in (2, 1, 3):
        slot = turn(zh, k, 4)
        r.vb_send[slot] = (r.v_own[slot] + r.va_recv[slot].astype(F32)).astype(BF16)
        start(
            remote(
                r.vb_send.at[slot], r.vb_recv.at[zh], r.vb_s.at[k], r.vb_r.at[zh], d, slot * 2 + c
            )
        )
    r.blend_t[...] = blend.T
    for k in (1, 3, 2):
        slot = turn(x, k, 4)
        arrived(r.cap_k.at[slot], r.ck_r.at[slot])
    r.cap_kt[...] = r.cap_k[...].reshape(512, 512).T
    own = r.v_own[zh] + r.va_recv[zh].astype(F32)
    for k in (1, 3, 2):
        slot = turn(zh, k, 4)
        arrived(r.vb_recv.at[slot], r.vb_r.at[slot])
        own = own + r.vb_recv[slot].astype(F32)
    r.vg[t] = own.astype(BF16)
    for k in (2, 1, 3):
        start(remote(r.vg.at[t], r.vg.at[t], r.vg_s.at[k], r.vg_r.at[t], d, turn(zh, k, 4) * 2 + c))
    start(remote(r.vg.at[t], r.vg.at[t], r.vg_s.at[0], r.vg_r.at[t], d, mate))
    for k in (1, 3, 2):
        slot = turn(y, k, 4)
        arrived(r.cap_v.at[slot], r.cv_r.at[slot])
    for q in range(4):
        r.cap_vt[q] = r.cap_v[:, q].reshape(512, 128).T
    for k in (1, 3, 2):
        slot = turn(zh, k, 4) * 2 + c
        arrived(r.vg.at[slot], r.vg_r.at[slot])
        start(remote(r.vg.at[slot], r.vg.at[slot], r.vg_s.at[4 + k], r.vg_r.at[slot], d, mate))
    arrived(r.vg.at[mate], r.vg_r.at[mate])
    for k in (1, 3, 2):
        slot = turn(zh, k, 4) * 2 + 1 - c
        arrived(r.vg.at[slot], r.vg_r.at[slot])

    predicted = r.hid_v[...] + r.vg[...].astype(F32).reshape(PADDED, 256)
    residual = predicted - jnp.concatenate([noise - clean, margin], axis=0)
    frames = jnp.full((PADDED, 1), r.motion_len[0], jnp.int32)
    live = lax.broadcasted_iota(jnp.int32, (PADDED, 1), 0) < frames
    row_weight = jnp.where(live, 1.0 / frames.astype(F32), 0.0)
    weighted = residual * row_weight
    loss_part = total(residual * weighted)
    d_vel = (2.0 * weighted).astype(BF16)
    d_att = nt(d_vel, mat_m).astype(BF16)

    heads = [d_att[:, 128 * h : 128 * h + 128] for h in (0, 1)]
    d_values = [nn(r.prob_t[h], heads[h]) for h in (0, 1)]
    r.dkx[1, zl] = jnp.concatenate(d_values, axis=1).astype(BF16)

    def dx_start(i):
        ref = r.dkx.at[i, zl]
        start(remote(ref, ref, r.dx_s.at[i], r.dx_r.at[i], other, t))

    dx_start(1)
    d_scores = []
    for h in (0, 1):
        d_prob = nt(heads[h], kv[:, 256 + 128 * h : 384 + 128 * h])
        delta = jnp.sum(probs[h] * d_prob, axis=1, keepdims=True)
        d_scores.append((probs[h] * (d_prob - delta) * SCALE).astype(BF16))
    d_keys = [tn(d_scores[h], query[:, 128 * h : 128 * h + 128]) for h in (0, 1)]
    r.dkx[0, zl] = jnp.concatenate(d_keys, axis=1).astype(BF16)
    dx_start(0)
    d_queries = [nn(d_scores[h], kv[:, 128 * h : 128 * h + 128]) for h in (0, 1)]
    d_query = jnp.concatenate(d_queries, axis=1).astype(BF16).astype(F32) * rstd
    mat_h = nn(r.blend_t[...], d_query.astype(BF16)).reshape(32, 8, 256)
    mat_g = nn(r.att_t[...], d_vel).reshape(32, 8, 256)
    r.hs[:, :, 0:256] = jnp.concatenate([mat_h, mat_g], axis=1).astype(BF16)
    frame_sum = jnp.sum(d_query, axis=0, keepdims=True)
    loss_high = loss_part.astype(BF16).astype(F32)
    which = lax.broadcasted_iota(jnp.int32, (16, 128), 0)
    extra = jnp.where(which == 2, loss_high, loss_part - loss_high)
    extra = jnp.where(which == 1, frame_sum[:, 128:256], extra)
    extra = jnp.where(which == 0, frame_sum[:, 0:128], extra)
    r.hs[:, :, 256:384] = jnp.broadcast_to(extra.astype(BF16)[None], (32, 16, 128))
    r.hr[d] = r.hs[d]

    def h_copy(k, peer):
        return remote(r.hs.at[peer], r.hr.at[d], r.hs_s.at[0], r.hs_r.at[0], peer, t)

    over_dp(lambda k, peer: h_copy(k, peer).start())

    arrived(r.dkx.at[1, 1 - zl], r.dx_r.at[1])
    r.dv[y] = r.dkx[1]
    for k in (1, 3, 2):
        start(
            remote(
                r.dv.at[y], r.dv.at[y], r.dv_s.at[k], r.dv_r.at[y], plane(x, turn(y, k, 4)), t
            )
        )
    arrived(r.dkx.at[0, 1 - zl], r.dx_r.at[0])
    r.dk[x] = r.dkx[0]
    for k in (1, 3, 2):
        start(
            remote(
                r.dk.at[x], r.dk.at[x], r.dk_s.at[k], r.dk_r.at[x], plane(turn(x, k, 4), y), t
            )
        )

    all_arrived(r.hr, r.hs_r.at[0])
    arrivals = r.hr[...].astype(F32)
    r.hg[d] = jnp.sum(arrivals[:, :, 0:256], axis=0).astype(BF16)

    def g_copy(k, peer):
        return remote(r.hg.at[d], r.hg.at[d], r.hg_s.at[0], r.hg_r.at[0], peer, t)

    over_dp(lambda k, peer: g_copy(k, peer).start())

    for k in (1, 3, 2):
        slot = turn(y, k, 4)
        arrived(r.dv.at[slot], r.dv_r.at[slot])
    all_v = r.dv[...].reshape(512, 256)
    for q in range(4):
        r.gv_send[q] = nn(r.cap_vt[q], all_v).astype(BF16)
    for k in (1, 3, 2):
        xx = turn(x, k, 4)
        start(
            remote(
                r.gv_send.at[xx], r.gv_recv.at[x], r.gv_s.at[k], r.gv_r.at[x], plane(xx, y), t
            )
        )
    r.gv_recv[x] = r.gv_send[x]
    for k in (1, 3, 2):
        slot = turn(x, k, 4)
        arrived(r.dk.at[slot], r.dk_r.at[slot])
    all_k = r.dk[...].reshape(512, 256)
    grad_k = nn(r.cap_kt[...], all_k).reshape(4, 128, 256)
    for q in range(4):
        r.gk_send[q] = grad_k[q].astype(BF16)
    for k in (1, 3, 2):
        yy = turn(y, k, 4)
        start(
            remote(
                r.gk_send.at[yy], r.gk_recv.at[y], r.gk_s.at[k], r.gk_r.at[y], plane(x, yy), t
            )
        )
    r.gk_recv[y] = r.gk_send[y]

    sums_p = jnp.concatenate([arrivals[:, 0, 256:384], arrivals[:, 1, 256:384]], axis=1)
    losses = arrivals[:, 2, 256:384] + arrivals[:, 3, 256:384]
    r.loss_out[...] = jnp.sum(losses, axis=0, keepdims=True) / 8192.0
    all_arrived(r.hg, r.hg_r.at[0])
    grads = r.hg[...].astype(F32)
    sum_h = grads[:, 0:8].reshape(256, 256)
    sum_g = grads[:, 8:16].reshape(256, 256).astype(BF16)
    r.packed_out[0:64] = nn(w_c, sum_h, HIGHEST) + tn(times_c, sums_p, HIGHEST)
    r.packed_out[320:384] = nt(r.vel[...], sum_g)
    for k in (1, 3, 2):
        slot = turn(y, k, 4)
        arrived(r.gk_recv.at[slot], r.gk_r.at[slot])
        slot = turn(x, k, 4)
        arrived(r.gv_recv.at[slot], r.gv_r.at[slot])
    r.packed_out[64:192] = jnp.sum(r.gk_recv[...].astype(F32), axis=0)
    r.packed_out[192:320] = jnp.sum(r.gv_recv[...].astype(F32), axis=0)

    for copy in pending:
        copy.wait_send()

    @pl.when(jnp.logical_not(inside))
    def _():
        cap_copy(0).wait_send()

    all_left(r.c0, r.c0_s.at[0])
    plane_left(r.zrb, r.zb_s.at[0])
    plane_left(r.zrf, r.zf_s.at[0])
    plane_left(r.agb, r.ab_s.at[0])
    plane_left(r.agf.at[c], r.af_s.at[0])
    all_left(r.hr, r.hs_s.at[0])
    all_left(r.hg, r.hg_s.at[0])


def unpack(loss, packed, loss_out, gq, gk, gv, go):
    loss_out[...] = loss[...]
    gq[...] = packed[0:64]
    gk[...] = packed[64:192]
    gv[...] = packed[192:320]
    go[...] = packed[320:384]


def rope_tables():
    inverse = 1000000.0 ** (-(np.arange(64, dtype=np.float32) * 2.0 / 128))
    angles = np.arange(64, dtype=np.float32)[:, None] * inverse[None, :].astype(np.float32)
    angles = np.concatenate([angles, angles], axis=1).astype(np.float32)
    sign = np.where(np.arange(128) < 64, -1.0, 1.0)[None, :]
    return np.cos(angles).astype(np.float32), (np.sin(angles) * sign).astype(np.float32)


def local(
    encoder_input_states,
    caption_lengths,
    encoder_input_gain,
    query_head_gain,
    key_head_gain,
    encoder_query_weight,
    encoder_key_weight,
    encoder_value_weight,
    encoder_output_weight,
    clean_motion,
    noise,
    timestep_index,
    motion_lengths,
    input_weight,
    velocity_weight,
    cross_query_weight,
    cross_key_weight,
    cross_value_weight,
    cross_output_weight,
):
    vmem = pl.BlockSpec(memory_space=pltpu.VMEM)
    hbm = pl.BlockSpec(memory_space=pl.ANY)
    smem = pl.BlockSpec(memory_space=pltpu.SMEM)
    spec = {name: vmem for name in INPUTS}
    for name in ("cap_len", "step_index", "motion_len"):
        spec[name] = smem
    for name in ("eq", "ek", "ev", "eo"):
        spec[name] = hbm
    cosine, sine = rope_tables()
    packed = pl.pallas_call(
        kernel,
        out_shape=[
            jax.ShapeDtypeStruct((1, 128), F32),
            jax.ShapeDtypeStruct((384, 256), F32),
        ],
        in_specs=[spec[name] for name in INPUTS],
        out_specs=[vmem] * 2,
        scratch_shapes=[pltpu.VMEM(shape, kind) for shape, kind in BUFFERS.values()]
        + [
            pltpu.SemaphoreType.DMA(shape if isinstance(shape, tuple) else (shape,))
            for shape in SEMAPHORES.values()
        ],
        compiler_params=pltpu.CompilerParams(
            collective_id=0, has_side_effects=True, vmem_limit_bytes=56 * 2**20
        ),
        name="motion_block",
    )(
        encoder_input_states,
        caption_lengths,
        timestep_index,
        motion_lengths,
        encoder_input_gain.reshape(8, 1, 512),
        query_head_gain.reshape(1, 128),
        key_head_gain.reshape(1, 128),
        jnp.asarray(cosine),
        jnp.asarray(sine),
        encoder_query_weight,
        encoder_key_weight,
        encoder_value_weight,
        encoder_output_weight,
        clean_motion,
        noise,
        input_weight.T,
        velocity_weight,
        cross_query_weight,
        cross_key_weight,
        cross_value_weight,
        cross_output_weight.T,
    )
    loss, gq, gk, gv, go = pl.pallas_call(
        unpack,
        out_shape=[
            jax.ShapeDtypeStruct((1, 128), F32),
            jax.ShapeDtypeStruct((64, 256), F32),
            jax.ShapeDtypeStruct((128, 256), F32),
            jax.ShapeDtypeStruct((128, 256), F32),
            jax.ShapeDtypeStruct((64, 256), F32),
        ],
        in_specs=[vmem] * 2,
        out_specs=[vmem] * 5,
        name="unpack",
    )(*packed)
    return (loss[0, 0], gq, gk, gv, go.T)


def solution(mesh):
    placed = (
        P("dp", None, "tensor"),
        P("dp"),
        P(),
        P(),
        P(),
        P(None, "tensor"),
        P(None, "tensor"),
        P(None, "tensor"),
        P("tensor", None),
        P("dp", None, None),
        P("dp", None, None),
        P("dp"),
        P("dp"),
        P(None, "dp"),
        P("dp", None),
        P("dp", "tensor"),
        P("dp", "tensor"),
        P("dp", "tensor"),
        P("tensor", "dp"),
    )
    return jax.shard_map(
        local,
        mesh=mesh,
        in_specs=placed,
        out_specs=(P(), P("dp", "tensor"), P("dp", "tensor"), P("dp", "tensor"), P("tensor", "dp")),
        check_vma=False,
    )
```

```python
import math
import types

import jax
import jax.numpy as jnp
import numpy as np
from jax import lax
from jax.experimental import pallas as pl
from jax.experimental.pallas import tpu as pltpu
from jax.sharding import PartitionSpec as P

F32 = jnp.float32
BF16 = jnp.bfloat16
MESH = pl.DeviceIdType.MESH
HIGHEST = lax.Precision.HIGHEST
EPSILON = 1e-06
STEPS = 1000
FRAMES = 360
PADDED = 384
SCALE = 1.0 / math.sqrt(128)

INPUTS = [
    "states", "cap_len", "step_index", "motion_len", "gain", "q_gain", "k_gain", "cosine", "sine",
    "eq", "ek", "ev", "eo", "clean", "noise", "w_in", "vel", "wq", "wk", "wv", "wo",
]
OUTPUTS = ["loss", "packed"]

BUFFERS = dict(
    w_qkv=((4096, 768), BF16),
    w_out=((512, 4096), BF16),
    c0=((32, 1, 384), F32),
    gx=((8, 64, 512), BF16),
    wkv=((16, 2, 64, 512), BF16),
    zsb=((16, 2, 16, 256), BF16),
    zrb=((16, 2, 16, 256), BF16),
    zsf=((16, 2, 8, 384), F32),
    zrf=((16, 2, 8, 384), F32),
    pzb=((2, 2, 16, 256), BF16),
    pzf=((2, 2, 8, 384), F32),
    agb=((16, 2, 16, 256), BF16),
    agf=((2, 16, 2, 8, 256), F32),
    ra_send=((4, 64, 512), BF16),
    ra_recv=((4, 64, 512), BF16),
    rb_send=((4, 64, 512), BF16),
    rb_recv=((4, 64, 512), BF16),
    r_own=((4, 64, 512), F32),
    cap_own=((64, 512), BF16),
    caps=((4, 2, 64, 512), BF16),
    kvx_send=((64, 512), BF16),
    kvx_recv=((64, 512), BF16),
    blend=((PADDED, 256), BF16),
    query=((PADDED, 256), BF16),
    hid_v=((PADDED, 256), F32),
    va_send=((4, 48, 256), BF16),
    va_recv=((4, 48, 256), BF16),
    v_own=((4, 48, 256), F32),
    vb_send=((4, 48, 256), BF16),
    vb_recv=((4, 48, 256), BF16),
    vg=((8, 48, 256), BF16),
    dkx=((2, 2, 64, 256), BF16),
    dk=((4, 2, 64, 256), BF16),
    dv=((4, 2, 64, 256), BF16),
    cap_k=((4, 2, 64, 512), BF16),
    cap_v=((4, 4, 2, 64, 128), BF16),
    cap_kt=((512, 512), BF16),
    cap_vt=((4, 128, 512), BF16),
    blend_t=((256, PADDED), BF16),
    att_t=((256, PADDED), BF16),
    prob_t=((2, 64, PADDED), BF16),
    gk_send=((4, 128, 256), BF16),
    gk_recv=((4, 128, 256), BF16),
    gv_send=((4, 128, 256), BF16),
    gv_recv=((4, 128, 256), BF16),
    hs=((32, 16, 384), BF16),
    hr=((32, 16, 384), BF16),
    hg=((32, 16, 256), BF16),
)

SEMAPHORES = dict(
    load=4,
    c0_s=1, c0_r=1,
    gx_s=8, gx_r=8,
    wkv_s=32, wkv_r=(16, 2),
    zb_s=1, zb_r=1, zf_s=1, zf_r=1, pb_s=1, pb_r=1, pf_s=1, pf_r=1,
    ab_s=1, ab_r=1, af_s=1, af_r=1, ap_s=1, ap_r=1,
    ra_s=4, ra_r=4, rb_s=4, rb_r=4,
    cp_s=8, cp_r=(4, 2),
    kvx_s=1, kvx_r=1,
    va_s=1, va_r=1, vb_s=4, vb_r=4, vg_s=8, vg_r=8,
    dx_s=2, dx_r=2, dk_s=4, dk_r=4, dv_s=4, dv_r=4,
    ck_s=4, ck_r=4, cv_s=4, cv_r=4,
    gk_s=4, gk_r=4, gv_s=4, gv_r=4,
    hs_s=1, hs_r=1, hg_s=1, hg_r=1,
)


def dot(a, b, left, right, precision=None):
    return lax.dot_general(
        a, b, (((left,), (right,)), ((), ())), precision=precision, preferred_element_type=F32
    )


def nn(a, b, precision=None):
    return dot(a, b, 1, 0, precision)


def nt(a, b, precision=None):
    return dot(a, b, 1, 1, precision)


def tn(a, b, precision=None):
    return dot(a, b, 0, 0, precision)


def softmax(scores):
    top = jnp.max(scores, axis=-1, keepdims=True)
    weights = jnp.exp(scores - top)
    return weights / jnp.sum(weights, axis=-1, keepdims=True)


def remote(source, target, send, receive, dp, tensor):
    return pltpu.make_async_remote_copy(
        src_ref=source,
        dst_ref=target,
        send_sem=send,
        recv_sem=receive,
        device_id=(dp, tensor),
        device_id_type=MESH,
    )


def kernel(*refs):
    names = INPUTS + [n + "_out" for n in OUTPUTS] + list(BUFFERS) + list(SEMAPHORES)
    r = types.SimpleNamespace(**dict(zip(names, refs, strict=True)))

    d = lax.axis_index("dp")
    t = lax.axis_index("tensor")
    zl = lax.div(d, 16)
    xy = lax.rem(d, 16)
    x = lax.div(xy, 4)
    y = lax.rem(xy, 4)
    zh = lax.div(t, 2)
    c = lax.rem(t, 2)
    mate = t + 1 - 2 * c
    other = (1 - zl) * 16 + xy
    pending = []

    def start(copy):
        copy.start()
        pending.append(copy)

    def turn(base, k, size):
        return lax.rem(base + k, size)

    def plane(xx, yy):
        return zl * 16 + xx * 4 + yy

    def arrived(slot, semaphore):
        remote(slot, slot, semaphore, semaphore, other, t).wait_recv()

    def all_arrived(buffer, semaphore):
        most = buffer.at[pl.ds(0, 31)]
        remote(most, most, semaphore, semaphore, other, t).wait_recv()

    def all_left(buffer, semaphore):
        most = buffer.at[pl.ds(0, 31)]
        remote(most, most, semaphore, semaphore, other, t).wait_send()

    def plane_arrived(buffer, semaphore):
        most = buffer.at[pl.ds(0, 15)]
        remote(most, most, semaphore, semaphore, other, t).wait_recv()

    def plane_left(buffer, semaphore):
        most = buffer.at[pl.ds(0, 15)]
        remote(most, most, semaphore, semaphore, other, t).wait_send()

    def over_plane(body):
        def step(k, carry):
            body(turn(xy, k, 16))
            return carry

        lax.fori_loop(1, 16, step, 0)

    def over_dp(body):
        def step(k, carry):
            body(k, turn(d, k, 32))
            return carry

        lax.fori_loop(1, 32, step, 0)

    loads = [
        pltpu.make_async_copy(r.eq, r.w_qkv.at[:, pl.ds(0, 512)], r.load.at[0]),
        pltpu.make_async_copy(r.ek, r.w_qkv.at[:, pl.ds(512, 128)], r.load.at[1]),
        pltpu.make_async_copy(r.ev, r.w_qkv.at[:, pl.ds(640, 128)], r.load.at[2]),
        pltpu.make_async_copy(r.eo, r.w_out, r.load.at[3]),
    ]
    for load in loads:
        load.start()

    barrier = pltpu.get_barrier_semaphore()

    def signal(dp, tensor):
        pl.semaphore_signal(barrier, inc=1, device_id=(dp, tensor), device_id_type=MESH)

    over_dp(lambda k, peer: signal(peer, t))
    signal(d, mate)
    for k in (1, 2, 3):
        signal(d, turn(zh, k, 4) * 2 + c)
        signal(other, turn(zh, k, 4) * 2 + c)

    r.gx[t] = r.states[0]
    wk_v = r.wk[...]
    wv_v = r.wv[...]
    for half in (0, 1):
        r.wkv[xy, half, :, 0:256] = wk_v[64 * half : 64 * half + 64]
        r.wkv[xy, half, :, 256:512] = wv_v[64 * half : 64 * half + 64]
    pl.semaphore_wait(barrier, 38)

    for k in (2, 1, 3):
        start(remote(r.gx.at[t], r.gx.at[t], r.gx_s.at[k], r.gx_r.at[t], d, turn(zh, k, 4) * 2 + c))
    start(remote(r.gx.at[t], r.gx.at[t], r.gx_s.at[0], r.gx_r.at[t], d, mate))

    def wkv_send(slot, half, dp, index):
        ref = r.wkv.at[slot, half]
        start(remote(ref, ref, r.wkv_s.at[index], r.wkv_r.at[slot, half], dp, t))

    for k in (1, 3, 2):
        wkv_send(xy, 0, plane(turn(x, k, 4), y), k - 1)
        wkv_send(xy, 1, plane(x, turn(y, k, 4)), 2 + k)

    w_in_v = r.w_in[...]
    w_in_t = w_in_v.astype(F32)
    decay = -math.log(10000.0) / 1024.0
    step_f = jnp.full((8, 128), r.step_index[0], jnp.int32).astype(F32)
    place = (
        lax.broadcasted_iota(jnp.int32, (8, 128), 0) * 128
        + lax.broadcasted_iota(jnp.int32, (8, 128), 1)
    ).astype(F32)
    all_angles = step_f * jnp.exp(decay * place)
    all_cos = jnp.cos(all_angles)
    all_sin = jnp.sin(all_angles)

    def total(tile):
        return jnp.sum(jnp.sum(tile, axis=1, keepdims=True), axis=0, keepdims=True)

    own_mean = total(all_cos + all_sin) / 2048.0
    time_square = total((all_cos - own_mean) ** 2 + (all_sin - own_mean) ** 2)
    lane = lax.broadcasted_iota(jnp.int32, (1, 128), 1)
    r.c0[d, :, 0:256] = jnp.sum(w_in_t, axis=0, keepdims=True)
    r.c0[d, :, 256:384] = jnp.where(lane == 0, step_f[0:1], own_mean)

    vel_v = r.vel[...]
    wq_v = r.wq[...]
    part_m = tn(r.wo[...], vel_v).reshape(32, 8, 256)
    part_b = tn(w_in_v, vel_v)

    def c0_copy(k, peer):
        return remote(r.c0.at[d], r.c0.at[d], r.c0_s.at[0], r.c0_r.at[0], peer, t)

    over_dp(lambda k, peer: c0_copy(k, peer).start())

    def wkv_second(first, k_list):
        for k in k_list:
            if k:
                slot = turn(x, k, 4) * 4 + y
                arrived(r.wkv.at[slot, 0], r.wkv_r.at[slot, 0])
                slot = x * 4 + turn(y, k, 4)
                arrived(r.wkv.at[slot, 1], r.wkv_r.at[slot, 1])
            for j in (1, 3, 2):
                wkv_send(turn(x, k, 4) * 4 + y, 0, plane(x, turn(y, j, 4)), first + 6 * k + j - 1)
                wkv_send(
                    x * 4 + turn(y, k, 4), 1, plane(turn(x, j, 4), y), first + 6 * k + 2 + j
                )

    wkv_second(6, (0, 1, 3, 2))

    for load in loads[:3]:
        load.wait()

    def project(slot, sums, square):
        chunk = r.gx[slot].astype(F32)
        square = square + jnp.sum(chunk * chunk, axis=1, keepdims=True)
        row = pl.multiple_of(slot * 512, 512)
        scaled = (chunk * r.gain[slot]).astype(BF16)
        return sums + nn(scaled, r.w_qkv[pl.ds(row, 512), :]), square

    sums, square = project(t, jnp.zeros((64, 768), F32), jnp.zeros((64, 1), F32))

    for k in (1, 3, 2):
        slot = turn(zh, k, 4) * 2 + c
        arrived(r.gx.at[slot], r.gx_r.at[slot])
        start(remote(r.gx.at[slot], r.gx.at[slot], r.gx_s.at[4 + k], r.gx_r.at[slot], d, mate))
        sums, square = project(slot, sums, square)

    arrived(r.gx.at[mate], r.gx_r.at[mate])
    sums, square = project(mate, sums, square)
    for k in (1, 3, 2):
        slot = turn(zh, k, 4) * 2 + (1 - c)
        arrived(r.gx.at[slot], r.gx_r.at[slot])
        sums, square = project(slot, sums, square)

    length = r.cap_len[0]
    rms = lax.rsqrt(square / 4096.0 + EPSILON)
    sums = sums * rms
    cosine = r.cosine[...]
    sine = r.sine[...]

    def turned(vectors, scaling):
        mean = jnp.mean(vectors * vectors, axis=1, keepdims=True)
        vectors = vectors * lax.rsqrt(mean + EPSILON) * scaling
        return (vectors * cosine + pltpu.roll(vectors, 64, 1) * sine).astype(BF16)

    q_gain = r.q_gain[...]
    queries = jnp.concatenate(
        [turned(sums[:, 128 * h : 128 * h + 128], q_gain) for h in range(4)], axis=0
    )
    keys = turned(sums[:, 512:640], r.k_gain[...])
    values = sums[:, 640:768].astype(BF16)
    scores = nt(queries, keys) * SCALE
    row = lax.rem(lax.broadcasted_iota(jnp.int32, (256, 64), 0), 64)
    col = lax.broadcasted_iota(jnp.int32, (256, 64), 1)
    scores = jnp.where((col <= row) & (col < length), scores, -1e30)
    mixed = nn(softmax(scores).astype(BF16), values).astype(BF16)
    mixed = jnp.concatenate([mixed[64 * h : 64 * h + 64] for h in range(4)], axis=1)

    loads[3].wait()
    for k in (1, 3, 2, 0):
        slot = turn(zh, k, 4)
        column = pl.multiple_of((slot * 2 + 1 - c) * 512, 512)
        r.ra_send[slot] = nn(mixed, r.w_out[:, pl.ds(column, 512)]).astype(BF16)
        start(
            remote(
                r.ra_send.at[slot], r.ra_recv.at[slot], r.ra_s.at[k], r.ra_r.at[slot], d, mate
            )
        )
    for k in (1, 3, 2, 0):
        slot = turn(zh, k, 4)
        column = pl.multiple_of((slot * 2 + c) * 512, 512)
        r.r_own[slot] = nn(mixed, r.w_out[:, pl.ds(column, 512)])
    for k in (2, 1, 3):
        slot = turn(zh, k, 4)
        arrived(r.ra_recv.at[slot], r.ra_r.at[slot])
        r.rb_send[slot] = (r.r_own[slot] + r.ra_recv[slot].astype(F32)).astype(BF16)
        start(
            remote(
                r.rb_send.at[slot], r.rb_recv.at[zh], r.rb_s.at[k], r.rb_r.at[zh], d, slot * 2 + c
            )
        )

    all_arrived(r.c0, r.c0_r.at[0])
    facts = r.c0[...].reshape(32, 384)
    w_mean = jnp.sum(facts[:, 0:256], axis=0, keepdims=True) / 2048.0
    steps = facts[:, 256:257]
    step_means = facts[:, 257:258]
    column = (
        lax.broadcasted_iota(jnp.int32, (1, 64), 1) + lax.rem(d, 16) * 64
    ).astype(F32)
    angles = steps * jnp.exp(decay * column)
    quarter = jnp.full((32, 64), zl, jnp.int32).astype(F32) * (math.pi / 2.0)
    times = jnp.cos(angles - quarter)
    times_c = times - step_means
    w_c = w_in_t - w_mean
    part_a = tn(w_c.astype(BF16), wq_v).reshape(32, 8, 256)
    slabs_b = jnp.concatenate([part_a, part_m], axis=1).astype(BF16)
    first_core = jnp.full((256, 256), c, jnp.int32) == 0
    part_f = jnp.where(first_core, part_b, tn(w_c, w_c, HIGHEST))
    slabs_f = part_f.reshape(32, 8, 256)
    time_rows = jnp.concatenate(
        [
            nn(times_c, wq_v.astype(F32), HIGHEST),
            nn(times, vel_v.astype(F32), HIGHEST),
            nn(times_c, w_c, HIGHEST),
        ],
        axis=1,
    )
    for z in (0, 1):
        here = slice(16 * z, 16 * z + 16)
        r.zsb[:, z] = slabs_b[here]
        r.zsf[:, z, :, 0:256] = slabs_f[here]
        for i in range(8):
            part = time_rows[here, 128 * i : 128 * i + 128] if i < 6 else jnp.zeros((16, 128), F32)
            r.zsf[:, z, i, 256:384] = part
    r.zrb[xy] = r.zsb[xy]
    r.zrf[xy] = r.zsf[xy]

    def z_start(peer):
        dp = zl * 16 + peer
        remote(r.zsb.at[peer], r.zrb.at[xy], r.zb_s.at[0], r.zb_r.at[0], dp, t).start()
        remote(r.zsf.at[peer], r.zrf.at[xy], r.zf_s.at[0], r.zf_r.at[0], dp, t).start()

    over_plane(z_start)

    slot = zh
    arrived(r.ra_recv.at[slot], r.ra_r.at[slot])
    own = r.r_own[slot] + r.ra_recv[slot].astype(F32)
    for k in (1, 3, 2):
        slot = turn(zh, k, 4)
        arrived(r.rb_recv.at[slot], r.rb_r.at[slot])
        own = own + r.rb_recv[slot].astype(F32)
    r.cap_own[...] = (r.states[0].astype(F32) + own).astype(BF16)

    target = lax.div(zh, 2)
    mine = lax.rem(t, 4)
    inside = target == zl

    def cap_copy(k):
        return remote(
            r.cap_own,
            r.caps.at[mine, zl],
            r.cp_s.at[k],
            r.cp_r.at[mine, zl],
            target * 16 + xy,
            turn(zh, k, 4) * 2 + c,
        )

    for k in (2, 1, 3):
        start(cap_copy(k))

    @pl.when(inside)
    def _():
        r.caps[mine, zl] = r.cap_own[...]

    @pl.when(jnp.logical_not(inside))
    def _():
        cap_copy(0).start()

    plane_arrived(r.zrb, r.zb_r.at[0])
    plane_arrived(r.zrf, r.zf_r.at[0])
    plane_b = jnp.sum(r.zrb[...].astype(F32), axis=0)
    plane_f = jnp.sum(r.zrf[...], axis=0)
    r.pzb[zl] = plane_b.astype(BF16)
    r.pzf[zl] = plane_f
    start(remote(r.pzb.at[zl], r.pzb.at[zl], r.pb_s.at[0], r.pb_r.at[0], other, t))
    start(remote(r.pzf.at[zl], r.pzf.at[zl], r.pf_s.at[0], r.pf_r.at[0], other, t))

    for k in (0, 1, 2, 3):
        for j in (1, 2, 3):
            slot = turn(x, k, 4) * 4 + turn(y, j, 4)
            arrived(r.wkv.at[slot, 0], r.wkv_r.at[slot, 0])
            slot = turn(x, j, 4) * 4 + turn(y, k, 4)
            arrived(r.wkv.at[slot, 1], r.wkv_r.at[slot, 1])

    forwards = []
    for z in (0, 1):
        for near in (0, 1):
            chunk = near * 2 + c
            ref = r.caps.at[chunk, z]
            own_slot = inside & (chunk == mine) & (z == zl)

            @pl.when(jnp.logical_not(own_slot))
            def _(ref=ref, chunk=chunk, z=z):
                arrived(ref, r.cp_r.at[chunk, z])

            start(remote(ref, ref, r.cp_s.at[4 + 2 * z + near], r.cp_r.at[chunk, z], d, mate))

    arrived(r.pzb.at[1 - zl], r.pb_r.at[0])
    arrived(r.pzf.at[1 - zl], r.pf_r.at[0])
    r.agb[xy] = (plane_b + r.pzb[1 - zl].astype(F32)).astype(BF16)
    slabs = plane_f + r.pzf[1 - zl]
    r.agf[c, xy] = slabs[:, :, 0:256]
    late = jnp.full((8, 128), zl, jnp.int32) == 1
    rows = jnp.where(late, slabs[1, :, 256:384], slabs[0, :, 256:384])
    time_own = jnp.concatenate([rows[i : i + 1] for i in range(6)], axis=1)

    def a_start(peer):
        dp = zl * 16 + peer
        remote(r.agb.at[xy], r.agb.at[xy], r.ab_s.at[0], r.ab_r.at[0], dp, t).start()
        remote(r.agf.at[c, xy], r.agf.at[c, xy], r.af_s.at[0], r.af_r.at[0], dp, t).start()

    over_plane(a_start)

    def project_caption(chunk):
        rows = r.caps[chunk].reshape(128, 512)
        weights = r.wkv[pl.ds(chunk * 4, 4)].reshape(512, 512)
        return nn(rows, weights)

    both = project_caption(c) + project_caption(2 + c)
    for near in (0, 1):
        for z in (0, 1):
            chunk = near * 2 + 1 - c
            arrived(r.caps.at[chunk, z], r.cp_r.at[chunk, z])
        both = both + project_caption(near * 2 + 1 - c)
    second = jnp.full((64, 512), zl, jnp.int32) == 1
    r.kvx_send[...] = jnp.where(second, both[0:64], both[64:128]).astype(BF16)
    start(remote(r.kvx_send, r.kvx_recv, r.kvx_s.at[0], r.kvx_r.at[0], other, t))

    r.cap_k[x] = r.caps[x]
    for q in range(4):
        column = pl.multiple_of(y * 128, 128)
        r.cap_v[y, q] = r.caps[q, :, :, pl.ds(column, 128)]
    for k in (1, 3, 2):
        xx = turn(x, k, 4)
        start(
            remote(r.caps.at[xx], r.cap_k.at[x], r.ck_s.at[k], r.ck_r.at[x], plane(xx, y), t)
        )
        yy = turn(y, k, 4)
        column = pl.multiple_of(yy * 128, 128)
        start(
            remote(
                r.caps.at[:, :, :, pl.ds(column, 128)],
                r.cap_v.at[y],
                r.cv_s.at[k],
                r.cv_r.at[y],
                plane(x, yy),
                t,
            )
        )

    clean = r.clean[0].astype(F32)
    noise = r.noise[0].astype(F32)
    tau = jnp.full((1, 256), r.step_index[0], jnp.int32).astype(F32) / STEPS
    margin = jnp.zeros((PADDED - FRAMES, 256), F32)
    blend_f = jnp.concatenate([(1.0 - tau) * clean + tau * noise, margin], axis=0)
    r.blend[...] = blend_f.astype(BF16)
    blend = r.blend[...]
    blend_f = blend.astype(F32)
    plane_arrived(r.agb, r.ab_r.at[0])
    plane_arrived(r.agf.at[c], r.af_r.at[0])
    start(remote(r.agf.at[c], r.agf.at[c], r.ap_s.at[0], r.ap_r.at[0], d, mate))
    matrices = r.agb[...].astype(F32)

    def planes(slabs):
        return jnp.concatenate([slabs[:, z].reshape(128, 256) for z in (0, 1)], axis=0)

    mat_a = planes(matrices[:, :, 0:8]).astype(BF16)
    mat_m = planes(matrices[:, :, 8:16]).astype(BF16)
    arrived(r.agf.at[1 - c], r.ap_r.at[0])
    mat_b = planes(r.agf[0])
    mat_s = planes(r.agf[1])
    r.hid_v[...] = nn(blend_f, mat_b, HIGHEST) + time_own[:, 256:512]
    spread = (nn(blend_f, mat_s, HIGHEST) + 2.0 * time_own[:, 512:768]) * blend_f
    variance = (jnp.sum(spread, axis=1, keepdims=True) + time_square) / 2048.0
    rstd = lax.rsqrt(jnp.maximum(variance, 0.0) + EPSILON)
    r.query[...] = ((nn(blend, mat_a) + time_own[:, 0:256]) * rstd).astype(BF16)

    kv_own = jnp.where(second, both[64:128], both[0:64])
    arrived(r.kvx_recv, r.kvx_r.at[0])
    kv = (kv_own + r.kvx_recv[...].astype(F32)).astype(BF16)

    query = r.query[...]
    allowed = lax.broadcasted_iota(jnp.int32, (PADDED, 64), 1) < length
    probs = []
    attended = []
    for h in (0, 1):
        span = slice(128 * h, 128 * h + 128)
        scores = nt(query[:, span], kv[:, span]) * SCALE
        prob = softmax(jnp.where(allowed, scores, -1e30))
        probs.append(prob)
        attended.append(nn(prob.astype(BF16), kv[:, 256 + 128 * h : 384 + 128 * h]).astype(BF16))
    attended = jnp.concatenate(attended, axis=1)
    branch = nn(attended, mat_m).reshape(8, 48, 256)

    first_half = jnp.full((48, 256), c, jnp.int32) == 0
    for q in range(4):
        r.va_send[q] = jnp.where(first_half, branch[2 * q + 1], branch[2 * q]).astype(BF16)
        r.v_own[q] = jnp.where(first_half, branch[2 * q], branch[2 * q + 1])
    start(remote(r.va_send, r.va_recv, r.va_s.at[0], r.va_r.at[0], d, mate))
    r.att_t[...] = attended.T
    for h in (0, 1):
        r.prob_t[h] = probs[h].astype(BF16).T
    arrived(r.va_recv, r.va_r.at[0])
    for k in (2, 1, 3):
        slot = turn(zh, k, 4)
        r.vb_send[slot] = (r.v_own[slot] + r.va_recv[slot].astype(F32)).astype(BF16)
        start(
            remote(
                r.vb_send.at[slot], r.vb_recv.at[zh], r.vb_s.at[k], r.vb_r.at[zh], d, slot * 2 + c
            )
        )
    r.blend_t[...] = blend.T
    for k in (1, 3, 2):
        slot = turn(x, k, 4)
        arrived(r.cap_k.at[slot], r.ck_r.at[slot])
    r.cap_kt[...] = r.cap_k[...].reshape(512, 512).T
    own = r.v_own[zh] + r.va_recv[zh].astype(F32)
    for k in (1, 3, 2):
        slot = turn(zh, k, 4)
        arrived(r.vb_recv.at[slot], r.vb_r.at[slot])
        own = own + r.vb_recv[slot].astype(F32)
    r.vg[t] = own.astype(BF16)
    for k in (2, 1, 3):
        start(remote(r.vg.at[t], r.vg.at[t], r.vg_s.at[k], r.vg_r.at[t], d, turn(zh, k, 4) * 2 + c))
    start(remote(r.vg.at[t], r.vg.at[t], r.vg_s.at[0], r.vg_r.at[t], d, mate))
    for k in (1, 3, 2):
        slot = turn(y, k, 4)
        arrived(r.cap_v.at[slot], r.cv_r.at[slot])
    for q in range(4):
        r.cap_vt[q] = r.cap_v[:, q].reshape(512, 128).T
    for k in (1, 3, 2):
        slot = turn(zh, k, 4) * 2 + c
        arrived(r.vg.at[slot], r.vg_r.at[slot])
        start(remote(r.vg.at[slot], r.vg.at[slot], r.vg_s.at[4 + k], r.vg_r.at[slot], d, mate))
    arrived(r.vg.at[mate], r.vg_r.at[mate])
    for k in (1, 3, 2):
        slot = turn(zh, k, 4) * 2 + 1 - c
        arrived(r.vg.at[slot], r.vg_r.at[slot])

    predicted = r.hid_v[...] + r.vg[...].astype(F32).reshape(PADDED, 256)
    residual = predicted - jnp.concatenate([noise - clean, margin], axis=0)
    frames = jnp.full((PADDED, 1), r.motion_len[0], jnp.int32)
    live = lax.broadcasted_iota(jnp.int32, (PADDED, 1), 0) < frames
    row_weight = jnp.where(live, 1.0 / frames.astype(F32), 0.0)
    weighted = residual * row_weight
    loss_part = total(residual * weighted)
    d_vel = (2.0 * weighted).astype(BF16)
    d_att = nt(d_vel, mat_m).astype(BF16)

    heads = [d_att[:, 128 * h : 128 * h + 128] for h in (0, 1)]
    d_values = [nn(r.prob_t[h], heads[h]) for h in (0, 1)]
    r.dkx[1, zl] = jnp.concatenate(d_values, axis=1).astype(BF16)

    def dx_start(i):
        ref = r.dkx.at[i, zl]
        start(remote(ref, ref, r.dx_s.at[i], r.dx_r.at[i], other, t))

    dx_start(1)
    d_scores = []
    for h in (0, 1):
        d_prob = nt(heads[h], kv[:, 256 + 128 * h : 384 + 128 * h])
        delta = jnp.sum(probs[h] * d_prob, axis=1, keepdims=True)
        d_scores.append((probs[h] * (d_prob - delta) * SCALE).astype(BF16))
    d_keys = [tn(d_scores[h], query[:, 128 * h : 128 * h + 128]) for h in (0, 1)]
    r.dkx[0, zl] = jnp.concatenate(d_keys, axis=1).astype(BF16)
    dx_start(0)
    d_queries = [nn(d_scores[h], kv[:, 128 * h : 128 * h + 128]) for h in (0, 1)]
    d_query = jnp.concatenate(d_queries, axis=1).astype(BF16).astype(F32) * rstd
    mat_h = nn(r.blend_t[...], d_query.astype(BF16)).reshape(32, 8, 256)
    mat_g = nn(r.att_t[...], d_vel).reshape(32, 8, 256)
    r.hs[:, :, 0:256] = jnp.concatenate([mat_h, mat_g], axis=1).astype(BF16)
    frame_sum = jnp.sum(d_query, axis=0, keepdims=True)
    loss_high = loss_part.astype(BF16).astype(F32)
    which = lax.broadcasted_iota(jnp.int32, (16, 128), 0)
    extra = jnp.where(which == 2, loss_high, loss_part - loss_high)
    extra = jnp.where(which == 1, frame_sum[:, 128:256], extra)
    extra = jnp.where(which == 0, frame_sum[:, 0:128], extra)
    r.hs[:, :, 256:384] = jnp.broadcast_to(extra.astype(BF16)[None], (32, 16, 128))
    r.hr[d] = r.hs[d]

    def h_copy(k, peer):
        return remote(r.hs.at[peer], r.hr.at[d], r.hs_s.at[0], r.hs_r.at[0], peer, t)

    over_dp(lambda k, peer: h_copy(k, peer).start())

    arrived(r.dkx.at[1, 1 - zl], r.dx_r.at[1])
    r.dv[y] = r.dkx[1]
    for k in (1, 3, 2):
        start(
            remote(
                r.dv.at[y], r.dv.at[y], r.dv_s.at[k], r.dv_r.at[y], plane(x, turn(y, k, 4)), t
            )
        )
    arrived(r.dkx.at[0, 1 - zl], r.dx_r.at[0])
    r.dk[x] = r.dkx[0]
    for k in (1, 3, 2):
        start(
            remote(
                r.dk.at[x], r.dk.at[x], r.dk_s.at[k], r.dk_r.at[x], plane(turn(x, k, 4), y), t
            )
        )

    all_arrived(r.hr, r.hs_r.at[0])
    arrivals = r.hr[...].astype(F32)
    r.hg[d] = jnp.sum(arrivals[:, :, 0:256], axis=0).astype(BF16)

    def g_copy(k, peer):
        return remote(r.hg.at[d], r.hg.at[d], r.hg_s.at[0], r.hg_r.at[0], peer, t)

    over_dp(lambda k, peer: g_copy(k, peer).start())

    for k in (1, 3, 2):
        slot = turn(y, k, 4)
        arrived(r.dv.at[slot], r.dv_r.at[slot])
    all_v = r.dv[...].reshape(512, 256)
    for q in range(4):
        r.gv_send[q] = nn(r.cap_vt[q], all_v).astype(BF16)
    for k in (1, 3, 2):
        xx = turn(x, k, 4)
        start(
            remote(
                r.gv_send.at[xx], r.gv_recv.at[x], r.gv_s.at[k], r.gv_r.at[x], plane(xx, y), t
            )
        )
    r.gv_recv[x] = r.gv_send[x]
    for k in (1, 3, 2):
        slot = turn(x, k, 4)
        arrived(r.dk.at[slot], r.dk_r.at[slot])
    all_k = r.dk[...].reshape(512, 256)
    grad_k = nn(r.cap_kt[...], all_k).reshape(4, 128, 256)
    for q in range(4):
        r.gk_send[q] = grad_k[q].astype(BF16)
    for k in (1, 3, 2):
        yy = turn(y, k, 4)
        start(
            remote(
                r.gk_send.at[yy], r.gk_recv.at[y], r.gk_s.at[k], r.gk_r.at[y], plane(x, yy), t
            )
        )
    r.gk_recv[y] = r.gk_send[y]

    sums_p = jnp.concatenate([arrivals[:, 0, 256:384], arrivals[:, 1, 256:384]], axis=1)
    losses = arrivals[:, 2, 256:384] + arrivals[:, 3, 256:384]
    r.loss_out[...] = jnp.sum(losses, axis=0, keepdims=True) / 8192.0
    all_arrived(r.hg, r.hg_r.at[0])
    grads = r.hg[...].astype(F32)
    sum_h = grads[:, 0:8].reshape(256, 256)
    sum_g = grads[:, 8:16].reshape(256, 256).astype(BF16)
    r.packed_out[0:64] = nn(w_c, sum_h, HIGHEST) + tn(times_c, sums_p, HIGHEST)
    r.packed_out[320:384] = nt(r.vel[...], sum_g)
    for k in (1, 3, 2):
        slot = turn(y, k, 4)
        arrived(r.gk_recv.at[slot], r.gk_r.at[slot])
        slot = turn(x, k, 4)
        arrived(r.gv_recv.at[slot], r.gv_r.at[slot])
    r.packed_out[64:192] = jnp.sum(r.gk_recv[...].astype(F32), axis=0)
    r.packed_out[192:320] = jnp.sum(r.gv_recv[...].astype(F32), axis=0)

    for copy in pending:
        copy.wait_send()

    @pl.when(jnp.logical_not(inside))
    def _():
        cap_copy(0).wait_send()

    all_left(r.c0, r.c0_s.at[0])
    plane_left(r.zrb, r.zb_s.at[0])
    plane_left(r.zrf, r.zf_s.at[0])
    plane_left(r.agb, r.ab_s.at[0])
    plane_left(r.agf.at[c], r.af_s.at[0])
    all_left(r.hr, r.hs_s.at[0])
    all_left(r.hg, r.hg_s.at[0])


def unpack(loss, packed, loss_out, gq, gk, gv, go):
    loss_out[...] = loss[...]
    gq[...] = packed[0:64]
    gk[...] = packed[64:192]
    gv[...] = packed[192:320]
    go[...] = packed[320:384]


def rope_tables():
    inverse = 1000000.0 ** (-(np.arange(64, dtype=np.float32) * 2.0 / 128))
    angles = np.arange(64, dtype=np.float32)[:, None] * inverse[None, :].astype(np.float32)
    angles = np.concatenate([angles, angles], axis=1).astype(np.float32)
    sign = np.where(np.arange(128) < 64, -1.0, 1.0)[None, :]
    return np.cos(angles).astype(np.float32), (np.sin(angles) * sign).astype(np.float32)


def local(
    encoder_input_states,
    caption_lengths,
    encoder_input_gain,
    query_head_gain,
    key_head_gain,
    encoder_query_weight,
    encoder_key_weight,
    encoder_value_weight,
    encoder_output_weight,
    clean_motion,
    noise,
    timestep_index,
    motion_lengths,
    input_weight,
    velocity_weight,
    cross_query_weight,
    cross_key_weight,
    cross_value_weight,
    cross_output_weight,
):
    vmem = pl.BlockSpec(memory_space=pltpu.VMEM)
    hbm = pl.BlockSpec(memory_space=pl.ANY)
    smem = pl.BlockSpec(memory_space=pltpu.SMEM)
    spec = {name: vmem for name in INPUTS}
    for name in ("cap_len", "step_index", "motion_len"):
        spec[name] = smem
    for name in ("eq", "ek", "ev", "eo"):
        spec[name] = hbm
    cosine, sine = rope_tables()
    packed = pl.pallas_call(
        kernel,
        out_shape=[
            jax.ShapeDtypeStruct((1, 128), F32),
            jax.ShapeDtypeStruct((384, 256), F32),
        ],
        in_specs=[spec[name] for name in INPUTS],
        out_specs=[vmem] * 2,
        scratch_shapes=[pltpu.VMEM(shape, kind) for shape, kind in BUFFERS.values()]
        + [
            pltpu.SemaphoreType.DMA(shape if isinstance(shape, tuple) else (shape,))
            for shape in SEMAPHORES.values()
        ],
        compiler_params=pltpu.CompilerParams(
            collective_id=0, has_side_effects=True, vmem_limit_bytes=56 * 2**20
        ),
        name="motion_block",
    )(
        encoder_input_states,
        caption_lengths,
        timestep_index,
        motion_lengths,
        encoder_input_gain.reshape(8, 1, 512),
        query_head_gain.reshape(1, 128),
        key_head_gain.reshape(1, 128),
        jnp.asarray(cosine),
        jnp.asarray(sine),
        encoder_query_weight,
        encoder_key_weight,
        encoder_value_weight,
        encoder_output_weight,
        clean_motion,
        noise,
        input_weight.T,
        velocity_weight,
        cross_query_weight,
        cross_key_weight,
        cross_value_weight,
        cross_output_weight.T,
    )
    loss, gq, gk, gv, go = pl.pallas_call(
        unpack,
        out_shape=[
            jax.ShapeDtypeStruct((1, 128), F32),
            jax.ShapeDtypeStruct((64, 256), F32),
            jax.ShapeDtypeStruct((128, 256), F32),
            jax.ShapeDtypeStruct((128, 256), F32),
            jax.ShapeDtypeStruct((64, 256), F32),
        ],
        in_specs=[vmem] * 2,
        out_specs=[vmem] * 5,
        name="unpack",
    )(*packed)
    return (loss[0, 0], gq, gk, gv, go.T)


def solution(mesh):
    placed = (
        P("dp", None, "tensor"),
        P("dp"),
        P(),
        P(),
        P(),
        P(None, "tensor"),
        P(None, "tensor"),
        P(None, "tensor"),
        P("tensor", None),
        P("dp", None, None),
        P("dp", None, None),
        P("dp"),
        P("dp"),
        P(None, "dp"),
        P("dp", None),
        P("dp", "tensor"),
        P("dp", "tensor"),
        P("dp", "tensor"),
        P("tensor", "dp"),
    )
    return jax.shard_map(
        local,
        mesh=mesh,
        in_specs=placed,
        out_specs=(P(), P("dp", "tensor"), P("dp", "tensor"), P("dp", "tensor"), P("tensor", "dp")),
        check_vma=False,
    )
```

```python
import math
import types

import jax
import jax.numpy as jnp
import numpy as np
from jax import lax
from jax.experimental import pallas as pl
from jax.experimental.pallas import tpu as pltpu
from jax.sharding import PartitionSpec as P

F32 = jnp.float32
BF16 = jnp.bfloat16
MESH = pl.DeviceIdType.MESH
HIGHEST = lax.Precision.HIGHEST
EPSILON = 1e-06
STEPS = 1000
FRAMES = 360
PADDED = 384
SCALE = 1.0 / math.sqrt(128)

INPUTS = [
    "states", "cap_len", "step_index", "motion_len", "gain", "q_gain", "k_gain", "cosine", "sine",
    "eq", "ek", "ev", "eo", "clean", "noise", "w_in", "vel", "wq", "wk", "wv", "wo",
]
OUTPUTS = ["loss", "packed"]

BUFFERS = dict(
    w_qkv=((4096, 768), BF16),
    w_out=((512, 4096), BF16),
    c0=((32, 1, 384), F32),
    gx=((8, 64, 512), BF16),
    wkv=((16, 2, 64, 512), BF16),
    zsb=((16, 2, 16, 256), BF16),
    zrb=((16, 2, 16, 256), BF16),
    zsf=((16, 2, 8, 384), F32),
    zrf=((16, 2, 8, 384), F32),
    pzb=((2, 2, 16, 256), BF16),
    pzf=((2, 2, 8, 384), F32),
    agb=((16, 2, 16, 256), BF16),
    agf=((2, 16, 2, 8, 256), F32),
    ra_send=((4, 64, 512), BF16),
    ra_recv=((4, 64, 512), BF16),
    rb_send=((4, 64, 512), BF16),
    rb_recv=((4, 64, 512), BF16),
    r_own=((4, 64, 512), F32),
    cap_own=((64, 512), BF16),
    caps=((4, 2, 64, 512), BF16),
    kvx_send=((64, 512), BF16),
    kvx_recv=((64, 512), BF16),
    blend=((PADDED, 256), BF16),
    query=((PADDED, 256), BF16),
    hid_v=((PADDED, 256), F32),
    va_send=((4, 48, 256), BF16),
    va_recv=((4, 48, 256), BF16),
    v_own=((4, 48, 256), F32),
    vb_send=((4, 48, 256), BF16),
    vb_recv=((4, 48, 256), BF16),
    vg=((8, 48, 256), BF16),
    dkx=((2, 2, 64, 256), BF16),
    dk=((4, 2, 64, 256), BF16),
    dv=((4, 2, 64, 256), BF16),
    cap_k=((4, 2, 64, 512), BF16),
    cap_v=((4, 4, 2, 64, 128), BF16),
    cap_kt=((512, 512), BF16),
    cap_vt=((4, 128, 512), BF16),
    blend_t=((256, PADDED), BF16),
    att_t=((256, PADDED), BF16),
    prob_t=((2, 64, PADDED), BF16),
    gk_send=((4, 128, 256), BF16),
    gk_recv=((4, 128, 256), BF16),
    gv_send=((4, 128, 256), BF16),
    gv_recv=((4, 128, 256), BF16),
    hs=((32, 16, 384), BF16),
    hr=((32, 16, 384), BF16),
    hg=((32, 16, 256), BF16),
)

SEMAPHORES = dict(
    load=4,
    c0_s=1, c0_r=1,
    gx_s=8, gx_r=8,
    wkv_s=32, wkv_r=(16, 2),
    zb_s=1, zb_r=1, zf_s=1, zf_r=1, pb_s=1, pb_r=1, pf_s=1, pf_r=1,
    ab_s=1, ab_r=1, af_s=1, af_r=1, ap_s=1, ap_r=1,
    ra_s=4, ra_r=4, rb_s=4, rb_r=4,
    cp_s=8, cp_r=(4, 2),
    kvx_s=1, kvx_r=1,
    va_s=1, va_r=1, vb_s=4, vb_r=4, vg_s=8, vg_r=8,
    dx_s=2, dx_r=2, dk_s=4, dk_r=4, dv_s=4, dv_r=4,
    ck_s=4, ck_r=4, cv_s=4, cv_r=4,
    gk_s=4, gk_r=4, gv_s=4, gv_r=4,
    hs_s=1, hs_r=1, hg_s=1, hg_r=1,
)


def dot(a, b, left, right, precision=None):
    return lax.dot_general(
        a, b, (((left,), (right,)), ((), ())), precision=precision, preferred_element_type=F32
    )


def nn(a, b, precision=None):
    return dot(a, b, 1, 0, precision)


def nt(a, b, precision=None):
    return dot(a, b, 1, 1, precision)


def tn(a, b, precision=None):
    return dot(a, b, 0, 0, precision)


def softmax(scores):
    top = jnp.max(scores, axis=-1, keepdims=True)
    weights = jnp.exp(scores - top)
    return weights / jnp.sum(weights, axis=-1, keepdims=True)


def remote(source, target, send, receive, dp, tensor):
    return pltpu.make_async_remote_copy(
        src_ref=source,
        dst_ref=target,
        send_sem=send,
        recv_sem=receive,
        device_id=(dp, tensor),
        device_id_type=MESH,
    )


def kernel(*refs):
    names = INPUTS + [n + "_out" for n in OUTPUTS] + list(BUFFERS) + list(SEMAPHORES)
    r = types.SimpleNamespace(**dict(zip(names, refs, strict=True)))

    d = lax.axis_index("dp")
    t = lax.axis_index("tensor")
    zl = lax.div(d, 16)
    xy = lax.rem(d, 16)
    x = lax.div(xy, 4)
    y = lax.rem(xy, 4)
    zh = lax.div(t, 2)
    c = lax.rem(t, 2)
    mate = t + 1 - 2 * c
    other = (1 - zl) * 16 + xy
    pending = []

    def start(copy):
        copy.start()
        pending.append(copy)

    def turn(base, k, size):
        return lax.rem(base + k, size)

    def plane(xx, yy):
        return zl * 16 + xx * 4 + yy

    def arrived(slot, semaphore):
        remote(slot, slot, semaphore, semaphore, other, t).wait_recv()

    def all_arrived(buffer, semaphore):
        most = buffer.at[pl.ds(0, 31)]
        remote(most, most, semaphore, semaphore, other, t).wait_recv()

    def all_left(buffer, semaphore):
        most = buffer.at[pl.ds(0, 31)]
        remote(most, most, semaphore, semaphore, other, t).wait_send()

    def plane_arrived(buffer, semaphore):
        most = buffer.at[pl.ds(0, 15)]
        remote(most, most, semaphore, semaphore, other, t).wait_recv()

    def plane_left(buffer, semaphore):
        most = buffer.at[pl.ds(0, 15)]
        remote(most, most, semaphore, semaphore, other, t).wait_send()

    def over_plane(body):
        def step(k, carry):
            body(turn(xy, k, 16))
            return carry

        lax.fori_loop(1, 16, step, 0)

    def over_dp(body):
        def step(k, carry):
            body(k, turn(d, k, 32))
            return carry

        lax.fori_loop(1, 32, step, 0)

    loads = [
        pltpu.make_async_copy(r.eq, r.w_qkv.at[:, pl.ds(0, 512)], r.load.at[0]),
        pltpu.make_async_copy(r.ek, r.w_qkv.at[:, pl.ds(512, 128)], r.load.at[1]),
        pltpu.make_async_copy(r.ev, r.w_qkv.at[:, pl.ds(640, 128)], r.load.at[2]),
        pltpu.make_async_copy(r.eo, r.w_out, r.load.at[3]),
    ]
    for load in loads:
        load.start()

    barrier = pltpu.get_barrier_semaphore()

    def signal(dp, tensor):
        pl.semaphore_signal(barrier, inc=1, device_id=(dp, tensor), device_id_type=MESH)

    over_dp(lambda k, peer: signal(peer, t))
    signal(d, mate)
    for k in (1, 2, 3):
        signal(d, turn(zh, k, 4) * 2 + c)
        signal(other, turn(zh, k, 4) * 2 + c)

    r.gx[t] = r.states[0]
    wk_v = r.wk[...]
    wv_v = r.wv[...]
    for half in (0, 1):
        r.wkv[xy, half, :, 0:256] = wk_v[64 * half : 64 * half + 64]
        r.wkv[xy, half, :, 256:512] = wv_v[64 * half : 64 * half + 64]
    pl.semaphore_wait(barrier, 38)

    for k in (2, 1, 3):
        start(remote(r.gx.at[t], r.gx.at[t], r.gx_s.at[k], r.gx_r.at[t], d, turn(zh, k, 4) * 2 + c))
    start(remote(r.gx.at[t], r.gx.at[t], r.gx_s.at[0], r.gx_r.at[t], d, mate))

    def wkv_send(slot, half, dp, index):
        ref = r.wkv.at[slot, half]
        start(remote(ref, ref, r.wkv_s.at[index], r.wkv_r.at[slot, half], dp, t))

    for k in (1, 3, 2):
        wkv_send(xy, 0, plane(turn(x, k, 4), y), k - 1)
        wkv_send(xy, 1, plane(x, turn(y, k, 4)), 2 + k)

    w_in_v = r.w_in[...]
    w_in_t = w_in_v.astype(F32)
    decay = -math.log(10000.0) / 1024.0
    step_f = jnp.full((8, 128), r.step_index[0], jnp.int32).astype(F32)
    place = (
        lax.broadcasted_iota(jnp.int32, (8, 128), 0) * 128
        + lax.broadcasted_iota(jnp.int32, (8, 128), 1)
    ).astype(F32)
    all_angles = step_f * jnp.exp(decay * place)
    all_cos = jnp.cos(all_angles)
    all_sin = jnp.sin(all_angles)

    def total(tile):
        return jnp.sum(jnp.sum(tile, axis=1, keepdims=True), axis=0, keepdims=True)

    own_mean = total(all_cos + all_sin) / 2048.0
    time_square = total((all_cos - own_mean) ** 2 + (all_sin - own_mean) ** 2)
    lane = lax.broadcasted_iota(jnp.int32, (1, 128), 1)
    r.c0[d, :, 0:256] = jnp.sum(w_in_t, axis=0, keepdims=True)
    r.c0[d, :, 256:384] = jnp.where(lane == 0, step_f[0:1], own_mean)

    vel_v = r.vel[...]
    wq_v = r.wq[...]
    part_m = tn(r.wo[...], vel_v).reshape(32, 8, 256)
    part_b = tn(w_in_v, vel_v)

    def c0_copy(k, peer):
        return remote(r.c0.at[d], r.c0.at[d], r.c0_s.at[0], r.c0_r.at[0], peer, t)

    over_dp(lambda k, peer: c0_copy(k, peer).start())

    def wkv_second(first, k_list):
        for k in k_list:
            if k:
                slot = turn(x, k, 4) * 4 + y
                arrived(r.wkv.at[slot, 0], r.wkv_r.at[slot, 0])
                slot = x * 4 + turn(y, k, 4)
                arrived(r.wkv.at[slot, 1], r.wkv_r.at[slot, 1])
            for j in (1, 3, 2):
                wkv_send(turn(x, k, 4) * 4 + y, 0, plane(x, turn(y, j, 4)), first + 6 * k + j - 1)
                wkv_send(
                    x * 4 + turn(y, k, 4), 1, plane(turn(x, j, 4), y), first + 6 * k + 2 + j
                )

    wkv_second(6, (0, 1, 3, 2))

    for load in loads[:3]:
        load.wait()

    def project(slot, sums, square):
        chunk = r.gx[slot].astype(F32)
        square = square + jnp.sum(chunk * chunk, axis=1, keepdims=True)
        row = pl.multiple_of(slot * 512, 512)
        scaled = (chunk * r.gain[slot]).astype(BF16)
        return sums + nn(scaled, r.w_qkv[pl.ds(row, 512), :]), square

    sums, square = project(t, jnp.zeros((64, 768), F32), jnp.zeros((64, 1), F32))

    for k in (1, 3, 2):
        slot = turn(zh, k, 4) * 2 + c
        arrived(r.gx.at[slot], r.gx_r.at[slot])
        start(remote(r.gx.at[slot], r.gx.at[slot], r.gx_s.at[4 + k], r.gx_r.at[slot], d, mate))
        sums, square = project(slot, sums, square)

    arrived(r.gx.at[mate], r.gx_r.at[mate])
    sums, square = project(mate, sums, square)
    for k in (1, 3, 2):
        slot = turn(zh, k, 4) * 2 + (1 - c)
        arrived(r.gx.at[slot], r.gx_r.at[slot])
        sums, square = project(slot, sums, square)

    length = r.cap_len[0]
    rms = lax.rsqrt(square / 4096.0 + EPSILON)
    sums = sums * rms
    cosine = r.cosine[...]
    sine = r.sine[...]

    def turned(vectors, scaling):
        mean = jnp.mean(vectors * vectors, axis=1, keepdims=True)
        vectors = vectors * lax.rsqrt(mean + EPSILON) * scaling
        return (vectors * cosine + pltpu.roll(vectors, 64, 1) * sine).astype(BF16)

    q_gain = r.q_gain[...]
    queries = jnp.concatenate(
        [turned(sums[:, 128 * h : 128 * h + 128], q_gain) for h in range(4)], axis=0
    )
    keys = turned(sums[:, 512:640], r.k_gain[...])
    values = sums[:, 640:768].astype(BF16)
    scores = nt(queries, keys) * SCALE
    row = lax.rem(lax.broadcasted_iota(jnp.int32, (256, 64), 0), 64)
    col = lax.broadcasted_iota(jnp.int32, (256, 64), 1)
    scores = jnp.where((col <= row) & (col < length), scores, -1e30)
    mixed = nn(softmax(scores).astype(BF16), values).astype(BF16)
    mixed = jnp.concatenate([mixed[64 * h : 64 * h + 64] for h in range(4)], axis=1)

    loads[3].wait()
    for k in (1, 3, 2, 0):
        slot = turn(zh, k, 4)
        column = pl.multiple_of((slot * 2 + 1 - c) * 512, 512)
        r.ra_send[slot] = nn(mixed, r.w_out[:, pl.ds(column, 512)]).astype(BF16)
        start(
            remote(
                r.ra_send.at[slot], r.ra_recv.at[slot], r.ra_s.at[k], r.ra_r.at[slot], d, mate
            )
        )
    for k in (1, 3, 2, 0):
        slot = turn(zh, k, 4)
        column = pl.multiple_of((slot * 2 + c) * 512, 512)
        r.r_own[slot] = nn(mixed, r.w_out[:, pl.ds(column, 512)])
    for k in (2, 1, 3):
        slot = turn(zh, k, 4)
        arrived(r.ra_recv.at[slot], r.ra_r.at[slot])
        r.rb_send[slot] = (r.r_own[slot] + r.ra_recv[slot].astype(F32)).astype(BF16)
        start(
            remote(
                r.rb_send.at[slot], r.rb_recv.at[zh], r.rb_s.at[k], r.rb_r.at[zh], d, slot * 2 + c
            )
        )

    all_arrived(r.c0, r.c0_r.at[0])
    facts = r.c0[...].reshape(32, 384)
    w_mean = jnp.sum(facts[:, 0:256], axis=0, keepdims=True) / 2048.0
    steps = facts[:, 256:257]
    step_means = facts[:, 257:258]
    column = (
        lax.broadcasted_iota(jnp.int32, (1, 64), 1) + lax.rem(d, 16) * 64
    ).astype(F32)
    angles = steps * jnp.exp(decay * column)
    quarter = jnp.full((32, 64), zl, jnp.int32).astype(F32) * (math.pi / 2.0)
    times = jnp.cos(angles - quarter)
    times_c = times - step_means
    w_c = w_in_t - w_mean
    part_a = tn(w_c.astype(BF16), wq_v).reshape(32, 8, 256)
    slabs_b = jnp.concatenate([part_a, part_m], axis=1).astype(BF16)
    first_core = jnp.full((256, 256), c, jnp.int32) == 0
    part_f = jnp.where(first_core, part_b, tn(w_c, w_c, HIGHEST))
    slabs_f = part_f.reshape(32, 8, 256)
    time_rows = jnp.concatenate(
        [
            nn(times_c, wq_v.astype(F32), HIGHEST),
            nn(times, vel_v.astype(F32), HIGHEST),
            nn(times_c, w_c, HIGHEST),
        ],
        axis=1,
    )
    for z in (0, 1):
        here = slice(16 * z, 16 * z + 16)
        r.zsb[:, z] = slabs_b[here]
        r.zsf[:, z, :, 0:256] = slabs_f[here]
        for i in range(8):
            part = time_rows[here, 128 * i : 128 * i + 128] if i < 6 else jnp.zeros((16, 128), F32)
            r.zsf[:, z, i, 256:384] = part
    r.zrb[xy] = r.zsb[xy]
    r.zrf[xy] = r.zsf[xy]

    def z_start(peer):
        dp = zl * 16 + peer
        remote(r.zsb.at[peer], r.zrb.at[xy], r.zb_s.at[0], r.zb_r.at[0], dp, t).start()
        remote(r.zsf.at[peer], r.zrf.at[xy], r.zf_s.at[0], r.zf_r.at[0], dp, t).start()

    over_plane(z_start)

    slot = zh
    arrived(r.ra_recv.at[slot], r.ra_r.at[slot])
    own = r.r_own[slot] + r.ra_recv[slot].astype(F32)
    for k in (1, 3, 2):
        slot = turn(zh, k, 4)
        arrived(r.rb_recv.at[slot], r.rb_r.at[slot])
        own = own + r.rb_recv[slot].astype(F32)
    r.cap_own[...] = (r.states[0].astype(F32) + own).astype(BF16)

    target = lax.div(zh, 2)
    mine = lax.rem(t, 4)
    inside = target == zl

    def cap_copy(k):
        return remote(
            r.cap_own,
            r.caps.at[mine, zl],
            r.cp_s.at[k],
            r.cp_r.at[mine, zl],
            target * 16 + xy,
            turn(zh, k, 4) * 2 + c,
        )

    for k in (2, 1, 3):
        start(cap_copy(k))

    @pl.when(inside)
    def _():
        r.caps[mine, zl] = r.cap_own[...]

    @pl.when(jnp.logical_not(inside))
    def _():
        cap_copy(0).start()

    plane_arrived(r.zrb, r.zb_r.at[0])
    plane_arrived(r.zrf, r.zf_r.at[0])
    plane_b = jnp.sum(r.zrb[...].astype(F32), axis=0)
    plane_f = jnp.sum(r.zrf[...], axis=0)
    r.pzb[zl] = plane_b.astype(BF16)
    r.pzf[zl] = plane_f
    start(remote(r.pzb.at[zl], r.pzb.at[zl], r.pb_s.at[0], r.pb_r.at[0], other, t))
    start(remote(r.pzf.at[zl], r.pzf.at[zl], r.pf_s.at[0], r.pf_r.at[0], other, t))

    arrived(r.pzb.at[1 - zl], r.pb_r.at[0])
    arrived(r.pzf.at[1 - zl], r.pf_r.at[0])
    r.agb[xy] = (plane_b + r.pzb[1 - zl].astype(F32)).astype(BF16)
    slabs = plane_f + r.pzf[1 - zl]
    r.agf[c, xy] = slabs[:, :, 0:256]
    late = jnp.full((8, 128), zl, jnp.int32) == 1
    rows = jnp.where(late, slabs[1, :, 256:384], slabs[0, :, 256:384])
    time_own = jnp.concatenate([rows[i : i + 1] for i in range(6)], axis=1)

    def a_start(peer):
        dp = zl * 16 + peer
        remote(r.agb.at[xy], r.agb.at[xy], r.ab_s.at[0], r.ab_r.at[0], dp, t).start()
        remote(r.agf.at[c, xy], r.agf.at[c, xy], r.af_s.at[0], r.af_r.at[0], dp, t).start()

    over_plane(a_start)

    for k in (0, 1, 2, 3):
        for j in (1, 2, 3):
            slot = turn(x, k, 4) * 4 + turn(y, j, 4)
            arrived(r.wkv.at[slot, 0], r.wkv_r.at[slot, 0])
            slot = turn(x, j, 4) * 4 + turn(y, k, 4)
            arrived(r.wkv.at[slot, 1], r.wkv_r.at[slot, 1])

    forwards = []
    for z in (0, 1):
        for near in (0, 1):
            chunk = near * 2 + c
            ref = r.caps.at[chunk, z]
            own_slot = inside & (chunk == mine) & (z == zl)

            @pl.when(jnp.logical_not(own_slot))
            def _(ref=ref, chunk=chunk, z=z):
                arrived(ref, r.cp_r.at[chunk, z])

            start(remote(ref, ref, r.cp_s.at[4 + 2 * z + near], r.cp_r.at[chunk, z], d, mate))

    def project_caption(chunk):
        rows = r.caps[chunk].reshape(128, 512)
        weights = r.wkv[pl.ds(chunk * 4, 4)].reshape(512, 512)
        return nn(rows, weights)

    both = project_caption(c) + project_caption(2 + c)
    for near in (0, 1):
        for z in (0, 1):
            chunk = near * 2 + 1 - c
            arrived(r.caps.at[chunk, z], r.cp_r.at[chunk, z])
        both = both + project_caption(near * 2 + 1 - c)
    second = jnp.full((64, 512), zl, jnp.int32) == 1
    r.kvx_send[...] = jnp.where(second, both[0:64], both[64:128]).astype(BF16)
    start(remote(r.kvx_send, r.kvx_recv, r.kvx_s.at[0], r.kvx_r.at[0], other, t))

    r.cap_k[x] = r.caps[x]
    for q in range(4):
        column = pl.multiple_of(y * 128, 128)
        r.cap_v[y, q] = r.caps[q, :, :, pl.ds(column, 128)]
    for k in (1, 3, 2):
        xx = turn(x, k, 4)
        start(
            remote(r.caps.at[xx], r.cap_k.at[x], r.ck_s.at[k], r.ck_r.at[x], plane(xx, y), t)
        )
        yy = turn(y, k, 4)
        column = pl.multiple_of(yy * 128, 128)
        start(
            remote(
                r.caps.at[:, :, :, pl.ds(column, 128)],
                r.cap_v.at[y],
                r.cv_s.at[k],
                r.cv_r.at[y],
                plane(x, yy),
                t,
            )
        )

    clean = r.clean[0].astype(F32)
    noise = r.noise[0].astype(F32)
    tau = jnp.full((1, 256), r.step_index[0], jnp.int32).astype(F32) / STEPS
    margin = jnp.zeros((PADDED - FRAMES, 256), F32)
    blend_f = jnp.concatenate([(1.0 - tau) * clean + tau * noise, margin], axis=0)
    r.blend[...] = blend_f.astype(BF16)
    blend = r.blend[...]
    blend_f = blend.astype(F32)
    plane_arrived(r.agb, r.ab_r.at[0])
    plane_arrived(r.agf.at[c], r.af_r.at[0])
    start(remote(r.agf.at[c], r.agf.at[c], r.ap_s.at[0], r.ap_r.at[0], d, mate))
    matrices = r.agb[...].astype(F32)

    def planes(slabs):
        return jnp.concatenate([slabs[:, z].reshape(128, 256) for z in (0, 1)], axis=0)

    mat_a = planes(matrices[:, :, 0:8]).astype(BF16)
    mat_m = planes(matrices[:, :, 8:16]).astype(BF16)
    arrived(r.agf.at[1 - c], r.ap_r.at[0])
    mat_b = planes(r.agf[0])
    mat_s = planes(r.agf[1])
    r.hid_v[...] = nn(blend_f, mat_b, HIGHEST) + time_own[:, 256:512]
    spread = (nn(blend_f, mat_s, HIGHEST) + 2.0 * time_own[:, 512:768]) * blend_f
    variance = (jnp.sum(spread, axis=1, keepdims=True) + time_square) / 2048.0
    rstd = lax.rsqrt(jnp.maximum(variance, 0.0) + EPSILON)
    r.query[...] = ((nn(blend, mat_a) + time_own[:, 0:256]) * rstd).astype(BF16)

    kv_own = jnp.where(second, both[64:128], both[0:64])
    arrived(r.kvx_recv, r.kvx_r.at[0])
    kv = (kv_own + r.kvx_recv[...].astype(F32)).astype(BF16)

    query = r.query[...]
    allowed = lax.broadcasted_iota(jnp.int32, (PADDED, 64), 1) < length
    probs = []
    attended = []
    for h in (0, 1):
        span = slice(128 * h, 128 * h + 128)
        scores = nt(query[:, span], kv[:, span]) * SCALE
        prob = softmax(jnp.where(allowed, scores, -1e30))
        probs.append(prob)
        attended.append(nn(prob.astype(BF16), kv[:, 256 + 128 * h : 384 + 128 * h]).astype(BF16))
    attended = jnp.concatenate(attended, axis=1)
    branch = nn(attended, mat_m).reshape(8, 48, 256)

    first_half = jnp.full((48, 256), c, jnp.int32) == 0
    for q in range(4):
        r.va_send[q] = jnp.where(first_half, branch[2 * q + 1], branch[2 * q]).astype(BF16)
        r.v_own[q] = jnp.where(first_half, branch[2 * q], branch[2 * q + 1])
    start(remote(r.va_send, r.va_recv, r.va_s.at[0], r.va_r.at[0], d, mate))
    r.att_t[...] = attended.T
    for h in (0, 1):
        r.prob_t[h] = probs[h].astype(BF16).T
    arrived(r.va_recv, r.va_r.at[0])
    for k in (2, 1, 3):
        slot = turn(zh, k, 4)
        r.vb_send[slot] = (r.v_own[slot] + r.va_recv[slot].astype(F32)).astype(BF16)
        start(
            remote(
                r.vb_send.at[slot], r.vb_recv.at[zh], r.vb_s.at[k], r.vb_r.at[zh], d, slot * 2 + c
            )
        )
    r.blend_t[...] = blend.T
    for k in (1, 3, 2):
        slot = turn(x, k, 4)
        arrived(r.cap_k.at[slot], r.ck_r.at[slot])
    r.cap_kt[...] = r.cap_k[...].reshape(512, 512).T
    own = r.v_own[zh] + r.va_recv[zh].astype(F32)
    for k in (1, 3, 2):
        slot = turn(zh, k, 4)
        arrived(r.vb_recv.at[slot], r.vb_r.at[slot])
        own = own + r.vb_recv[slot].astype(F32)
    r.vg[t] = own.astype(BF16)
    for k in (2, 1, 3):
        start(remote(r.vg.at[t], r.vg.at[t], r.vg_s.at[k], r.vg_r.at[t], d, turn(zh, k, 4) * 2 + c))
    start(remote(r.vg.at[t], r.vg.at[t], r.vg_s.at[0], r.vg_r.at[t], d, mate))
    for k in (1, 3, 2):
        slot = turn(y, k, 4)
        arrived(r.cap_v.at[slot], r.cv_r.at[slot])
    for q in range(4):
        r.cap_vt[q] = r.cap_v[:, q].reshape(512, 128).T
    for k in (1, 3, 2):
        slot = turn(zh, k, 4) * 2 + c
        arrived(r.vg.at[slot], r.vg_r.at[slot])
        start(remote(r.vg.at[slot], r.vg.at[slot], r.vg_s.at[4 + k], r.vg_r.at[slot], d, mate))
    arrived(r.vg.at[mate], r.vg_r.at[mate])
    for k in (1, 3, 2):
        slot = turn(zh, k, 4) * 2 + 1 - c
        arrived(r.vg.at[slot], r.vg_r.at[slot])

    predicted = r.hid_v[...] + r.vg[...].astype(F32).reshape(PADDED, 256)
    residual = predicted - jnp.concatenate([noise - clean, margin], axis=0)
    frames = jnp.full((PADDED, 1), r.motion_len[0], jnp.int32)
    live = lax.broadcasted_iota(jnp.int32, (PADDED, 1), 0) < frames
    row_weight = jnp.where(live, 1.0 / frames.astype(F32), 0.0)
    weighted = residual * row_weight
    loss_part = total(residual * weighted)
    d_vel = (2.0 * weighted).astype(BF16)
    d_att = nt(d_vel, mat_m).astype(BF16)

    heads = [d_att[:, 128 * h : 128 * h + 128] for h in (0, 1)]
    d_values = [nn(r.prob_t[h], heads[h]) for h in (0, 1)]
    r.dkx[1, zl] = jnp.concatenate(d_values, axis=1).astype(BF16)

    def dx_start(i):
        ref = r.dkx.at[i, zl]
        start(remote(ref, ref, r.dx_s.at[i], r.dx_r.at[i], other, t))

    dx_start(1)
    d_scores = []
    for h in (0, 1):
        d_prob = nt(heads[h], kv[:, 256 + 128 * h : 384 + 128 * h])
        delta = jnp.sum(probs[h] * d_prob, axis=1, keepdims=True)
        d_scores.append((probs[h] * (d_prob - delta) * SCALE).astype(BF16))
    d_keys = [tn(d_scores[h], query[:, 128 * h : 128 * h + 128]) for h in (0, 1)]
    r.dkx[0, zl] = jnp.concatenate(d_keys, axis=1).astype(BF16)
    dx_start(0)
    d_queries = [nn(d_scores[h], kv[:, 128 * h : 128 * h + 128]) for h in (0, 1)]
    d_query = jnp.concatenate(d_queries, axis=1).astype(BF16).astype(F32) * rstd
    mat_h = nn(r.blend_t[...], d_query.astype(BF16)).reshape(32, 8, 256)
    mat_g = nn(r.att_t[...], d_vel).reshape(32, 8, 256)
    r.hs[:, :, 0:256] = jnp.concatenate([mat_h, mat_g], axis=1).astype(BF16)
    frame_sum = jnp.sum(d_query, axis=0, keepdims=True)
    loss_high = loss_part.astype(BF16).astype(F32)
    which = lax.broadcasted_iota(jnp.int32, (16, 128), 0)
    extra = jnp.where(which == 2, loss_high, loss_part - loss_high)
    extra = jnp.where(which == 1, frame_sum[:, 128:256], extra)
    extra = jnp.where(which == 0, frame_sum[:, 0:128], extra)
    r.hs[:, :, 256:384] = jnp.broadcast_to(extra.astype(BF16)[None], (32, 16, 128))
    r.hr[d] = r.hs[d]

    def h_copy(k, peer):
        return remote(r.hs.at[peer], r.hr.at[d], r.hs_s.at[0], r.hs_r.at[0], peer, t)

    over_dp(lambda k, peer: h_copy(k, peer).start())

    arrived(r.dkx.at[1, 1 - zl], r.dx_r.at[1])
    r.dv[y] = r.dkx[1]
    for k in (1, 3, 2):
        start(
            remote(
                r.dv.at[y], r.dv.at[y], r.dv_s.at[k], r.dv_r.at[y], plane(x, turn(y, k, 4)), t
            )
        )
    arrived(r.dkx.at[0, 1 - zl], r.dx_r.at[0])
    r.dk[x] = r.dkx[0]
    for k in (1, 3, 2):
        start(
            remote(
                r.dk.at[x], r.dk.at[x], r.dk_s.at[k], r.dk_r.at[x], plane(turn(x, k, 4), y), t
            )
        )

    all_arrived(r.hr, r.hs_r.at[0])
    arrivals = r.hr[...].astype(F32)
    r.hg[d] = jnp.sum(arrivals[:, :, 0:256], axis=0).astype(BF16)

    def g_copy(k, peer):
        return remote(r.hg.at[d], r.hg.at[d], r.hg_s.at[0], r.hg_r.at[0], peer, t)

    over_dp(lambda k, peer: g_copy(k, peer).start())

    for k in (1, 3, 2):
        slot = turn(y, k, 4)
        arrived(r.dv.at[slot], r.dv_r.at[slot])
    all_v = r.dv[...].reshape(512, 256)
    for q in range(4):
        r.gv_send[q] = nn(r.cap_vt[q], all_v).astype(BF16)
    for k in (1, 3, 2):
        xx = turn(x, k, 4)
        start(
            remote(
                r.gv_send.at[xx], r.gv_recv.at[x], r.gv_s.at[k], r.gv_r.at[x], plane(xx, y), t
            )
        )
    r.gv_recv[x] = r.gv_send[x]
    for k in (1, 3, 2):
        slot = turn(x, k, 4)
        arrived(r.dk.at[slot], r.dk_r.at[slot])
    all_k = r.dk[...].reshape(512, 256)
    grad_k = nn(r.cap_kt[...], all_k).reshape(4, 128, 256)
    for q in range(4):
        r.gk_send[q] = grad_k[q].astype(BF16)
    for k in (1, 3, 2):
        yy = turn(y, k, 4)
        start(
            remote(
                r.gk_send.at[yy], r.gk_recv.at[y], r.gk_s.at[k], r.gk_r.at[y], plane(x, yy), t
            )
        )
    r.gk_recv[y] = r.gk_send[y]

    sums_p = jnp.concatenate([arrivals[:, 0, 256:384], arrivals[:, 1, 256:384]], axis=1)
    losses = arrivals[:, 2, 256:384] + arrivals[:, 3, 256:384]
    r.loss_out[...] = jnp.sum(losses, axis=0, keepdims=True) / 8192.0
    all_arrived(r.hg, r.hg_r.at[0])
    grads = r.hg[...].astype(F32)
    sum_h = grads[:, 0:8].reshape(256, 256)
    sum_g = grads[:, 8:16].reshape(256, 256).astype(BF16)
    r.packed_out[0:64] = nn(w_c, sum_h, HIGHEST) + tn(times_c, sums_p, HIGHEST)
    r.packed_out[320:384] = nt(r.vel[...], sum_g)
    for k in (1, 3, 2):
        slot = turn(y, k, 4)
        arrived(r.gk_recv.at[slot], r.gk_r.at[slot])
        slot = turn(x, k, 4)
        arrived(r.gv_recv.at[slot], r.gv_r.at[slot])
    r.packed_out[64:192] = jnp.sum(r.gk_recv[...].astype(F32), axis=0)
    r.packed_out[192:320] = jnp.sum(r.gv_recv[...].astype(F32), axis=0)

    for copy in pending:
        copy.wait_send()

    @pl.when(jnp.logical_not(inside))
    def _():
        cap_copy(0).wait_send()

    all_left(r.c0, r.c0_s.at[0])
    plane_left(r.zrb, r.zb_s.at[0])
    plane_left(r.zrf, r.zf_s.at[0])
    plane_left(r.agb, r.ab_s.at[0])
    plane_left(r.agf.at[c], r.af_s.at[0])
    all_left(r.hr, r.hs_s.at[0])
    all_left(r.hg, r.hg_s.at[0])


def unpack(loss, packed, loss_out, gq, gk, gv, go):
    loss_out[...] = loss[...]
    gq[...] = packed[0:64]
    gk[...] = packed[64:192]
    gv[...] = packed[192:320]
    go[...] = packed[320:384]


def rope_tables():
    inverse = 1000000.0 ** (-(np.arange(64, dtype=np.float32) * 2.0 / 128))
    angles = np.arange(64, dtype=np.float32)[:, None] * inverse[None, :].astype(np.float32)
    angles = np.concatenate([angles, angles], axis=1).astype(np.float32)
    sign = np.where(np.arange(128) < 64, -1.0, 1.0)[None, :]
    return np.cos(angles).astype(np.float32), (np.sin(angles) * sign).astype(np.float32)


def local(
    encoder_input_states,
    caption_lengths,
    encoder_input_gain,
    query_head_gain,
    key_head_gain,
    encoder_query_weight,
    encoder_key_weight,
    encoder_value_weight,
    encoder_output_weight,
    clean_motion,
    noise,
    timestep_index,
    motion_lengths,
    input_weight,
    velocity_weight,
    cross_query_weight,
    cross_key_weight,
    cross_value_weight,
    cross_output_weight,
):
    vmem = pl.BlockSpec(memory_space=pltpu.VMEM)
    hbm = pl.BlockSpec(memory_space=pl.ANY)
    smem = pl.BlockSpec(memory_space=pltpu.SMEM)
    spec = {name: vmem for name in INPUTS}
    for name in ("cap_len", "step_index", "motion_len"):
        spec[name] = smem
    for name in ("eq", "ek", "ev", "eo"):
        spec[name] = hbm
    cosine, sine = rope_tables()
    packed = pl.pallas_call(
        kernel,
        out_shape=[
            jax.ShapeDtypeStruct((1, 128), F32),
            jax.ShapeDtypeStruct((384, 256), F32),
        ],
        in_specs=[spec[name] for name in INPUTS],
        out_specs=[vmem] * 2,
        scratch_shapes=[pltpu.VMEM(shape, kind) for shape, kind in BUFFERS.values()]
        + [
            pltpu.SemaphoreType.DMA(shape if isinstance(shape, tuple) else (shape,))
            for shape in SEMAPHORES.values()
        ],
        compiler_params=pltpu.CompilerParams(
            collective_id=0, has_side_effects=True, vmem_limit_bytes=56 * 2**20
        ),
        name="motion_block",
    )(
        encoder_input_states,
        caption_lengths,
        timestep_index,
        motion_lengths,
        encoder_input_gain.reshape(8, 1, 512),
        query_head_gain.reshape(1, 128),
        key_head_gain.reshape(1, 128),
        jnp.asarray(cosine),
        jnp.asarray(sine),
        encoder_query_weight,
        encoder_key_weight,
        encoder_value_weight,
        encoder_output_weight,
        clean_motion,
        noise,
        input_weight.T,
        velocity_weight,
        cross_query_weight,
        cross_key_weight,
        cross_value_weight,
        cross_output_weight.T,
    )
    loss, gq, gk, gv, go = pl.pallas_call(
        unpack,
        out_shape=[
            jax.ShapeDtypeStruct((1, 128), F32),
            jax.ShapeDtypeStruct((64, 256), F32),
            jax.ShapeDtypeStruct((128, 256), F32),
            jax.ShapeDtypeStruct((128, 256), F32),
            jax.ShapeDtypeStruct((64, 256), F32),
        ],
        in_specs=[vmem] * 2,
        out_specs=[vmem] * 5,
        name="unpack",
    )(*packed)
    return (loss[0, 0], gq, gk, gv, go.T)


def solution(mesh):
    placed = (
        P("dp", None, "tensor"),
        P("dp"),
        P(),
        P(),
        P(),
        P(None, "tensor"),
        P(None, "tensor"),
        P(None, "tensor"),
        P("tensor", None),
        P("dp", None, None),
        P("dp", None, None),
        P("dp"),
        P("dp"),
        P(None, "dp"),
        P("dp", None),
        P("dp", "tensor"),
        P("dp", "tensor"),
        P("dp", "tensor"),
        P("tensor", "dp"),
    )
    return jax.shard_map(
        local,
        mesh=mesh,
        in_specs=placed,
        out_specs=(P(), P("dp", "tensor"), P("dp", "tensor"), P("dp", "tensor"), P("tensor", "dp")),
        check_vma=False,
    )
```
